512 devices in a mesh: rep: 64 (over z_hi, y, x), tp: 8 (over z_lo, core).
Axes of the slice: x: 4, y: 4, z: 16 (z_hi: 4, z_lo: 4; z = z_hi * 4 + z_lo), core: 2. Of those that a mesh axis runs over, the one named last changes fastest.
Arguments:
- hidden: bfloat16 [64, 2, 4, 8192], P('rep', None, None, 'tp')
- norm_gain: bfloat16 [8192], replicated, may hold values from 0.5 to 1.5
- kv_weight: bfloat16 [8192, 2048], P(None, 'tp'), may hold values from -0.0625 to 0.0625
- delta_tiles: bfloat16 [64, 128, 1024], P('rep', None, 'tp'), may hold values from -0.0625 to 0.0625
- tile_blocks: int32 [64, 8], P('rep', 'tp'), may hold values from 0 to 127, as said below
- tile_counts: int32 [64, 8], P('rep', 'tp'), may hold values from 0 to 1
- queries: bfloat16 [64, 2, 4, 8192], P('rep', None, None, 'tp')
- kv_cache: bfloat16 [64, 4, 256, 2048], P('rep', None, None, 'tp')
- positions: int32 [64, 4], P('rep'), may hold values from 64 to 256
Outputs:
- new_entries: bfloat16 [64, 2, 4, 2048], P('rep', None, None, 'tp')
- attended: bfloat16 [64, 2, 4, 8192], P('rep', None, None, 'tp')
The draws below stay inside these ranges and needn't reach their ends.
Inputs may be any that keep to these rules, and one draw needn't show every extreme that they name: `tile_blocks`: trainer shard r holds only tiles of row block r, so its ids are 2 * r or 2 * r + 1.
All inputs are finite; a program needn't handle non-finite values.
Results may differ from the reference program's by a relative error of at most 0.017.
Values may be sent and summed in bfloat16 or wider, within the bound.
A program may use at most 64 MiB of HBM per device.

```python
import math
import jax
import jax.numpy as jnp
from jax import lax

D = 8192
HD = 128
QH = 8
TILE = 128
STEPS = 2
ROWS = 4
CACHE = 256
KMAX = 1
N_REP = 64
N_TP = 8


def shared_cache(key):
    return jax.random.normal(key, (N_REP, ROWS, CACHE, N_TP * 2 * HD), jnp.float32)


def draw_kv_cache(key, part):
    cache_values = shared_cache(key)
    key = jax.random.fold_in(key, 5)
    roughness = jnp.exp(jax.random.uniform(key, (N_REP, ROWS, CACHE, 1), jnp.float32, -0.35, 0.35))
    return (cache_values * roughness).astype(jnp.bfloat16)


def draw_queries(key, part):
    key = jax.random.fold_in(key, 9)
    query_values = jax.random.normal(key, (N_REP, STEPS, ROWS, N_TP, QH, HD), jnp.float32)
    return query_values.reshape(N_REP, STEPS, ROWS, N_TP * QH * HD).astype(jnp.bfloat16)


def draw_hidden(key, part):
    key = jax.random.fold_in(key, 3)
    first_key, second_key = jax.random.split(key, 2)
    shape = (N_REP, STEPS, ROWS, D)
    core = jax.random.normal(first_key, shape, jnp.float32)
    row_scale = jnp.exp(jax.random.uniform(second_key, (N_REP, STEPS, ROWS, 1), jnp.float32, 0.0, math.log(10.0)))
    column_scale = jnp.exp(jax.random.uniform(jax.random.fold_in(key, 4), (D,), jnp.float32, 0.0, math.log(10.0)))
    return (core * row_scale * column_scale).astype(jnp.bfloat16)


def draw_tile_blocks(key, part):
    key = jax.random.fold_in(key, 7)
    owned_ids = 2 * KMAX
    scores = jax.random.randint(key, (N_REP, N_TP, owned_ids), 0, 2 ** 20) * owned_ids + jnp.arange(owned_ids, dtype=jnp.int32)
    scores = scores.at[0, 0, 0].set(-1).at[N_REP - 1, 0, owned_ids - 1].set(-1)
    chosen = jnp.argsort(scores, axis=-1, stable=True)[..., :KMAX].astype(jnp.int32)
    global_ids = chosen + jnp.arange(N_REP, dtype=jnp.int32)[:, None, None] * owned_ids
    return jnp.transpose(global_ids, (0, 2, 1)).reshape(N_REP * KMAX, N_TP).astype(jnp.int32)


def draw_tile_counts(key, part):
    key = jax.random.fold_in(key, 6)
    counts = jax.random.randint(key, (N_REP, N_TP), 0, KMAX + 1)
    return counts.at[0, :].set(KMAX).at[1, 0].set(0).astype(jnp.int32)


def draw_positions(key, part):
    key = jax.random.fold_in(key, 8)
    filled = jax.random.randint(key, (N_REP, ROWS), CACHE // 4, CACHE + 1)
    return filled.at[0, 0].set(CACHE).at[1, 0].set(CACHE // 4).astype(jnp.int32)


def levels(key, dims, shards, smallest, largest):
    level = 1.0
    for axis_at, shards_of in shards:
        draws = jax.random.uniform(jax.random.fold_in(jax.random.fold_in(key, 6), axis_at), (shards_of,), jnp.float32, smallest / len(shards), largest / len(shards))
        level = level * jnp.repeat(jnp.exp(draws), dims[axis_at] // shards_of).reshape((-1,) + (1,) * (len(dims) - 1 - axis_at))
    return level


def gaussian(rng, extent, scale, reach, cuts=(), kind=jnp.bfloat16):
    result = jax.random.normal(rng, extent, jnp.float32) * scale
    if len(cuts) > 0:
        result = levels(rng, extent, cuts, -0.22, 0.18) * result
    return jnp.clip(result, min=-reach, max=reach).astype(kind)


def setup_inputs(seed: int = 0) -> dict:
    seeds = jax.random.split(jax.random.key(seed), 10)
    return {
        "hidden": draw_hidden(jax.random.fold_in(seeds[9], 71), 0),
        "norm_gain": jnp.clip(1.0 + 0.1 * jax.random.normal(seeds[1], (D,), jnp.float32), 0.5, 1.5).astype(jnp.bfloat16),
        "kv_weight": gaussian(seeds[2], (D, N_TP * 2 * HD), D ** -0.5, 0.0625, ((1, 8),)),
        "delta_tiles": gaussian(seeds[3], (N_REP * KMAX, TILE, N_TP * HD), D ** -0.5, 0.0625, ((0, 64), (2, 8))),
        "tile_blocks": draw_tile_blocks(jax.random.fold_in(seeds[9], 71), 0),
        "tile_counts": draw_tile_counts(jax.random.fold_in(seeds[9], 71), 0),
        "queries": draw_queries(jax.random.fold_in(seeds[9], 71), 0),
        "kv_cache": draw_kv_cache(jax.random.fold_in(seeds[9], 71), 0),
        "positions": draw_positions(jax.random.fold_in(seeds[9], 71), 0),
    }


EPS = 1e-06
THETA = 1000000.0

def rotate_keys(keys, position, head_dim):
    half_dim = head_dim // 2
    inverse = THETA ** (-(jnp.arange(half_dim, dtype=jnp.float32) * 2.0) / head_dim)
    angles = position.astype(jnp.float32)[..., None] * inverse
    cosine = jnp.cos(angles)
    sine = jnp.sin(angles)
    first_half = keys[..., :half_dim]
    second_half = keys[..., half_dim:]
    return jnp.concatenate([first_half * cosine - second_half * sine, second_half * cosine + first_half * sine], axis=-1)

def tile_products(normed_f, tiles_f, block_ids, is_valid, tile_rows, head_dim):
    row_total = normed_f.shape[0]
    split_rows = normed_f.reshape(row_total, normed_f.shape[1] // tile_rows, tile_rows)
    chosen = split_rows[:, block_ids // 2, :]
    products = jnp.einsum('nki,kio->kno', chosen, tiles_f, precision=lax.Precision.HIGHEST)
    products = products * is_valid.astype(jnp.float32)[:, None, None]
    picker = (block_ids[:, None] % 2 == jnp.arange(2, dtype=jnp.int32)[None, :]).astype(jnp.float32)
    placed = jnp.einsum('kno,kc->nco', products, picker, precision=lax.Precision.HIGHEST)
    return placed.reshape(row_total, 2 * head_dim)

def reference(hidden, norm_gain, kv_weight, delta_tiles, tile_blocks, tile_counts, queries, kv_cache, positions):
    row_total = N_REP * STEPS * ROWS
    flat = hidden.astype(jnp.float32).reshape(row_total, D)
    normed = (flat * lax.rsqrt(lax.optimization_barrier(jnp.mean(flat * flat, axis=-1, keepdims=True)) + EPS) * norm_gain.astype(jnp.float32)).astype(jnp.bfloat16)
    projected = jnp.dot(normed, kv_weight, preferred_element_type=jnp.float32)
    normed_f = normed.astype(jnp.float32)
    slot_index = jnp.arange(N_REP * KMAX, dtype=jnp.int32) % KMAX
    updates = []
    for head_index in range(N_TP):
        is_valid = slot_index < jnp.repeat(tile_counts[:, head_index], KMAX)
        tiles_f = delta_tiles[:, :, head_index * HD:(head_index + 1) * HD].astype(jnp.float32)
        updates.append(tile_products(normed_f, tiles_f, tile_blocks[:, head_index], is_valid, TILE, HD))
    combined = (projected + jnp.concatenate(updates, axis=1)).reshape(N_REP, STEPS, ROWS, N_TP, 2 * HD)
    moment = positions[:, None, :] + jnp.arange(STEPS, dtype=jnp.int32)[None, :, None]
    rotated = rotate_keys(combined[..., :HD], moment[..., None], HD)
    entries = jnp.concatenate([rotated, combined[..., HD:]], axis=-1).astype(jnp.bfloat16)
    queries_f = queries.astype(jnp.float32).reshape(N_REP, STEPS, ROWS, N_TP, QH, HD)
    cache = kv_cache.reshape(N_REP, ROWS, CACHE, N_TP, 2 * HD)
    scale = HD ** (-0.5)
    old_mask = jnp.arange(CACHE, dtype=jnp.int32)[None, None, None, None, :] < positions[:, None, :, None, None]
    new_mask = jnp.arange(STEPS, dtype=jnp.int32)[None, None, None, None, :] <= jnp.arange(STEPS, dtype=jnp.int32)[None, :, None, None, None]
    outputs = []
    for head_index in range(N_TP):
        query_head = queries_f[:, :, :, head_index]
        cached_keys = cache[:, :, :, head_index, :HD].astype(jnp.float32)
        cached_values = cache[:, :, :, head_index, HD:].astype(jnp.float32)
        fresh_keys = entries[:, :, :, head_index, :HD].astype(jnp.float32)
        fresh_values = entries[:, :, :, head_index, HD:].astype(jnp.float32)
        old_scores = jnp.einsum('asrhd,arjd->asrhj', query_head, cached_keys, precision=lax.Precision.HIGHEST) * scale
        new_scores = jnp.einsum('asrhd,atrd->asrht', query_head, fresh_keys, precision=lax.Precision.HIGHEST) * scale
        scores = jnp.concatenate([jnp.where(old_mask, old_scores, -1e+30), jnp.where(new_mask, new_scores, -1e+30)], axis=-1)
        peak = lax.optimization_barrier(jnp.max(scores, axis=-1, keepdims=True))
        raised = jnp.exp(scores - peak)
        weights = (raised / lax.optimization_barrier(jnp.sum(raised, axis=-1, keepdims=True))).astype(jnp.bfloat16)
        weights = lax.optimization_barrier(weights).astype(jnp.float32)
        mixed = jnp.einsum('asrhj,arjd->asrhd', weights[..., :CACHE], cached_values, precision=lax.Precision.HIGHEST)
        mixed = mixed + jnp.einsum('asrht,atrd->asrhd', weights[..., CACHE:], fresh_values, precision=lax.Precision.HIGHEST)
        outputs.append(mixed.astype(jnp.bfloat16))
    attended = jnp.stack(outputs, axis=3).reshape(N_REP, STEPS, ROWS, N_TP * QH * HD)
    return (entries.reshape(N_REP, STEPS, ROWS, N_TP * 2 * HD), attended)
```

```python
import functools
import math

import jax
import jax.numpy as jnp
from jax import lax
from jax.experimental import pallas as pl
from jax.experimental.pallas import tpu as pltpu
from jax.sharding import PartitionSpec as P

EPS = 1e-06
THETA = 1000000.0
F32 = jnp.float32
BF16 = jnp.bfloat16
LIFT = 1024.0

GROUPS = 4
PLACES = 16
SIDE = 4
ROWS = 8


def kernel(
    hidden,
    gain,
    weight,
    tile,
    blocks,
    counts,
    queries,
    cache,
    positions,
    entries_out,
    attended_out,
    hidden_v,
    send_v,
    recv_v,
    xb_v,
    tile_v,
    weight_v,
    gain_v,
    query_v,
    cache_v,
    part_v,
    ret_send,
    ret_recv,
    ssq_send,
    ssq_recv,
    positions_s,
    local_sem,
    hid_send_sem,
    hid_recv_sem,
    core_send_sem,
    core_recv_sem,
    tile_send_sem,
    tile_recv_sem,
    ret_send_sem,
    ret_recv_sem,
    ssq_send_sem,
    ssq_recv_sem,
):
    rep = lax.axis_index("rep")
    tp = lax.axis_index("tp")
    h, place = rep // PLACES, rep % PLACES
    y, x = place // SIDE, place % SIDE
    l, c = tp // 2, tp % 2

    def device(group, chip):
        return {"rep": group * PLACES + place, "tp": chip * 2 + c}

    def neighbour(offset, sign):
        dy, dx = offset // SIDE, offset % SIDE
        if sign > 0:
            return ((y + dy) % SIDE) * SIDE + (x + dx) % SIDE
        return ((y + SIDE - dy) % SIDE) * SIDE + (x + SIDE - dx) % SIDE

    partner = {"rep": rep, "tp": l * 2 + (1 - c)}
    offsets = sorted(
        range(1, PLACES), key=lambda o: min(o // SIDE, SIDE - o // SIDE) + min(o % SIDE, SIDE - o % SIDE)
    )

    barrier = pltpu.get_barrier_semaphore()

    def greet(where):
        pl.semaphore_signal(barrier, inc=1, device_id=where, device_id_type=pl.DeviceIdType.MESH)

    def local(source, target, index):
        return pltpu.make_async_copy(source, target, local_sem.at[index])

    hidden_load = local(hidden, hidden_v, 0)
    tile_load = local(tile.at[0], tile_v.at[place, pl.ds(0, 128)], 1)
    positions_load = local(positions, positions_s, 4)
    query_load = local(queries, query_v, 5)
    cache_load = local(cache.at[0], cache_v, 6)
    gain_load = local(gain.at[pl.ds(pl.multiple_of(h * 16, 16), 16)], gain_v, 7)
    weight_load = local(weight.at[pl.ds(pl.multiple_of(h * 2048, 2048), 2048)], weight_v, 8)
    hidden_load.start()

    for k in range(GROUPS):
        @pl.when((k != l) | (h != l))
        def _():
            greet(device(l, k))
            greet(device(k, h))

        @pl.when(k != h)
        def _():
            greet(device(k, l))

    greet(partner)
    for offset in offsets:
        greet({"rep": h * PLACES + neighbour(offset, 1), "tp": tp})

    tile_load.start()
    positions_load.start()
    query_load.start()
    cache_load.start()
    gain_load.start()
    weight_load.start()

    hidden_load.wait()
    mine = jnp.concatenate([hidden_v[0, 0].astype(F32), hidden_v[0, 1].astype(F32)], axis=0)
    send_v[...] = jnp.concatenate([mine[:, :512], mine[:, 512:]], axis=0).astype(BF16)
    valid = jnp.where(counts[0, 0] > 0, 1.0, 0.0)
    is_key = jnp.where(blocks[0, 0] % 2 == 0, 1.0, 0.0)
    tile_v[place, 128:144] = jnp.concatenate(
        [jnp.full((8, 128), valid * is_key, F32), jnp.full((8, 128), valid * (1.0 - is_key), F32)], axis=0
    ).astype(BF16)
    tile_load.wait()

    pl.semaphore_wait(barrier, 19 + jnp.where(h == l, 6, 8))

    def hidden_copy(chip):
        return pltpu.make_async_remote_copy(
            src_ref=send_v,
            dst_ref=recv_v.at[h, c],
            send_sem=hid_send_sem.at[chip],
            recv_sem=hid_recv_sem.at[h],
            device_id=device(l, chip),
            device_id_type=pl.DeviceIdType.MESH,
        )

    hidden_keep = pltpu.make_async_copy(send_v, recv_v.at[h, c], hid_recv_sem.at[h])
    for k in range(GROUPS):
        @pl.when((k != l) | (h != l))
        def _():
            hidden_copy(k).start()

        @pl.when((k == l) & (h == l))
        def _():
            hidden_keep.start()

    def tile_copy(number):
        offset = offsets[number]
        return pltpu.make_async_remote_copy(
            src_ref=tile_v.at[place],
            dst_ref=tile_v.at[place],
            send_sem=tile_send_sem.at[number],
            recv_sem=tile_recv_sem.at[place],
            device_id={"rep": h * PLACES + neighbour(offset, 1), "tp": tp},
            device_id_type=pl.DeviceIdType.MESH,
        )

    for number in range(PLACES - 1):
        tile_copy(number).start()

    query_load.wait()
    positions_load.wait()
    all_queries = jnp.concatenate([query_v[0, 0].astype(F32), query_v[0, 1].astype(F32)], axis=0)
    heads = all_queries.shape[1] // 128
    query = jnp.concatenate([all_queries[:, i * 128 : i * 128 + 128] for i in range(heads)], axis=0).astype(BF16)
    rows = heads * ROWS
    cache_load.wait()
    length = cache_v.shape[1]
    row = lax.broadcasted_iota(jnp.int32, (rows, length), 0)
    column = lax.broadcasted_iota(jnp.int32, (rows, length), 1)
    sequence = row % 4
    scores = jnp.zeros((rows, length), F32)
    filled = jnp.zeros((rows, length), jnp.int32)
    for r in range(4):
        keys = cache_v[r, :, :128]
        product = lax.dot_general(query, keys, (((1,), (1,)), ((), ())), preferred_element_type=F32)
        scores = jnp.where(sequence == r, product, scores)
        filled = jnp.where(sequence == r, positions_s[0, r], filled)
    scale = 128 ** (-0.5)
    scores = jnp.where(column < filled, scores * scale, -1e30)
    old_peak = jnp.max(scores, axis=-1, keepdims=True)
    raised = jnp.exp(scores - old_peak)
    old_sum = jnp.sum(raised, axis=-1, keepdims=True)
    old_mixed = jnp.zeros((rows, 128), F32)
    for r in range(4):
        chosen = jnp.where(sequence == r, raised, 0.0).astype(BF16)
        old_mixed = old_mixed + jnp.dot(chosen, cache_v[r, :, 128:], preferred_element_type=F32)

    token = lax.broadcasted_iota(jnp.int32, (ROWS, 128), 0)
    lane = lax.broadcasted_iota(jnp.int32, (ROWS, 128), 1)
    moment = token // 4
    for r in range(4):
        moment = jnp.where(token % 4 == r, token // 4 + positions_s[0, r], moment)
    inverse = jnp.exp((lane % 64).astype(F32) * (-2.0 * math.log(THETA) / 128))
    angle = moment.astype(F32) * inverse
    cosine = jnp.cos(angle)
    sine = jnp.where(lane < 64, -1.0, 1.0) * jnp.sin(angle)

    def core_copy(k, half):
        return pltpu.make_async_remote_copy(
            src_ref=recv_v.at[k, half],
            dst_ref=recv_v.at[k, half],
            send_sem=core_send_sem.at[k],
            recv_sem=core_recv_sem.at[k],
            device_id=partner,
            device_id_type=pl.DeviceIdType.MESH,
        )

    for k in range(GROUPS):
        pltpu.make_async_copy(send_v, recv_v.at[k, c], hid_recv_sem.at[k]).wait()
        core_copy(k, c).start()

    gain_load.wait()
    weight_load.wait()
    base = jnp.zeros((GROUPS * ROWS, 256), F32)
    squares = [jnp.zeros((ROWS, 128), F32) for _ in range(GROUPS)]
    for half in (c, 1 - c):
        if half is not c:
            for k in range(GROUPS):
                core_copy(k, half).wait_recv()
        pieces = [recv_v[k, half].astype(F32) for k in range(GROUPS)]
        gains = gain_v[...].astype(F32)
        gains = jnp.where(half == 0, gains[:8], gains[8:]) * LIFT
        for b in range(8):
            raw = [
                piece[(b // 4) * 8 : (b // 4) * 8 + 8, (b % 4) * 128 : (b % 4) * 128 + 128] for piece in pieces
            ]
            for k in range(GROUPS):
                squares[k] = squares[k] + raw[k] * raw[k]
            xb_v[half * 8 + b] = (jnp.concatenate(raw, axis=0) * gains[b : b + 1]).astype(BF16)
        joined = jnp.concatenate([xb_v[half * 8 + b] for b in range(8)], axis=1)
        base = base + jnp.dot(
            joined, weight_v[pl.ds(pl.multiple_of(half * 1024, 1024), 1024)], preferred_element_type=F32
        )
    squares = [jnp.broadcast_to(jnp.sum(s, axis=-1, keepdims=True), (ROWS, 128)) for s in squares]
    for k in range(GROUPS):
        ssq_send[k] = squares[k]

    def back(offset):
        return (h + offset) % GROUPS

    def ssq_copy(offset):
        return pltpu.make_async_remote_copy(
            src_ref=ssq_send.at[back(offset)],
            dst_ref=ssq_recv.at[h],
            send_sem=ssq_send_sem.at[offset - 1],
            recv_sem=ssq_recv_sem.at[h],
            device_id=device(back(offset), l),
            device_id_type=pl.DeviceIdType.MESH,
        )

    for offset in range(1, GROUPS):
        ssq_copy(offset).start()

    key_part = base[:, :128]
    value_part = base[:, 128:]
    for number in range(-1, PLACES - 1):
        if number < 0:
            slot = place
        else:
            slot = neighbour(offsets[number], -1)
            pltpu.make_async_copy(tile_v.at[slot], tile_v.at[slot], tile_recv_sem.at[slot]).wait()
        product = jnp.dot(xb_v[slot], tile_v[slot, 0:128], preferred_element_type=F32)
        flags = tile_v[slot, 128:144].astype(F32)
        key_part = key_part + product * flags[0:1]
        value_part = value_part + product * flags[8:9]

    for k in range(GROUPS):
        both = jnp.concatenate([key_part[k * 8 : k * 8 + 8], value_part[k * 8 : k * 8 + 8]], axis=0)
        part_v[k] = both
        ret_send[k] = both.astype(BF16)

    def ret_copy(offset):
        return pltpu.make_async_remote_copy(
            src_ref=ret_send.at[back(offset)],
            dst_ref=ret_recv.at[h],
            send_sem=ret_send_sem.at[offset - 1],
            recv_sem=ret_recv_sem.at[h],
            device_id=device(back(offset), l),
            device_id_type=pl.DeviceIdType.MESH,
        )

    for offset in range(1, GROUPS):
        ret_copy(offset).start()

    total = part_v[h]
    square = ssq_send[h]
    for offset in range(1, GROUPS):
        group = back(offset)
        pltpu.make_async_copy(ssq_recv.at[group], ssq_recv.at[group], ssq_recv_sem.at[group]).wait()
        square = square + ssq_recv[group]
    rate = lax.rsqrt(square / 8192.0 + EPS) * (1.0 / LIFT)
    for offset in range(1, GROUPS):
        group = back(offset)
        pltpu.make_async_copy(ret_recv.at[group], ret_recv.at[group], ret_recv_sem.at[group]).wait()
        total = total + ret_recv[group].astype(F32)

    new_keys = jnp.where(rate > 0.0, total[:8] * rate, 0.0)
    new_values = jnp.where(rate > 0.0, total[8:] * rate, 0.0)
    rotated = new_keys * cosine + pltpu.roll(new_keys, 64, 1) * sine
    new_entries = jnp.concatenate([rotated, new_values], axis=1)
    entries_out[0, 0] = new_entries[:4].astype(BF16)
    entries_out[0, 1] = new_entries[4:].astype(BF16)

    blank = jnp.zeros((ROWS, 128), F32)
    fresh_keys = jnp.concatenate([rotated, blank], axis=0).astype(BF16)
    fresh_values = jnp.concatenate([new_values, blank], axis=0).astype(BF16)
    new_scores = lax.dot_general(query, fresh_keys, (((1,), (1,)), ((), ())), preferred_element_type=F32)
    new_row = lax.broadcasted_iota(jnp.int32, (rows, 16), 0)
    new_column = lax.broadcasted_iota(jnp.int32, (rows, 16), 1)
    seen = (
        (new_column < 8) & (new_column % 4 == new_row % 4) & (new_column // 4 <= (new_row // 4) % 2)
    )
    new_scores = jnp.where(seen, new_scores * scale, -1e30)
    peak = jnp.maximum(old_peak, jnp.max(new_scores, axis=-1, keepdims=True))
    new_raised = jnp.exp(new_scores - peak)
    shrink = jnp.exp(old_peak - peak)
    all_sum = old_sum * shrink + jnp.sum(new_raised, axis=-1, keepdims=True)
    mixed = old_mixed * shrink + jnp.dot(new_raised.astype(BF16), fresh_values, preferred_element_type=F32)
    mixed = mixed / all_sum
    wide = jnp.concatenate([mixed[i * 8 : i * 8 + 8] for i in range(heads)], axis=1)
    attended_out[0, 0] = wide[:4].astype(BF16)
    attended_out[0, 1] = wide[4:].astype(BF16)

    for k in range(GROUPS):
        @pl.when((k != l) | (h != l))
        def _():
            hidden_copy(k).wait_send()

        core_copy(k, c).wait_send()
    for number in range(PLACES - 1):
        tile_copy(number).wait_send()
    for offset in range(1, GROUPS):
        ssq_copy(offset).wait_send()
        ret_copy(offset).wait_send()


def shards(hidden, norm_gain, kv_weight, delta_tiles, tile_blocks, tile_counts, queries, kv_cache, positions):
    anywhere = pl.BlockSpec(memory_space=pltpu.HBM)
    vmem = pl.BlockSpec(memory_space=pltpu.VMEM)
    dma = pltpu.SemaphoreType.DMA
    return pl.pallas_call(
        kernel,
        out_shape=(
            jax.ShapeDtypeStruct((1, 2, 4, 256), BF16),
            jax.ShapeDtypeStruct((1, 2, 4, 1024), BF16),
        ),
        in_specs=[anywhere] * 4 + [pl.BlockSpec(memory_space=pltpu.SMEM)] * 2 + [anywhere] * 3,
        out_specs=(vmem, vmem),
        scratch_shapes=[
            pltpu.VMEM((1, 2, 4, 1024), BF16),
            pltpu.VMEM((16, 512), BF16),
            pltpu.VMEM((4, 2, 16, 512), BF16),
            pltpu.VMEM((16, 32, 128), BF16),
            pltpu.VMEM((16, 144, 128), BF16),
            pltpu.VMEM((2048, 256), BF16),
            pltpu.VMEM((16, 128), BF16),
            pltpu.VMEM((1, 2, 4, 1024), BF16),
            pltpu.VMEM((4, 256, 256), BF16),
            pltpu.VMEM((4, 16, 128), F32),
            pltpu.VMEM((4, 16, 128), BF16),
            pltpu.VMEM((4, 16, 128), BF16),
            pltpu.VMEM((4, 8, 128), F32),
            pltpu.VMEM((4, 8, 128), F32),
            pltpu.SMEM((1, 4), jnp.int32),
            dma((9,)),
            dma((4,)),
            dma((4,)),
            dma((4,)),
            dma((4,)),
            dma((15,)),
            dma((16,)),
            dma((3,)),
            dma((4,)),
            dma((3,)),
            dma((4,)),
        ],
        compiler_params=pltpu.CompilerParams(
            collective_id=0, has_side_effects=True, vmem_limit_bytes=63 * 1024 * 1024
        ),
    )(
        hidden,
        norm_gain.reshape(64, 128),
        kv_weight,
        delta_tiles,
        tile_blocks,
        tile_counts,
        queries,
        kv_cache,
        positions,
    )


def solution(mesh):
    return jax.shard_map(
        shards,
        mesh=mesh,
        in_specs=(
            P("rep", None, None, "tp"),
            P(),
            P(None, "tp"),
            P("rep", None, "tp"),
            P("rep", "tp"),
            P("rep", "tp"),
            P("rep", None, None, "tp"),
            P("rep", None, None, "tp"),
            P("rep", None),
        ),
        out_specs=(P("rep", None, None, "tp"), P("rep", None, None, "tp")),
        check_vma=False,
    )
```

```python
import math

import jax
import jax.numpy as jnp
from jax import lax
from jax.experimental import pallas as pl
from jax.experimental.pallas import tpu as pltpu
from jax.sharding import PartitionSpec as P

EPS = 1e-06
THETA = 1000000.0
F32 = jnp.float32
BF16 = jnp.bfloat16
MESH = pl.DeviceIdType.MESH

GROUPS = 4
PLACES = 16
SIDE = 4
TP = 8
ROWS = 8
GREETED = {0: (2, 3, 1), 1: (2,), 2: (), 3: ()}


def kernel(
    hidden,
    gain,
    weight,
    tile,
    blocks,
    counts,
    queries,
    cache,
    positions,
    entries_out,
    attended_out,
    hidden_v,
    all_v,
    x_v,
    give_v,
    got_v,
    xh_v,
    tile_v,
    flag_v,
    weight_v,
    gain_v,
    query_v,
    cache_v,
    ret_send,
    ret_recv,
    positions_s,
    local_sem,
    tp_ready,
    plane_ready,
    z_ready,
    hid_send_sem,
    hid_recv_sem,
    give_send_sem,
    give_recv_sem,
    tile_send_sem,
    tile_recv_sem,
    flag_send_sem,
    flag_recv_sem,
    ret_send_sem,
    ret_recv_sem,
):
    rep = lax.axis_index("rep")
    tp = lax.axis_index("tp")
    h, place = rep // PLACES, rep % PLACES
    y, x = place // SIDE, place % SIDE
    greetings = jnp.where(h == 2, 2, jnp.where(h == 0, 0, 1))

    def in_tp(t):
        return {"rep": rep, "tp": t}

    def in_plane(p):
        return {"rep": h * PLACES + p, "tp": tp}

    def in_z(group):
        return {"rep": group * PLACES + place, "tp": tp}

    def neighbour(offset, sign):
        dy, dx = offset // SIDE, offset % SIDE
        if sign > 0:
            return ((y + dy) % SIDE) * SIDE + (x + dx) % SIDE
        return ((y + SIDE - dy) % SIDE) * SIDE + (x + SIDE - dx) % SIDE

    def hops(offset):
        dy, dx = offset // SIDE, offset % SIDE
        return min(dy, SIDE - dy) + min(dx, SIDE - dx)

    offsets = sorted(range(1, PLACES), key=lambda o: -hops(o))

    def local(source, target, index):
        return pltpu.make_async_copy(source, target, local_sem.at[index])

    hidden_load = local(hidden, hidden_v, 0)
    tile_load = local(tile.at[0], tile_v.at[h], 1)
    positions_load = local(positions, positions_s, 2)
    query_load = local(queries, query_v, 3)
    cache_load = local(cache.at[0], cache_v, 4)
    gain_load = local(gain, gain_v, 5)
    weight_load = local(weight, weight_v, 6)
    hidden_load.start()

    barrier = pltpu.get_barrier_semaphore()

    def signal(semaphore, where):
        pl.semaphore_signal(semaphore, inc=1, device_id=where, device_id_type=MESH)

    for group in range(GROUPS):
        @pl.when(h == group)
        def _():
            for later in GREETED[group]:
                signal(barrier, in_z(later))

    for t in range(1, TP):
        @pl.when(t > tp)
        def _():
            signal(barrier, in_tp(t))

    for p in range(1, PLACES):
        @pl.when(p > place)
        def _():
            signal(barrier, in_plane(p))

    valid = jnp.where(counts[0, 0] > 0, 1.0, 0.0)
    is_key = jnp.where(blocks[0, 0] % 2 == 0, 1.0, 0.0)
    flag_v[h] = jnp.concatenate(
        [jnp.full((8, 128), valid * is_key, F32), jnp.full((8, 128), valid * (1.0 - is_key), F32)], axis=0
    ).astype(BF16)

    @pl.when(place + tp + greetings > 0)
    def _():
        pl.semaphore_wait(barrier, place + tp + greetings)


    def tile_copy(source, group, number):
        return pltpu.make_async_remote_copy(
            src_ref=tile.at[0] if source is None else tile_v.at[source],
            dst_ref=tile_v.at[h if source is None else source],
            send_sem=tile_send_sem.at[number],
            recv_sem=tile_recv_sem.at[h if source is None else source],
            device_id=in_z(group),
            device_id_type=MESH,
        )

    def flag_copy(source, group, number):
        slot = h if source is None else source
        return pltpu.make_async_remote_copy(
            src_ref=flag_v.at[slot],
            dst_ref=flag_v.at[slot],
            send_sem=flag_send_sem.at[number],
            recv_sem=flag_recv_sem.at[slot],
            device_id=in_z(group),
            device_id_type=MESH,
        )

    def tile_start(source, group, number):
        tile_copy(source, group, number).start()
        flag_copy(source, group, number).start()

    def arrive(group):
        pltpu.make_async_copy(tile_v.at[group], tile_v.at[group], tile_recv_sem.at[group]).wait()
        pltpu.make_async_copy(flag_v.at[group], flag_v.at[group], flag_recv_sem.at[group]).wait()

    @pl.when(h > 0)
    def _():
        tile_start(None, 0, 0)

        @pl.when(h != 2)
        def _():
            signal(z_ready.at[h], in_z(0))

        @pl.when(h == 2)
        def _():
            signal(z_ready.at[h], in_z(1))

    for t in range(TP - 1):
        @pl.when(t < tp)
        def _():
            signal(tp_ready, in_tp(t))

    for p in range(PLACES - 1):
        @pl.when(p < place)
        def _():
            signal(plane_ready, in_plane(p))

    hidden_load.wait()
    mine = jnp.concatenate([hidden_v[0, 0].astype(F32), hidden_v[0, 1].astype(F32)], axis=0)
    all_v[tp] = jnp.concatenate([mine[:, :512], mine[:, 512:]], axis=0).astype(BF16)

    def hidden_copy(t):
        return pltpu.make_async_remote_copy(
            src_ref=all_v.at[tp],
            dst_ref=all_v.at[tp],
            send_sem=hid_send_sem.at[t],
            recv_sem=hid_recv_sem.at[tp],
            device_id=in_tp(t),
            device_id_type=MESH,
        )

    for t in range(TP - 1):
        @pl.when(t < tp)
        def _():
            hidden_copy(t).start()

    @pl.when(tp < TP - 1)
    def _():
        pl.semaphore_wait(tp_ready, TP - 1 - tp)

    for t in range(TP - 1, 0, -1):
        @pl.when(t > tp)
        def _():
            hidden_copy(t).start()

    gain_load.start()
    query_load.start()
    positions_load.start()
    cache_load.start()
    tile_load.start()
    weight_load.start()

    query_load.wait()
    positions_load.wait()
    all_queries = jnp.concatenate([query_v[0, 0].astype(F32), query_v[0, 1].astype(F32)], axis=0)
    heads = all_queries.shape[1] // 128
    query = jnp.concatenate([all_queries[:, i * 128 : i * 128 + 128] for i in range(heads)], axis=0).astype(BF16)
    rows = heads * ROWS
    cache_load.wait()
    length = cache_v.shape[1]
    row = lax.broadcasted_iota(jnp.int32, (rows, length), 0)
    column = lax.broadcasted_iota(jnp.int32, (rows, length), 1)
    sequence = row % 4
    scores = jnp.zeros((rows, length), F32)
    filled = jnp.zeros((rows, length), jnp.int32)
    for r in range(4):
        keys = cache_v[r, :, :128]
        product = lax.dot_general(query, keys, (((1,), (1,)), ((), ())), preferred_element_type=F32)
        scores = jnp.where(sequence == r, product, scores)
        filled = jnp.where(sequence == r, positions_s[0, r], filled)
    scale = 128 ** (-0.5)
    scores = jnp.where(column < filled, scores * scale, -1e30)
    old_peak = jnp.max(scores, axis=-1, keepdims=True)
    raised = jnp.exp(scores - old_peak)
    old_sum = jnp.sum(raised, axis=-1, keepdims=True)
    old_mixed = jnp.zeros((rows, 128), F32)
    for r in range(4):
        chosen = jnp.where(sequence == r, raised, 0.0).astype(BF16)
        old_mixed = old_mixed + jnp.dot(chosen, cache_v[r, :, 128:], preferred_element_type=F32)

    token = lax.broadcasted_iota(jnp.int32, (ROWS, 128), 0)
    lane = lax.broadcasted_iota(jnp.int32, (ROWS, 128), 1)
    moment = token // 4
    for r in range(4):
        moment = jnp.where(token % 4 == r, token // 4 + positions_s[0, r], moment)
    inverse = jnp.exp((lane % 64).astype(F32) * (-2.0 * math.log(THETA) / 128))
    angle = moment.astype(F32) * inverse
    cosine = jnp.cos(angle)
    sine = jnp.where(lane < 64, -1.0, 1.0) * jnp.sin(angle)

    for t in range(TP):
        @pl.when(t != tp)
        def _():
            pltpu.make_async_copy(all_v.at[t], all_v.at[t], hid_recv_sem.at[t]).wait()

    squares = jnp.zeros((ROWS, 128), F32)
    for t in range(TP):
        piece = all_v[t].astype(F32)
        for b in range(8):
            part = piece[(b // 4) * 8 : (b // 4) * 8 + 8, (b % 4) * 128 : (b % 4) * 128 + 128]
            squares = squares + part * part
    rate = lax.rsqrt(jnp.sum(squares, axis=-1, keepdims=True) / 8192.0 + EPS)
    rate = jnp.broadcast_to(rate, (ROWS, 128))
    gain_load.wait()
    gains = gain_v[...].astype(F32)
    normed = []
    for t in range(TP):
        piece = all_v[t].astype(F32)
        for b in range(8):
            part = piece[(b // 4) * 8 : (b // 4) * 8 + 8, (b % 4) * 128 : (b % 4) * 128 + 128]
            normed.append(part * rate * gains[t * 8 + b : t * 8 + b + 1])
    for p in range(PLACES):
        give_v[p] = jnp.concatenate([normed[group * 16 + p] for group in range(GROUPS)], axis=0).astype(BF16)

    def give_copy(number):
        there = neighbour(offsets[number], 1)
        return pltpu.make_async_remote_copy(
            src_ref=give_v.at[there],
            dst_ref=got_v.at[place],
            send_sem=give_send_sem.at[number],
            recv_sem=give_recv_sem.at[place],
            device_id=in_plane(there),
            device_id_type=MESH,
        )

    @pl.when(place < PLACES - 1)
    def _():
        pl.semaphore_wait(plane_ready, PLACES - 1 - place)

    for number in range(PLACES - 1):
        give_copy(number).start()

    @pl.when(h == 0)
    def _():
        pl.semaphore_wait(z_ready.at[1], 1)
        tile_start(None, 1, 0)

    got_v[place] = give_v[place]

    for t in range(TP):
        x_v[t] = jnp.concatenate(normed[t * 8 : t * 8 + 8], axis=1).astype(BF16)
    weight_load.wait()

    def project(t, total):
        rows_of = weight_v[pl.ds(pl.multiple_of(t * 1024, 1024), 1024)]
        return total + jnp.dot(x_v[t], rows_of, preferred_element_type=F32)

    base = lax.fori_loop(0, TP, project, jnp.zeros((ROWS, 256), F32))

    first, second, third = (
        jnp.where(h == 0, 1, 0),
        jnp.where(h == 0, 3, jnp.where(h == 1, 2, 1)),
        jnp.where((h == 0) | (h == 3), 2, 3),
    )

    @pl.when(h == 0)
    def _():
        pl.semaphore_wait(z_ready.at[3], 1)
        tile_start(None, 3, 1)

    @pl.when(h == 2)
    def _():
        tile_start(None, 1, 1)

    arrive(first)

    @pl.when(h == 1)
    def _():
        pl.semaphore_wait(z_ready.at[2], 1)
        tile_start(0, 2, 1)
        tile_start(None, 2, 2)

    arrive(second)

    @pl.when(h == 0)
    def _():
        tile_start(1, 3, 2)
        tile_start(3, 1, 3)


    for number in range(PLACES - 1):
        there = neighbour(offsets[number], -1)
        pltpu.make_async_copy(got_v.at[there], got_v.at[there], give_recv_sem.at[there]).wait()
    for p in range(0, PLACES, 2):
        even, odd = got_v[p].astype(F32), got_v[p + 1].astype(F32)
        for group in range(GROUPS):
            xh_v[group, p * 8 : p * 8 + 16] = jnp.concatenate(
                [even[group * 8 : group * 8 + 8], odd[group * 8 : group * 8 + 8]], axis=0
            ).astype(BF16)

    def multiply(group, key_part, value_part):
        product = jnp.dot(xh_v[group], tile_v[group], preferred_element_type=F32)
        flags = flag_v[group].astype(F32)
        return key_part + product * flags[0:1], value_part + product * flags[8:9]

    blank = jnp.zeros((PLACES * ROWS, 128), F32)
    tile_load.wait()
    key_part, value_part = multiply(h, blank, blank)
    key_part, value_part = multiply(first, key_part, value_part)
    key_part, value_part = multiply(second, key_part, value_part)
    arrive(third)

    @pl.when(h == 1)
    def _():
        tile_start(3, 2, 3)

    key_part, value_part = multiply(third, key_part, value_part)

    def ret_copy(number):
        there = neighbour(offsets[number], 1)
        return pltpu.make_async_remote_copy(
            src_ref=ret_send.at[there],
            dst_ref=ret_recv.at[place],
            send_sem=ret_send_sem.at[number],
            recv_sem=ret_recv_sem.at[place],
            device_id=in_plane(there),
            device_id_type=MESH,
        )

    for p in range(PLACES):
        ret_send[p] = jnp.concatenate([key_part[p * 8 : p * 8 + 8], value_part[p * 8 : p * 8 + 8]], axis=0).astype(BF16)
    for number in range(PLACES - 1):
        ret_copy(number).start()

    @pl.when(h == 0)
    def _():
        tile_start(2, 3, 4)

    total = ret_send[place].astype(F32)
    for number in range(PLACES - 2, -1, -1):
        there = neighbour(offsets[number], -1)
        pltpu.make_async_copy(ret_recv.at[there], ret_recv.at[there], ret_recv_sem.at[there]).wait()
        total = total + ret_recv[there].astype(F32)
    new_keys = base[:, :128] + total[:8]
    new_values = base[:, 128:] + total[8:]

    rotated = new_keys * cosine + pltpu.roll(new_keys, 64, 1) * sine
    new_entries = jnp.concatenate([rotated, new_values], axis=1)
    entries_out[0, 0] = new_entries[:4].astype(BF16)
    entries_out[0, 1] = new_entries[4:].astype(BF16)

    empty = jnp.zeros((ROWS, 128), F32)
    fresh_keys = jnp.concatenate([rotated, empty], axis=0).astype(BF16)
    fresh_values = jnp.concatenate([new_values, empty], axis=0).astype(BF16)
    new_scores = lax.dot_general(query, fresh_keys, (((1,), (1,)), ((), ())), preferred_element_type=F32)
    new_row = lax.broadcasted_iota(jnp.int32, (rows, 16), 0)
    new_column = lax.broadcasted_iota(jnp.int32, (rows, 16), 1)
    seen = (
        (new_column < 8) & (new_column % 4 == new_row % 4) & (new_column // 4 <= (new_row // 4) % 2)
    )
    new_scores = jnp.where(seen, new_scores * scale, -1e30)
    peak = jnp.maximum(old_peak, jnp.max(new_scores, axis=-1, keepdims=True))
    new_raised = jnp.exp(new_scores - peak)
    shrink = jnp.exp(old_peak - peak)
    all_sum = old_sum * shrink + jnp.sum(new_raised, axis=-1, keepdims=True)
    mixed = old_mixed * shrink + jnp.dot(new_raised.astype(BF16), fresh_values, preferred_element_type=F32)
    mixed = mixed / all_sum
    wide = jnp.concatenate([mixed[i * 8 : i * 8 + 8] for i in range(heads)], axis=1)
    attended_out[0, 0] = wide[:4].astype(BF16)
    attended_out[0, 1] = wide[4:].astype(BF16)

    for t in range(TP):
        @pl.when(t != tp)
        def _():
            hidden_copy(t).wait_send()

    for number in range(5):
        @pl.when(number < jnp.where(h == 0, 5, jnp.where(h == 1, 4, jnp.where(h == 2, 2, 1))))
        def _():
            tile_copy(None, 0, number).wait_send()
            flag_copy(None, 0, number).wait_send()

    for number in range(PLACES - 1):
        give_copy(number).wait_send()
        ret_copy(number).wait_send()


def shards(hidden, norm_gain, kv_weight, delta_tiles, tile_blocks, tile_counts, queries, kv_cache, positions):
    def hbm(array):
        return pltpu.with_memory_space_constraint(array, pltpu.HBM)

    anywhere = pl.BlockSpec(memory_space=pltpu.HBM)
    scalar = pl.BlockSpec(memory_space=pltpu.SMEM)
    vmem = pl.BlockSpec(memory_space=pltpu.VMEM)
    dma = pltpu.SemaphoreType.DMA
    regular = pltpu.SemaphoreType.REGULAR
    return pl.pallas_call(
        kernel,
        out_shape=(
            jax.ShapeDtypeStruct((1, 2, 4, 256), BF16),
            jax.ShapeDtypeStruct((1, 2, 4, 1024), BF16),
        ),
        in_specs=[anywhere] * 4 + [scalar] * 2 + [anywhere] * 3,
        out_specs=(vmem, vmem),
        scratch_shapes=[
            pltpu.VMEM((1, 2, 4, 1024), BF16),
            pltpu.VMEM((TP, 16, 512), BF16),
            pltpu.VMEM((TP, ROWS, 1024), BF16),
            pltpu.VMEM((PLACES, 32, 128), BF16),
            pltpu.VMEM((PLACES, 32, 128), BF16),
            pltpu.VMEM((GROUPS, 128, 128), BF16),
            pltpu.VMEM((GROUPS, 128, 128), BF16),
            pltpu.VMEM((GROUPS, 16, 128), BF16),
            pltpu.VMEM((8192, 256), BF16),
            pltpu.VMEM((64, 128), BF16),
            pltpu.VMEM((1, 2, 4, 1024), BF16),
            pltpu.VMEM((4, 256, 256), BF16),
            pltpu.VMEM((PLACES, 16, 128), BF16),
            pltpu.VMEM((PLACES, 16, 128), BF16),
            pltpu.SMEM((1, 4), jnp.int32),
            dma((7,)),
            regular,
            regular,
            regular((GROUPS,)),
            dma((TP,)),
            dma((TP,)),
            dma((PLACES - 1,)),
            dma((PLACES,)),
            dma((5,)),
            dma((GROUPS,)),
            dma((5,)),
            dma((GROUPS,)),
            dma((PLACES - 1,)),
            dma((PLACES,)),
        ],
        compiler_params=pltpu.CompilerParams(
            collective_id=0, has_side_effects=True, vmem_limit_bytes=24 * 1024 * 1024
        ),
    )(
        hbm(hidden),
        hbm(norm_gain.reshape(64, 128)),
        hbm(kv_weight),
        hbm(delta_tiles),
        tile_blocks,
        tile_counts,
        hbm(queries),
        hbm(kv_cache),
        hbm(positions),
    )


def solution(mesh):
    return jax.shard_map(
        shards,
        mesh=mesh,
        in_specs=(
            P("rep", None, None, "tp"),
            P(),
            P(None, "tp"),
            P("rep", None, "tp"),
            P("rep", "tp"),
            P("rep", "tp"),
            P("rep", None, None, "tp"),
            P("rep", None, None, "tp"),
            P("rep", None),
        ),
        out_specs=(P("rep", None, None, "tp"), P("rep", None, None, "tp")),
        check_vma=False,
    )
```

```python
import math

import jax
import jax.numpy as jnp
from jax import lax
from jax.experimental import pallas as pl
from jax.experimental.pallas import tpu as pltpu
from jax.sharding import PartitionSpec as P

EPS = 1e-06
THETA = 1000000.0
F32 = jnp.float32
BF16 = jnp.bfloat16
MESH = pl.DeviceIdType.MESH

GROUPS = 4
PLACES = 16
SIDE = 4
TP = 8
ROWS = 8
GREETED = {0: (2, 3, 1), 1: (2,), 2: (), 3: ()}


def kernel(
    hidden,
    gain,
    weight,
    tile,
    blocks,
    counts,
    queries,
    cache,
    positions,
    entries_out,
    attended_out,
    hidden_v,
    all_v,
    x_v,
    give_v,
    got_v,
    xh_v,
    tile_v,
    flag_v,
    weight_v,
    gain_v,
    query_v,
    cache_v,
    ret_send,
    ret_recv,
    positions_s,
    local_sem,
    tp_ready,
    plane_ready,
    z_ready,
    hid_send_sem,
    hid_recv_sem,
    give_send_sem,
    give_recv_sem,
    tile_send_sem,
    tile_recv_sem,
    flag_send_sem,
    flag_recv_sem,
    ret_send_sem,
    ret_recv_sem,
):
    rep = lax.axis_index("rep")
    tp = lax.axis_index("tp")
    h, place = rep // PLACES, rep % PLACES
    y, x = place // SIDE, place % SIDE
    greetings = jnp.where(h == 2, 2, jnp.where(h == 0, 0, 1))

    def in_tp(t):
        return {"rep": rep, "tp": t}

    def in_plane(p):
        return {"rep": h * PLACES + p, "tp": tp}

    def in_z(group):
        return {"rep": group * PLACES + place, "tp": tp}

    def neighbour(offset, sign):
        dy, dx = offset // SIDE, offset % SIDE
        if sign > 0:
            return ((y + dy) % SIDE) * SIDE + (x + dx) % SIDE
        return ((y + SIDE - dy) % SIDE) * SIDE + (x + SIDE - dx) % SIDE

    def hops(offset):
        dy, dx = offset // SIDE, offset % SIDE
        return min(dy, SIDE - dy) + min(dx, SIDE - dx)

    offsets = sorted(range(1, PLACES), key=lambda o: -hops(o))

    def local(source, target, index):
        return pltpu.make_async_copy(source, target, local_sem.at[index])

    hidden_load = local(hidden, hidden_v, 0)
    tile_load = local(tile.at[0], tile_v.at[h], 1)
    positions_load = local(positions, positions_s, 2)
    query_load = local(queries, query_v, 3)
    cache_load = local(cache.at[0], cache_v, 4)
    gain_load = local(gain, gain_v, 5)
    weight_load = local(weight, weight_v, 6)
    hidden_load.start()

    barrier = pltpu.get_barrier_semaphore()

    def signal(semaphore, where):
        pl.semaphore_signal(semaphore, inc=1, device_id=where, device_id_type=MESH)

    for group in range(GROUPS):
        @pl.when(h == group)
        def _():
            for later in GREETED[group]:
                signal(barrier, in_z(later))

    for t in range(1, TP):
        @pl.when(t > tp)
        def _():
            signal(barrier, in_tp(t))

    for p in range(1, PLACES):
        @pl.when(p > place)
        def _():
            signal(barrier, in_plane(p))

    valid = jnp.where(counts[0, 0] > 0, 1.0, 0.0)
    is_key = jnp.where(blocks[0, 0] % 2 == 0, 1.0, 0.0)
    flag_v[h] = jnp.concatenate(
        [jnp.full((1, 128), valid * is_key, F32), jnp.full((1, 128), valid * (1.0 - is_key), F32)], axis=0
    )

    @pl.when(place + tp + greetings > 0)
    def _():
        pl.semaphore_wait(barrier, place + tp + greetings)


    def tile_copy(source, group, number):
        return pltpu.make_async_remote_copy(
            src_ref=tile.at[0] if source is None else tile_v.at[source],
            dst_ref=tile_v.at[h if source is None else source],
            send_sem=tile_send_sem.at[number],
            recv_sem=tile_recv_sem.at[h if source is None else source],
            device_id=in_z(group),
            device_id_type=MESH,
        )

    def flag_copy(source, group, number):
        slot = h if source is None else source
        return pltpu.make_async_remote_copy(
            src_ref=flag_v.at[slot],
            dst_ref=flag_v.at[slot],
            send_sem=flag_send_sem.at[number],
            recv_sem=flag_recv_sem.at[slot],
            device_id=in_z(group),
            device_id_type=MESH,
        )

    def tile_start(source, group, number):
        tile_copy(source, group, number).start()
        flag_copy(source, group, number).start()

    def arrive(group):
        pltpu.make_async_copy(tile_v.at[group], tile_v.at[group], tile_recv_sem.at[group]).wait()
        pltpu.make_async_copy(flag_v.at[group], flag_v.at[group], flag_recv_sem.at[group]).wait()

    @pl.when(h > 0)
    def _():
        tile_start(None, 0, 0)

        signal(z_ready.at[h], in_z(0))

        @pl.when(h == 2)
        def _():
            signal(z_ready.at[h], in_z(1))

    for t in range(TP - 1):
        @pl.when(t < tp)
        def _():
            signal(tp_ready, in_tp(t))

    for p in range(PLACES - 1):
        @pl.when(p < place)
        def _():
            signal(plane_ready, in_plane(p))

    gain_load.start()
    query_load.start()
    positions_load.start()
    cache_load.start()
    tile_load.start()
    weight_load.start()

    hidden_load.wait()
    mine = jnp.concatenate([hidden_v[0, 0].astype(F32), hidden_v[0, 1].astype(F32)], axis=0)
    all_v[tp] = jnp.concatenate([mine[:, :512], mine[:, 512:]], axis=0).astype(BF16)

    def hidden_copy(t):
        return pltpu.make_async_remote_copy(
            src_ref=all_v.at[tp],
            dst_ref=all_v.at[tp],
            send_sem=hid_send_sem.at[t],
            recv_sem=hid_recv_sem.at[tp],
            device_id=in_tp(t),
            device_id_type=MESH,
        )

    for t in range(TP - 1):
        @pl.when(t < tp)
        def _():
            hidden_copy(t).start()

    @pl.when(tp < TP - 1)
    def _():
        pl.semaphore_wait(tp_ready, TP - 1 - tp)

    for t in range(TP - 1, 0, -1):
        @pl.when(t > tp)
        def _():
            hidden_copy(t).start()

    query_load.wait()
    positions_load.wait()
    all_queries = jnp.concatenate([query_v[0, 0].astype(F32), query_v[0, 1].astype(F32)], axis=0)
    heads = all_queries.shape[1] // 128
    query = jnp.concatenate([all_queries[:, i * 128 : i * 128 + 128] for i in range(heads)], axis=0).astype(BF16)
    rows = heads * ROWS
    cache_load.wait()
    length = cache_v.shape[1]
    row = lax.broadcasted_iota(jnp.int32, (rows, length), 0)
    column = lax.broadcasted_iota(jnp.int32, (rows, length), 1)
    sequence = row % 4
    scores = jnp.zeros((rows, length), F32)
    filled = jnp.zeros((rows, length), jnp.int32)
    for r in range(4):
        keys = cache_v[r, :, :128]
        product = lax.dot_general(query, keys, (((1,), (1,)), ((), ())), preferred_element_type=F32)
        scores = jnp.where(sequence == r, product, scores)
        filled = jnp.where(sequence == r, positions_s[0, r], filled)
    scale = 128 ** (-0.5)
    scores = jnp.where(column < filled, scores * scale, -1e30)
    old_peak = jnp.max(scores, axis=-1, keepdims=True)
    raised = jnp.exp(scores - old_peak)
    old_sum = jnp.sum(raised, axis=-1, keepdims=True)
    old_mixed = jnp.zeros((rows, 128), F32)
    for r in range(4):
        chosen = jnp.where(sequence == r, raised, 0.0).astype(BF16)
        old_mixed = old_mixed + jnp.dot(chosen, cache_v[r, :, 128:], preferred_element_type=F32)

    token = lax.broadcasted_iota(jnp.int32, (ROWS, 128), 0)
    lane = lax.broadcasted_iota(jnp.int32, (ROWS, 128), 1)
    moment = token // 4
    for r in range(4):
        moment = jnp.where(token % 4 == r, token // 4 + positions_s[0, r], moment)
    inverse = jnp.exp((lane % 64).astype(F32) * (-2.0 * math.log(THETA) / 128))
    angle = moment.astype(F32) * inverse
    cosine = jnp.cos(angle)
    sine = jnp.where(lane < 64, -1.0, 1.0) * jnp.sin(angle)

    @pl.when(h == 0)
    def _():
        pl.semaphore_wait(z_ready.at[1], 1)
        tile_start(None, 1, 0)

    @pl.when(h == 1)
    def _():
        pl.semaphore_wait(z_ready.at[2], 1)
        tile_start(None, 2, 1)
        arrive(0)
        tile_start(0, 2, 2)
        pl.semaphore_wait(z_ready.at[3], 1)
        signal(z_ready.at[3], in_z(2))

    @pl.when(h == 2)
    def _():
        tile_start(None, 1, 1)

    @pl.when(h == 3)
    def _():
        pl.semaphore_wait(z_ready.at[1], 1)
        tile_start(None, 1, 1)

    for t in range(TP):
        @pl.when(t != tp)
        def _():
            pltpu.make_async_copy(all_v.at[t], all_v.at[t], hid_recv_sem.at[t]).wait()

    squares = jnp.zeros((ROWS, 128), F32)
    for t in range(TP):
        piece = all_v[t].astype(F32)
        for b in range(8):
            part = piece[(b // 4) * 8 : (b // 4) * 8 + 8, (b % 4) * 128 : (b % 4) * 128 + 128]
            squares = squares + part * part
    rate = lax.rsqrt(jnp.sum(squares, axis=-1, keepdims=True) / 8192.0 + EPS)
    rate = jnp.broadcast_to(rate, (ROWS, 128))
    gain_load.wait()
    gains = gain_v[...].astype(F32)
    normed = []
    for t in range(TP):
        piece = all_v[t].astype(F32)
        for b in range(8):
            part = piece[(b // 4) * 8 : (b // 4) * 8 + 8, (b % 4) * 128 : (b % 4) * 128 + 128]
            normed.append(part * rate * gains[t * 8 + b : t * 8 + b + 1])
    for p in range(PLACES):
        give_v[p] = jnp.concatenate([normed[group * 16 + p] for group in range(GROUPS)], axis=0).astype(BF16)

    def give_copy(number):
        there = neighbour(offsets[number], 1)
        return pltpu.make_async_remote_copy(
            src_ref=give_v.at[there],
            dst_ref=got_v.at[place],
            send_sem=give_send_sem.at[number],
            recv_sem=give_recv_sem.at[place],
            device_id=in_plane(there),
            device_id_type=MESH,
        )

    @pl.when(place < PLACES - 1)
    def _():
        pl.semaphore_wait(plane_ready, PLACES - 1 - place)

    for number in range(PLACES - 1):
        give_copy(number).start()
    got_v[place] = give_v[place]

    first = jnp.where((h == 0) | (h == 2), 1, 0)
    second = jnp.where(h == 0, 3, jnp.where(h == 1, 2, jnp.where(h == 2, 0, 1)))
    third = jnp.where((h == 0) | (h == 3), 2, 3)

    @pl.when(h == 0)
    def _():
        pl.semaphore_wait(z_ready.at[3], 1)
        signal(z_ready.at[1], in_z(3))
        signal(z_ready.at[3], in_z(1))
        tile_start(None, 3, 1)

    @pl.when(h == 2)
    def _():
        pl.semaphore_wait(z_ready.at[3], 1)
        tile_start(None, 3, 2)

    @pl.when(h != 1)
    def _():
        arrive(first)

    @pl.when(h == 0)
    def _():
        tile_start(1, 3, 2)

    for t in range(TP):
        x_v[t] = jnp.concatenate(normed[t * 8 : t * 8 + 8], axis=1).astype(BF16)
    weight_load.wait()

    def project(t, total):
        rows_of = weight_v[pl.ds(pl.multiple_of(t * 1024, 1024), 1024)]
        return total + jnp.dot(x_v[t], rows_of, preferred_element_type=F32)

    base = lax.fori_loop(0, TP, project, jnp.zeros((ROWS, 256), F32))

    @pl.when(h == 0)
    def _():
        pl.semaphore_wait(z_ready.at[2], 1)
        signal(z_ready.at[2], in_z(3))

    @pl.when(h == 3)
    def _():
        pl.semaphore_wait(z_ready.at[2], 1)
        tile_start(None, 2, 2)

    arrive(second)

    for number in range(PLACES - 1):
        there = neighbour(offsets[number], -1)
        pltpu.make_async_copy(got_v.at[there], got_v.at[there], give_recv_sem.at[there]).wait()
    for p in range(0, PLACES, 2):
        even, odd = got_v[p].astype(F32), got_v[p + 1].astype(F32)
        for group in range(GROUPS):
            xh_v[group, p * 8 : p * 8 + 16] = jnp.concatenate(
                [even[group * 8 : group * 8 + 8], odd[group * 8 : group * 8 + 8]], axis=0
            ).astype(BF16)

    def multiply(group, key_part, value_part):
        product = jnp.dot(xh_v[group], tile_v[group], preferred_element_type=F32)
        flags = flag_v[group]
        return key_part + product * flags[0:1], value_part + product * flags[1:2]

    blank = jnp.zeros((PLACES * ROWS, 128), F32)
    tile_load.wait()
    key_part, value_part = multiply(h, blank, blank)
    key_part, value_part = multiply(first, key_part, value_part)
    key_part, value_part = multiply(second, key_part, value_part)
    arrive(third)

    key_part, value_part = multiply(third, key_part, value_part)

    def ret_copy(number):
        there = neighbour(offsets[number], 1)
        return pltpu.make_async_remote_copy(
            src_ref=ret_send.at[there],
            dst_ref=ret_recv.at[place],
            send_sem=ret_send_sem.at[number],
            recv_sem=ret_recv_sem.at[place],
            device_id=in_plane(there),
            device_id_type=MESH,
        )

    for p in range(PLACES):
        ret_send[p] = jnp.concatenate([key_part[p * 8 : p * 8 + 8], value_part[p * 8 : p * 8 + 8]], axis=0).astype(BF16)
    for number in range(PLACES - 1):
        ret_copy(number).start()

    total = ret_send[place].astype(F32)
    for number in range(PLACES - 2, -1, -1):
        there = neighbour(offsets[number], -1)
        pltpu.make_async_copy(ret_recv.at[there], ret_recv.at[there], ret_recv_sem.at[there]).wait()
        total = total + ret_recv[there].astype(F32)
    new_keys = base[:, :128] + total[:8]
    new_values = base[:, 128:] + total[8:]

    rotated = new_keys * cosine + pltpu.roll(new_keys, 64, 1) * sine
    new_entries = jnp.concatenate([rotated, new_values], axis=1)
    entries_out[0, 0] = new_entries[:4].astype(BF16)
    entries_out[0, 1] = new_entries[4:].astype(BF16)

    empty = jnp.zeros((ROWS, 128), F32)
    fresh_keys = jnp.concatenate([rotated, empty], axis=0).astype(BF16)
    fresh_values = jnp.concatenate([new_values, empty], axis=0).astype(BF16)
    new_scores = lax.dot_general(query, fresh_keys, (((1,), (1,)), ((), ())), preferred_element_type=F32)
    new_row = lax.broadcasted_iota(jnp.int32, (rows, 16), 0)
    new_column = lax.broadcasted_iota(jnp.int32, (rows, 16), 1)
    seen = (
        (new_column < 8) & (new_column % 4 == new_row % 4) & (new_column // 4 <= (new_row // 4) % 2)
    )
    new_scores = jnp.where(seen, new_scores * scale, -1e30)
    peak = jnp.maximum(old_peak, jnp.max(new_scores, axis=-1, keepdims=True))
    new_raised = jnp.exp(new_scores - peak)
    shrink = jnp.exp(old_peak - peak)
    all_sum = old_sum * shrink + jnp.sum(new_raised, axis=-1, keepdims=True)
    mixed = old_mixed * shrink + jnp.dot(new_raised.astype(BF16), fresh_values, preferred_element_type=F32)
    mixed = mixed / all_sum
    wide = jnp.concatenate([mixed[i * 8 : i * 8 + 8] for i in range(heads)], axis=1)
    attended_out[0, 0] = wide[:4].astype(BF16)
    attended_out[0, 1] = wide[4:].astype(BF16)

    for t in range(TP):
        @pl.when(t != tp)
        def _():
            hidden_copy(t).wait_send()

    for number in range(GROUPS - 1):
        tile_copy(None, 0, number).wait_send()
        flag_copy(None, 0, number).wait_send()

    for number in range(PLACES - 1):
        give_copy(number).wait_send()
        ret_copy(number).wait_send()


def shards(hidden, norm_gain, kv_weight, delta_tiles, tile_blocks, tile_counts, queries, kv_cache, positions):
    def hbm(array):
        return pltpu.with_memory_space_constraint(array, pltpu.HBM)

    anywhere = pl.BlockSpec(memory_space=pltpu.HBM)
    scalar = pl.BlockSpec(memory_space=pltpu.SMEM)
    vmem = pl.BlockSpec(memory_space=pltpu.VMEM)
    dma = pltpu.SemaphoreType.DMA
    regular = pltpu.SemaphoreType.REGULAR
    return pl.pallas_call(
        kernel,
        out_shape=(
            jax.ShapeDtypeStruct((1, 2, 4, 256), BF16),
            jax.ShapeDtypeStruct((1, 2, 4, 1024), BF16),
        ),
        in_specs=[anywhere] * 4 + [scalar] * 2 + [anywhere] * 3,
        out_specs=(vmem, vmem),
        scratch_shapes=[
            pltpu.VMEM((1, 2, 4, 1024), BF16),
            pltpu.VMEM((TP, 16, 512), BF16),
            pltpu.VMEM((TP, ROWS, 1024), BF16),
            pltpu.VMEM((PLACES, 32, 128), BF16),
            pltpu.VMEM((PLACES, 32, 128), BF16),
            pltpu.VMEM((GROUPS, 128, 128), BF16),
            pltpu.VMEM((GROUPS, 128, 128), BF16),
            pltpu.VMEM((GROUPS, 2, 128), F32),
            pltpu.VMEM((8192, 256), BF16),
            pltpu.VMEM((64, 128), BF16),
            pltpu.VMEM((1, 2, 4, 1024), BF16),
            pltpu.VMEM((4, 256, 256), BF16),
            pltpu.VMEM((PLACES, 16, 128), BF16),
            pltpu.VMEM((PLACES, 16, 128), BF16),
            pltpu.SMEM((1, 4), jnp.int32),
            dma((7,)),
            regular,
            regular,
            regular((GROUPS,)),
            dma((TP,)),
            dma((TP,)),
            dma((PLACES - 1,)),
            dma((PLACES,)),
            dma((GROUPS - 1,)),
            dma((GROUPS,)),
            dma((GROUPS - 1,)),
            dma((GROUPS,)),
            dma((PLACES - 1,)),
            dma((PLACES,)),
        ],
        compiler_params=pltpu.CompilerParams(
            collective_id=0, has_side_effects=True, vmem_limit_bytes=24 * 1024 * 1024
        ),
    )(
        hbm(hidden),
        hbm(norm_gain.reshape(64, 128)),
        hbm(kv_weight),
        hbm(delta_tiles),
        tile_blocks,
        tile_counts,
        hbm(queries),
        hbm(kv_cache),
        hbm(positions),
    )


def solution(mesh):
    return jax.shard_map(
        shards,
        mesh=mesh,
        in_specs=(
            P("rep", None, None, "tp"),
            P(),
            P(None, "tp"),
            P("rep", None, "tp"),
            P("rep", "tp"),
            P("rep", "tp"),
            P("rep", None, None, "tp"),
            P("rep", None, None, "tp"),
            P("rep", None),
        ),
        out_specs=(P("rep", None, None, "tp"), P("rep", None, None, "tp")),
        check_vma=False,
    )
```

```python
import math

import jax
import jax.numpy as jnp
from jax import lax
from jax.experimental import pallas as pl
from jax.experimental.pallas import tpu as pltpu
from jax.sharding import PartitionSpec as P

EPS = 1e-06
THETA = 1000000.0
F32 = jnp.float32
BF16 = jnp.bfloat16
MESH = pl.DeviceIdType.MESH

GROUPS = 4
PLACES = 16
SIDE = 4
TP = 8
ROWS = 8
GREETED = {0: (2, 3, 1), 1: (2,), 2: (), 3: ()}


def kernel(
    hidden,
    gain,
    weight,
    tile,
    blocks,
    counts,
    queries,
    cache,
    positions,
    entries_out,
    attended_out,
    hidden_v,
    all_v,
    x_v,
    give_v,
    got_v,
    xh_v,
    tile_v,
    flag_v,
    weight_v,
    gain_v,
    query_v,
    cache_v,
    ret_send,
    ret_recv,
    positions_s,
    local_sem,
    tp_ready,
    plane_ready,
    z_ready,
    hid_send_sem,
    hid_recv_sem,
    give_send_sem,
    give_recv_sem,
    tile_send_sem,
    tile_recv_sem,
    flag_send_sem,
    flag_recv_sem,
    ret_send_sem,
    ret_recv_sem,
):
    rep = lax.axis_index("rep")
    tp = lax.axis_index("tp")
    h, place = rep // PLACES, rep % PLACES
    y, x = place // SIDE, place % SIDE
    greetings = jnp.where(h == 2, 2, jnp.where(h == 0, 0, 1))

    def in_tp(t):
        return {"rep": rep, "tp": t}

    def in_plane(p):
        return {"rep": h * PLACES + p, "tp": tp}

    def in_z(group):
        return {"rep": group * PLACES + place, "tp": tp}

    def neighbour(offset, sign):
        dy, dx = offset // SIDE, offset % SIDE
        if sign > 0:
            return ((y + dy) % SIDE) * SIDE + (x + dx) % SIDE
        return ((y + SIDE - dy) % SIDE) * SIDE + (x + SIDE - dx) % SIDE

    def hops(offset):
        dy, dx = offset // SIDE, offset % SIDE
        return min(dy, SIDE - dy) + min(dx, SIDE - dx)

    offsets = sorted(range(1, PLACES), key=lambda o: -hops(o))

    def local(source, target, index):
        return pltpu.make_async_copy(source, target, local_sem.at[index])

    hidden_load = local(hidden, hidden_v, 0)
    tile_load = local(tile.at[0], tile_v.at[h], 1)
    positions_load = local(positions, positions_s, 2)
    query_load = local(queries, query_v, 3)
    cache_load = local(cache.at[0], cache_v, 4)
    gain_load = local(gain, gain_v, 5)
    weight_load = local(weight, weight_v, 6)
    hidden_load.start()

    barrier = pltpu.get_barrier_semaphore()

    def signal(semaphore, where):
        pl.semaphore_signal(semaphore, inc=1, device_id=where, device_id_type=MESH)

    for group in range(GROUPS):
        @pl.when(h == group)
        def _():
            for later in GREETED[group]:
                signal(barrier, in_z(later))

    for t in range(1, TP):
        @pl.when(t > tp)
        def _():
            signal(barrier, in_tp(t))

    for p in range(1, PLACES):
        @pl.when(p > place)
        def _():
            signal(barrier, in_plane(p))

    valid = jnp.where(counts[0, 0] > 0, 1.0, 0.0)
    is_key = jnp.where(blocks[0, 0] % 2 == 0, 1.0, 0.0)
    flag_v[h] = jnp.concatenate(
        [jnp.full((1, 128), valid * is_key, F32), jnp.full((1, 128), valid * (1.0 - is_key), F32)], axis=0
    )

    hidden_load.wait()
    mine = jnp.concatenate([hidden_v[0, 0].astype(F32), hidden_v[0, 1].astype(F32)], axis=0)
    all_v[tp] = jnp.concatenate([mine[:, :512], mine[:, 512:]], axis=0).astype(BF16)

    @pl.when(place + tp + greetings > 0)
    def _():
        pl.semaphore_wait(barrier, place + tp + greetings)


    def tile_copy(source, group, number):
        return pltpu.make_async_remote_copy(
            src_ref=tile.at[0] if source is None else tile_v.at[source],
            dst_ref=tile_v.at[h if source is None else source],
            send_sem=tile_send_sem.at[number],
            recv_sem=tile_recv_sem.at[h if source is None else source],
            device_id=in_z(group),
            device_id_type=MESH,
        )

    def flag_copy(source, group, number):
        slot = h if source is None else source
        return pltpu.make_async_remote_copy(
            src_ref=flag_v.at[slot],
            dst_ref=flag_v.at[slot],
            send_sem=flag_send_sem.at[number],
            recv_sem=flag_recv_sem.at[slot],
            device_id=in_z(group),
            device_id_type=MESH,
        )

    def tile_start(source, group, number):
        tile_copy(source, group, number).start()
        flag_copy(source, group, number).start()

    def arrive(group):
        pltpu.make_async_copy(tile_v.at[group], tile_v.at[group], tile_recv_sem.at[group]).wait()
        pltpu.make_async_copy(flag_v.at[group], flag_v.at[group], flag_recv_sem.at[group]).wait()

    @pl.when(h > 0)
    def _():
        tile_start(None, 0, 0)

        signal(z_ready.at[h], in_z(0))

        @pl.when(h == 2)
        def _():
            signal(z_ready.at[h], in_z(1))

    for t in range(TP - 1):
        @pl.when(t < tp)
        def _():
            signal(tp_ready, in_tp(t))


    def hidden_copy(t):
        return pltpu.make_async_remote_copy(
            src_ref=all_v.at[tp],
            dst_ref=all_v.at[tp],
            send_sem=hid_send_sem.at[t],
            recv_sem=hid_recv_sem.at[tp],
            device_id=in_tp(t),
            device_id_type=MESH,
        )

    def hidden_back():
        for t in range(TP - 1):
            @pl.when(t < tp)
            def _():
                hidden_copy(t).start()

    def hidden_on():
        @pl.when(tp < TP - 1)
        def _():
            pl.semaphore_wait(tp_ready, TP - 1 - tp)

        for t in range(TP - 1, 0, -1):
            @pl.when(t > tp)
            def _():
                hidden_copy(t).start()

    pl.when(h != 2)(hidden_back)
    for p in range(PLACES - 1):
        @pl.when(p < place)
        def _():
            signal(plane_ready, in_plane(p))

    gain_load.start()
    query_load.start()
    positions_load.start()
    cache_load.start()
    tile_load.start()
    weight_load.start()

    pl.when(h != 2)(hidden_on)
    query_load.wait()
    positions_load.wait()
    all_queries = jnp.concatenate([query_v[0, 0].astype(F32), query_v[0, 1].astype(F32)], axis=0)
    heads = all_queries.shape[1] // 128
    query = jnp.concatenate([all_queries[:, i * 128 : i * 128 + 128] for i in range(heads)], axis=0).astype(BF16)
    rows = heads * ROWS
    cache_load.wait()
    length = cache_v.shape[1]
    row = lax.broadcasted_iota(jnp.int32, (rows, length), 0)
    column = lax.broadcasted_iota(jnp.int32, (rows, length), 1)
    sequence = row % 4
    scores = jnp.zeros((rows, length), F32)
    filled = jnp.zeros((rows, length), jnp.int32)
    for r in range(4):
        keys = cache_v[r, :, :128]
        product = lax.dot_general(query, keys, (((1,), (1,)), ((), ())), preferred_element_type=F32)
        scores = jnp.where(sequence == r, product, scores)
        filled = jnp.where(sequence == r, positions_s[0, r], filled)
    scale = 128 ** (-0.5)
    scores = jnp.where(column < filled, scores * scale, -1e30)
    old_peak = jnp.max(scores, axis=-1, keepdims=True)
    raised = jnp.exp(scores - old_peak)
    old_sum = jnp.sum(raised, axis=-1, keepdims=True)
    old_mixed = jnp.zeros((rows, 128), F32)
    for r in range(4):
        chosen = jnp.where(sequence == r, raised, 0.0).astype(BF16)
        old_mixed = old_mixed + jnp.dot(chosen, cache_v[r, :, 128:], preferred_element_type=F32)

    token = lax.broadcasted_iota(jnp.int32, (ROWS, 128), 0)
    lane = lax.broadcasted_iota(jnp.int32, (ROWS, 128), 1)
    moment = token // 4
    for r in range(4):
        moment = jnp.where(token % 4 == r, token // 4 + positions_s[0, r], moment)
    inverse = jnp.exp((lane % 64).astype(F32) * (-2.0 * math.log(THETA) / 128))
    angle = moment.astype(F32) * inverse
    cosine = jnp.cos(angle)
    sine = jnp.where(lane < 64, -1.0, 1.0) * jnp.sin(angle)

    @pl.when(h == 2)
    def _():
        hidden_back()
        hidden_on()

    @pl.when(h == 0)
    def _():
        pl.semaphore_wait(z_ready.at[1], 1)
        tile_start(None, 1, 0)
        pl.semaphore_wait(z_ready.at[3], 1)
        signal(z_ready.at[1], in_z(3))
        signal(z_ready.at[3], in_z(1))
        tile_start(None, 3, 1)

    @pl.when(h == 1)
    def _():
        pl.semaphore_wait(z_ready.at[2], 1)
        tile_start(None, 2, 1)
        arrive(0)
        tile_start(0, 2, 2)
        pl.semaphore_wait(z_ready.at[3], 1)
        signal(z_ready.at[3], in_z(2))

    @pl.when(h == 2)
    def _():
        tile_start(None, 1, 1)

    @pl.when(h == 3)
    def _():
        pl.semaphore_wait(z_ready.at[1], 1)
        tile_start(None, 1, 1)

    for t in range(TP):
        @pl.when(t != tp)
        def _():
            pltpu.make_async_copy(all_v.at[t], all_v.at[t], hid_recv_sem.at[t]).wait()

    squares = jnp.zeros((ROWS, 128), F32)
    for t in range(TP):
        piece = all_v[t].astype(F32)
        for b in range(8):
            part = piece[(b // 4) * 8 : (b // 4) * 8 + 8, (b % 4) * 128 : (b % 4) * 128 + 128]
            squares = squares + part * part
    rate = lax.rsqrt(jnp.sum(squares, axis=-1, keepdims=True) / 8192.0 + EPS)
    rate = jnp.broadcast_to(rate, (ROWS, 128))
    gain_load.wait()
    gains = gain_v[...].astype(F32)
    normed = []
    for t in range(TP):
        piece = all_v[t].astype(F32)
        for b in range(8):
            part = piece[(b // 4) * 8 : (b // 4) * 8 + 8, (b % 4) * 128 : (b % 4) * 128 + 128]
            normed.append(part * rate * gains[t * 8 + b : t * 8 + b + 1])
    for p in range(PLACES):
        give_v[p] = jnp.concatenate([normed[group * 16 + p] for group in range(GROUPS)], axis=0).astype(BF16)

    def give_copy(number):
        there = neighbour(offsets[number], 1)
        return pltpu.make_async_remote_copy(
            src_ref=give_v.at[there],
            dst_ref=got_v.at[place],
            send_sem=give_send_sem.at[number],
            recv_sem=give_recv_sem.at[place],
            device_id=in_plane(there),
            device_id_type=MESH,
        )

    @pl.when(place < PLACES - 1)
    def _():
        pl.semaphore_wait(plane_ready, PLACES - 1 - place)

    for number in range(PLACES - 1):
        give_copy(number).start()
    got_v[place] = give_v[place]

    first = jnp.where((h == 0) | (h == 2), 1, 0)
    second = jnp.where(h == 0, 3, jnp.where(h == 1, 2, jnp.where(h == 2, 0, 1)))
    third = jnp.where((h == 0) | (h == 3), 2, 3)

    @pl.when(h == 2)
    def _():
        pl.semaphore_wait(z_ready.at[3], 1)
        tile_start(None, 3, 2)

    @pl.when(h == 3)
    def _():
        pl.semaphore_wait(z_ready.at[2], 1)
        tile_start(None, 2, 2)

    @pl.when(h != 1)
    def _():
        arrive(first)

    @pl.when(h == 0)
    def _():
        tile_start(1, 3, 2)

    for t in range(TP):
        x_v[t] = jnp.concatenate(normed[t * 8 : t * 8 + 8], axis=1).astype(BF16)
    weight_load.wait()

    def project(t, total):
        rows_of = weight_v[pl.ds(pl.multiple_of(t * 1024, 1024), 1024)]
        return total + jnp.dot(x_v[t], rows_of, preferred_element_type=F32)

    base = lax.fori_loop(0, TP, project, jnp.zeros((ROWS, 256), F32))

    @pl.when(h == 0)
    def _():
        pl.semaphore_wait(z_ready.at[2], 1)
        signal(z_ready.at[2], in_z(3))

    arrive(second)

    for number in range(PLACES - 1):
        there = neighbour(offsets[number], -1)
        pltpu.make_async_copy(got_v.at[there], got_v.at[there], give_recv_sem.at[there]).wait()
    for p in range(0, PLACES, 2):
        even, odd = got_v[p].astype(F32), got_v[p + 1].astype(F32)
        for group in range(GROUPS):
            xh_v[group, p * 8 : p * 8 + 16] = jnp.concatenate(
                [even[group * 8 : group * 8 + 8], odd[group * 8 : group * 8 + 8]], axis=0
            ).astype(BF16)

    def multiply(group, key_part, value_part):
        product = jnp.dot(xh_v[group], tile_v[group], preferred_element_type=F32)
        flags = flag_v[group]
        return key_part + product * flags[0:1], value_part + product * flags[1:2]

    blank = jnp.zeros((PLACES * ROWS, 128), F32)
    tile_load.wait()
    key_part, value_part = multiply(h, blank, blank)
    key_part, value_part = multiply(first, key_part, value_part)
    key_part, value_part = multiply(second, key_part, value_part)
    arrive(third)

    key_part, value_part = multiply(third, key_part, value_part)

    def ret_copy(number):
        there = neighbour(offsets[number], 1)
        return pltpu.make_async_remote_copy(
            src_ref=ret_send.at[there],
            dst_ref=ret_recv.at[place],
            send_sem=ret_send_sem.at[number],
            recv_sem=ret_recv_sem.at[place],
            device_id=in_plane(there),
            device_id_type=MESH,
        )

    for p in range(PLACES):
        ret_send[p] = jnp.concatenate([key_part[p * 8 : p * 8 + 8], value_part[p * 8 : p * 8 + 8]], axis=0).astype(BF16)
    for number in range(PLACES - 1):
        ret_copy(number).start()

    total = ret_send[place].astype(F32)
    for number in range(PLACES - 2, -1, -1):
        there = neighbour(offsets[number], -1)
        pltpu.make_async_copy(ret_recv.at[there], ret_recv.at[there], ret_recv_sem.at[there]).wait()
        total = total + ret_recv[there].astype(F32)
    new_keys = base[:, :128] + total[:8]
    new_values = base[:, 128:] + total[8:]

    rotated = new_keys * cosine + pltpu.roll(new_keys, 64, 1) * sine
    new_entries = jnp.concatenate([rotated, new_values], axis=1)
    entries_out[0, 0] = new_entries[:4].astype(BF16)
    entries_out[0, 1] = new_entries[4:].astype(BF16)

    empty = jnp.zeros((ROWS, 128), F32)
    fresh_keys = jnp.concatenate([rotated, empty], axis=0).astype(BF16)
    fresh_values = jnp.concatenate([new_values, empty], axis=0).astype(BF16)
    new_scores = lax.dot_general(query, fresh_keys, (((1,), (1,)), ((), ())), preferred_element_type=F32)
    new_row = lax.broadcasted_iota(jnp.int32, (rows, 16), 0)
    new_column = lax.broadcasted_iota(jnp.int32, (rows, 16), 1)
    seen = (
        (new_column < 8) & (new_column % 4 == new_row % 4) & (new_column // 4 <= (new_row // 4) % 2)
    )
    new_scores = jnp.where(seen, new_scores * scale, -1e30)
    peak = jnp.maximum(old_peak, jnp.max(new_scores, axis=-1, keepdims=True))
    new_raised = jnp.exp(new_scores - peak)
    shrink = jnp.exp(old_peak - peak)
    all_sum = old_sum * shrink + jnp.sum(new_raised, axis=-1, keepdims=True)
    mixed = old_mixed * shrink + jnp.dot(new_raised.astype(BF16), fresh_values, preferred_element_type=F32)
    mixed = mixed / all_sum
    wide = jnp.concatenate([mixed[i * 8 : i * 8 + 8] for i in range(heads)], axis=1)
    attended_out[0, 0] = wide[:4].astype(BF16)
    attended_out[0, 1] = wide[4:].astype(BF16)

    for t in range(TP):
        @pl.when(t != tp)
        def _():
            hidden_copy(t).wait_send()

    for number in range(GROUPS - 1):
        tile_copy(None, 0, number).wait_send()
        flag_copy(None, 0, number).wait_send()

    for number in range(PLACES - 1):
        give_copy(number).wait_send()
        ret_copy(number).wait_send()


def hand_over(entries, attended, entries_out, attended_out, sem):
    copies = (
        pltpu.make_async_copy(entries, entries_out, sem.at[0]),
        pltpu.make_async_copy(attended, attended_out, sem.at[1]),
    )
    for copy in copies:
        copy.start()
    for copy in copies:
        copy.wait()


def shards(hidden, norm_gain, kv_weight, delta_tiles, tile_blocks, tile_counts, queries, kv_cache, positions):
    def hbm(array):
        return pltpu.with_memory_space_constraint(array, pltpu.HBM)

    anywhere = pl.BlockSpec(memory_space=pltpu.HBM)
    scalar = pl.BlockSpec(memory_space=pltpu.SMEM)
    vmem = pl.BlockSpec(memory_space=pltpu.VMEM)
    dma = pltpu.SemaphoreType.DMA
    regular = pltpu.SemaphoreType.REGULAR
    entries, attended = pl.pallas_call(
        kernel,
        out_shape=(
            jax.ShapeDtypeStruct((1, 2, 4, 256), BF16),
            jax.ShapeDtypeStruct((1, 2, 4, 1024), BF16),
        ),
        in_specs=[anywhere] * 4 + [scalar] * 2 + [anywhere] * 3,
        out_specs=(vmem, vmem),
        scratch_shapes=[
            pltpu.VMEM((1, 2, 4, 1024), BF16),
            pltpu.VMEM((TP, 16, 512), BF16),
            pltpu.VMEM((TP, ROWS, 1024), BF16),
            pltpu.VMEM((PLACES, 32, 128), BF16),
            pltpu.VMEM((PLACES, 32, 128), BF16),
            pltpu.VMEM((GROUPS, 128, 128), BF16),
            pltpu.VMEM((GROUPS, 128, 128), BF16),
            pltpu.VMEM((GROUPS, 2, 128), F32),
            pltpu.VMEM((8192, 256), BF16),
            pltpu.VMEM((64, 128), BF16),
            pltpu.VMEM((1, 2, 4, 1024), BF16),
            pltpu.VMEM((4, 256, 256), BF16),
            pltpu.VMEM((PLACES, 16, 128), BF16),
            pltpu.VMEM((PLACES, 16, 128), BF16),
            pltpu.SMEM((1, 4), jnp.int32),
            dma((7,)),
            regular,
            regular,
            regular((GROUPS,)),
            dma((TP,)),
            dma((TP,)),
            dma((PLACES - 1,)),
            dma((PLACES,)),
            dma((GROUPS - 1,)),
            dma((GROUPS,)),
            dma((GROUPS - 1,)),
            dma((GROUPS,)),
            dma((PLACES - 1,)),
            dma((PLACES,)),
        ],
        compiler_params=pltpu.CompilerParams(
            collective_id=0, has_side_effects=True, vmem_limit_bytes=24 * 1024 * 1024
        ),
    )(
        hbm(hidden),
        hbm(norm_gain.reshape(64, 128)),
        hbm(kv_weight),
        hbm(delta_tiles),
        tile_blocks,
        tile_counts,
        hbm(queries),
        hbm(kv_cache),
        hbm(positions),
    )
    return pl.pallas_call(
        hand_over,
        out_shape=(
            jax.ShapeDtypeStruct((1, 2, 4, 256), BF16),
            jax.ShapeDtypeStruct((1, 2, 4, 1024), BF16),
        ),
        in_specs=[vmem, vmem],
        out_specs=(anywhere, anywhere),
        scratch_shapes=[dma((2,))],
        compiler_params=pltpu.CompilerParams(vmem_limit_bytes=1024 * 1024),
    )(
        pltpu.with_memory_space_constraint(entries, pltpu.VMEM),
        pltpu.with_memory_space_constraint(attended, pltpu.VMEM),
    )


def solution(mesh):
    return jax.shard_map(
        shards,
        mesh=mesh,
        in_specs=(
            P("rep", None, None, "tp"),
            P(),
            P(None, "tp"),
            P("rep", None, "tp"),
            P("rep", "tp"),
            P("rep", "tp"),
            P("rep", None, None, "tp"),
            P("rep", None, None, "tp"),
            P("rep", None),
        ),
        out_specs=(P("rep", None, None, "tp"), P("rep", None, None, "tp")),
        check_vma=False,
    )
```

```python
import math

import jax
import jax.numpy as jnp
from jax import lax
from jax.experimental import pallas as pl
from jax.experimental.pallas import tpu as pltpu
from jax.sharding import PartitionSpec as P

EPS = 1e-06
THETA = 1000000.0
F32 = jnp.float32
BF16 = jnp.bfloat16
MESH = pl.DeviceIdType.MESH

GROUPS = 4
PLACES = 16
SIDE = 4
TP = 8
CHIPS = 4
ROWS = 8
GREETED = {0: (2, 3, 1), 1: (2,), 2: (), 3: ()}


def kernel(
    hidden,
    gain,
    weight,
    tile,
    blocks,
    counts,
    queries,
    cache,
    positions,
    entries_out,
    attended_out,
    hidden_v,
    all_v,
    x_v,
    give_v,
    got_v,
    xh_v,
    tile_v,
    flag_v,
    weight_v,
    gain_v,
    query_v,
    cache_v,
    ret_send,
    ret_recv,
    positions_s,
    local_sem,
    core_ready,
    tp_ready,
    plane_ready,
    z_ready,
    hid_send_sem,
    hid_recv_sem,
    core_send_sem,
    give_send_sem,
    give_recv_sem,
    tile_send_sem,
    tile_recv_sem,
    flag_send_sem,
    flag_recv_sem,
    ret_send_sem,
    ret_recv_sem,
):
    rep = lax.axis_index("rep")
    tp = lax.axis_index("tp")
    h, place = rep // PLACES, rep % PLACES
    l, c = tp // 2, tp % 2
    partner = {"rep": rep, "tp": tp + 1 - 2 * c}
    y, x = place // SIDE, place % SIDE
    greetings = jnp.where(h == 2, 2, jnp.where(h == 0, 0, 1))

    def in_chip(chip):
        return {"rep": rep, "tp": chip * 2 + c}

    def in_plane(p):
        return {"rep": h * PLACES + p, "tp": tp}

    def in_z(group):
        return {"rep": group * PLACES + place, "tp": tp}

    def neighbour(offset, sign):
        dy, dx = offset // SIDE, offset % SIDE
        if sign > 0:
            return ((y + dy) % SIDE) * SIDE + (x + dx) % SIDE
        return ((y + SIDE - dy) % SIDE) * SIDE + (x + SIDE - dx) % SIDE

    def hops(offset):
        dy, dx = offset // SIDE, offset % SIDE
        return min(dy, SIDE - dy) + min(dx, SIDE - dx)

    offsets = sorted(range(1, PLACES), key=lambda o: -hops(o))

    def local(source, target, index):
        return pltpu.make_async_copy(source, target, local_sem.at[index])

    hidden_load = local(hidden, hidden_v, 0)
    tile_load = local(tile.at[0], tile_v.at[h], 1)
    positions_load = local(positions, positions_s, 2)
    query_load = local(queries, query_v, 3)
    cache_load = local(cache.at[0], cache_v, 4)
    gain_load = local(gain, gain_v, 5)
    weight_load = local(weight, weight_v, 6)
    tile_load.start()
    hidden_load.start()

    barrier = pltpu.get_barrier_semaphore()

    def signal(semaphore, where):
        pl.semaphore_signal(semaphore, inc=1, device_id=where, device_id_type=MESH)

    for group in range(GROUPS):
        @pl.when(h == group)
        def _():
            for later in GREETED[group]:
                signal(barrier, in_z(later))

    @pl.when(c == 0)
    def _():
        signal(barrier, partner)

    for chip in range(1, CHIPS):
        @pl.when(chip > l)
        def _():
            signal(barrier, in_chip(chip))

    for p in range(1, PLACES):
        @pl.when(p > place)
        def _():
            signal(barrier, in_plane(p))

    valid = jnp.where(counts[0, 0] > 0, 1.0, 0.0)
    is_key = jnp.where(blocks[0, 0] % 2 == 0, 1.0, 0.0)
    flag_v[h] = jnp.concatenate(
        [jnp.full((1, 128), valid * is_key, F32), jnp.full((1, 128), valid * (1.0 - is_key), F32)], axis=0
    )

    @pl.when(place + l + c + greetings > 0)
    def _():
        pl.semaphore_wait(barrier, place + l + c + greetings)


    def tile_copy(source, group, number):
        return pltpu.make_async_remote_copy(
            src_ref=tile_v.at[h if source is None else source],
            dst_ref=tile_v.at[h if source is None else source],
            send_sem=tile_send_sem.at[number],
            recv_sem=tile_recv_sem.at[h if source is None else source],
            device_id=in_z(group),
            device_id_type=MESH,
        )

    def flag_copy(source, group, number):
        slot = h if source is None else source
        return pltpu.make_async_remote_copy(
            src_ref=flag_v.at[slot],
            dst_ref=flag_v.at[slot],
            send_sem=flag_send_sem.at[number],
            recv_sem=flag_recv_sem.at[slot],
            device_id=in_z(group),
            device_id_type=MESH,
        )

    def tile_start(source, group, number):
        tile_copy(source, group, number).start()
        flag_copy(source, group, number).start()

    def arrive(group):
        pltpu.make_async_copy(tile_v.at[group], tile_v.at[group], tile_recv_sem.at[group]).wait()
        pltpu.make_async_copy(flag_v.at[group], flag_v.at[group], flag_recv_sem.at[group]).wait()

    tile_load.wait()

    @pl.when((h == 1) | (h == 3))
    def _():
        signal(z_ready.at[h], in_z(0))
        pl.when(c == 0)(lambda: tile_start(None, 0, 0))

    @pl.when(h == 2)
    def _():
        pl.when(c == 0)(lambda: tile_start(None, 0, 0))
        signal(z_ready.at[h], in_z(1))
        signal(z_ready.at[h], in_z(0))

    @pl.when(c == 1)
    def _():
        signal(core_ready, partner)

    for chip in range(CHIPS - 1):
        @pl.when(chip < l)
        def _():
            signal(tp_ready, in_chip(chip))

    hidden_load.wait()
    mine = jnp.concatenate([hidden_v[0, 0].astype(F32), hidden_v[0, 1].astype(F32)], axis=0)
    all_v[tp] = jnp.concatenate([mine[:, :512], mine[:, 512:]], axis=0).astype(BF16)


    def hidden_copy(chip):
        return pltpu.make_async_remote_copy(
            src_ref=all_v.at[tp],
            dst_ref=all_v.at[tp],
            send_sem=hid_send_sem.at[chip],
            recv_sem=hid_recv_sem.at[tp],
            device_id=in_chip(chip),
            device_id_type=MESH,
        )

    def core_copy(chip):
        source = chip * 2 + c
        return pltpu.make_async_remote_copy(
            src_ref=all_v.at[source],
            dst_ref=all_v.at[source],
            send_sem=core_send_sem.at[chip],
            recv_sem=hid_recv_sem.at[source],
            device_id=partner,
            device_id_type=MESH,
        )

    def hidden_arrive(t):
        pltpu.make_async_copy(all_v.at[t], all_v.at[t], hid_recv_sem.at[t]).wait()

    def hidden_back():
        for chip in range(CHIPS - 1):
            @pl.when(chip < l)
            def _():
                hidden_copy(chip).start()

    def hidden_on():
        @pl.when(l < CHIPS - 1)
        def _():
            pl.semaphore_wait(tp_ready, CHIPS - 1 - l)

        for chip in range(CHIPS - 1, 0, -1):
            @pl.when(chip > l)
            def _():
                hidden_copy(chip).start()

        @pl.when(c == 0)
        def _():
            pl.semaphore_wait(core_ready, 1)

        core_copy(l).start()

    pl.when(h != 2)(hidden_back)
    for p in range(PLACES - 1):
        @pl.when(p < place)
        def _():
            signal(plane_ready, in_plane(p))

    gain_load.start()
    query_load.start()
    positions_load.start()
    cache_load.start()
    weight_load.start()

    pl.when((h != 0) & (c == 1))(lambda: tile_start(None, 0, 0))
    pl.when(h != 2)(hidden_on)
    query_load.wait()
    positions_load.wait()
    all_queries = jnp.concatenate([query_v[0, 0].astype(F32), query_v[0, 1].astype(F32)], axis=0)
    heads = all_queries.shape[1] // 128
    query = jnp.concatenate([all_queries[:, i * 128 : i * 128 + 128] for i in range(heads)], axis=0).astype(BF16)
    rows = heads * ROWS
    cache_load.wait()
    length = cache_v.shape[1]
    row = lax.broadcasted_iota(jnp.int32, (rows, length), 0)
    column = lax.broadcasted_iota(jnp.int32, (rows, length), 1)
    sequence = row % 4
    scores = jnp.zeros((rows, length), F32)
    filled = jnp.zeros((rows, length), jnp.int32)
    for r in range(4):
        keys = cache_v[r, :, :128]
        product = lax.dot_general(query, keys, (((1,), (1,)), ((), ())), preferred_element_type=F32)
        scores = jnp.where(sequence == r, product, scores)
        filled = jnp.where(sequence == r, positions_s[0, r], filled)
    scale = 128 ** (-0.5)
    scores = jnp.where(column < filled, scores * scale, -1e30)
    old_peak = jnp.max(scores, axis=-1, keepdims=True)
    raised = jnp.exp(scores - old_peak)
    old_sum = jnp.sum(raised, axis=-1, keepdims=True)
    old_mixed = jnp.zeros((rows, 128), F32)
    for r in range(4):
        chosen = jnp.where(sequence == r, raised, 0.0).astype(BF16)
        old_mixed = old_mixed + jnp.dot(chosen, cache_v[r, :, 128:], preferred_element_type=F32)

    token = lax.broadcasted_iota(jnp.int32, (ROWS, 128), 0)
    lane = lax.broadcasted_iota(jnp.int32, (ROWS, 128), 1)
    moment = token // 4
    for r in range(4):
        moment = jnp.where(token % 4 == r, token // 4 + positions_s[0, r], moment)
    inverse = jnp.exp((lane % 64).astype(F32) * (-2.0 * math.log(THETA) / 128))
    angle = moment.astype(F32) * inverse
    cosine = jnp.cos(angle)
    sine = jnp.where(lane < 64, -1.0, 1.0) * jnp.sin(angle)

    @pl.when(h == 2)
    def _():
        hidden_back()
        hidden_on()

    @pl.when(h == 0)
    def _():
        pl.semaphore_wait(z_ready.at[1], 1)
        tile_start(None, 1, 0)

    for chip in range(CHIPS):
        @pl.when(chip != l)
        def _():
            hidden_arrive(chip * 2 + c)
            core_copy(chip).start()

    @pl.when(h == 0)
    def _():
        pl.semaphore_wait(z_ready.at[3], 1)
        signal(z_ready.at[3], in_z(1))
        tile_start(None, 3, 1)

    @pl.when(h == 1)
    def _():
        pl.semaphore_wait(z_ready.at[2], 1)
        tile_start(None, 2, 1)

    @pl.when(h == 2)
    def _():
        tile_start(None, 1, 1)

    for chip in range(CHIPS):
        hidden_arrive(chip * 2 + 1 - c)

    squares = jnp.zeros((ROWS, 128), F32)
    for t in range(TP):
        piece = all_v[t].astype(F32)
        for b in range(8):
            part = piece[(b // 4) * 8 : (b // 4) * 8 + 8, (b % 4) * 128 : (b % 4) * 128 + 128]
            squares = squares + part * part
    rate = lax.rsqrt(jnp.sum(squares, axis=-1, keepdims=True) / 8192.0 + EPS)
    rate = jnp.broadcast_to(rate, (ROWS, 128))
    gain_load.wait()
    gains = gain_v[...].astype(F32)
    normed = []
    for t in range(TP):
        piece = all_v[t].astype(F32)
        for b in range(8):
            part = piece[(b // 4) * 8 : (b // 4) * 8 + 8, (b % 4) * 128 : (b % 4) * 128 + 128]
            normed.append(part * rate * gains[t * 8 + b : t * 8 + b + 1])
    for p in range(PLACES):
        give_v[p] = jnp.concatenate([normed[group * 16 + p] for group in range(GROUPS)], axis=0).astype(BF16)

    def give_copy(number):
        there = neighbour(offsets[number], 1)
        return pltpu.make_async_remote_copy(
            src_ref=give_v.at[there],
            dst_ref=got_v.at[place],
            send_sem=give_send_sem.at[number],
            recv_sem=give_recv_sem.at[place],
            device_id=in_plane(there),
            device_id_type=MESH,
        )

    @pl.when(place < PLACES - 1)
    def _():
        pl.semaphore_wait(plane_ready, PLACES - 1 - place)

    for number in range(PLACES - 1):
        give_copy(number).start()
    got_v[place] = give_v[place]

    @pl.when(h == 1)
    def _():
        pl.semaphore_wait(z_ready.at[3], 1)
        signal(z_ready.at[3], in_z(2))
        arrive(0)
        tile_start(0, 2, 2)

    first = jnp.where((h == 0) | (h == 2), 1, 0)
    second = jnp.where(h == 0, 3, jnp.where(h == 1, 2, jnp.where(h == 2, 0, 1)))
    third = jnp.where((h == 0) | (h == 3), 2, 3)

    @pl.when(h == 2)
    def _():
        pl.semaphore_wait(z_ready.at[3], 1)
        tile_start(None, 3, 2)

    @pl.when(h == 3)
    def _():
        pl.semaphore_wait(z_ready.at[2], 1)
        tile_start(None, 2, 1)

    @pl.when(h != 1)
    def _():
        arrive(first)

    @pl.when(h == 0)
    def _():
        tile_start(1, 3, 2)

    for t in range(TP):
        x_v[t] = jnp.concatenate(normed[t * 8 : t * 8 + 8], axis=1).astype(BF16)
    weight_load.wait()

    def project(t, total):
        rows_of = weight_v[pl.ds(pl.multiple_of(t * 1024, 1024), 1024)]
        return total + jnp.dot(x_v[t], rows_of, preferred_element_type=F32)

    base = lax.fori_loop(0, TP, project, jnp.zeros((ROWS, 256), F32))

    @pl.when(h == 0)
    def _():
        pl.semaphore_wait(z_ready.at[2], 1)
        signal(z_ready.at[2], in_z(3))

    arrive(second)
    pl.when(h == 0)(lambda: tile_start(3, 1, 3))

    for number in range(PLACES - 1):
        there = neighbour(offsets[number], -1)
        pltpu.make_async_copy(got_v.at[there], got_v.at[there], give_recv_sem.at[there]).wait()
    for p in range(0, PLACES, 2):
        even, odd = got_v[p].astype(F32), got_v[p + 1].astype(F32)
        for group in range(GROUPS):
            xh_v[group, p * 8 : p * 8 + 16] = jnp.concatenate(
                [even[group * 8 : group * 8 + 8], odd[group * 8 : group * 8 + 8]], axis=0
            ).astype(BF16)

    def multiply(group, key_part, value_part):
        product = jnp.dot(xh_v[group], tile_v[group], preferred_element_type=F32)
        flags = flag_v[group]
        return key_part + product * flags[0:1], value_part + product * flags[1:2]

    blank = jnp.zeros((PLACES * ROWS, 128), F32)
    key_part, value_part = multiply(h, blank, blank)
    key_part, value_part = multiply(first, key_part, value_part)
    key_part, value_part = multiply(second, key_part, value_part)
    arrive(third)

    key_part, value_part = multiply(third, key_part, value_part)

    def ret_copy(number):
        there = neighbour(offsets[number], 1)
        return pltpu.make_async_remote_copy(
            src_ref=ret_send.at[there],
            dst_ref=ret_recv.at[place],
            send_sem=ret_send_sem.at[number],
            recv_sem=ret_recv_sem.at[place],
            device_id=in_plane(there),
            device_id_type=MESH,
        )

    for p in range(PLACES):
        ret_send[p] = jnp.concatenate([key_part[p * 8 : p * 8 + 8], value_part[p * 8 : p * 8 + 8]], axis=0).astype(BF16)
    for number in range(PLACES - 1):
        ret_copy(number).start()

    total = ret_send[place].astype(F32)
    for number in range(PLACES - 2, -1, -1):
        there = neighbour(offsets[number], -1)
        pltpu.make_async_copy(ret_recv.at[there], ret_recv.at[there], ret_recv_sem.at[there]).wait()
        total = total + ret_recv[there].astype(F32)
    new_keys = base[:, :128] + total[:8]
    new_values = base[:, 128:] + total[8:]

    rotated = new_keys * cosine + pltpu.roll(new_keys, 64, 1) * sine
    new_entries = jnp.concatenate([rotated, new_values], axis=1)
    entries_out[0, 0] = new_entries[:4].astype(BF16)
    entries_out[0, 1] = new_entries[4:].astype(BF16)

    empty = jnp.zeros((ROWS, 128), F32)
    fresh_keys = jnp.concatenate([rotated, empty], axis=0).astype(BF16)
    fresh_values = jnp.concatenate([new_values, empty], axis=0).astype(BF16)
    new_scores = lax.dot_general(query, fresh_keys, (((1,), (1,)), ((), ())), preferred_element_type=F32)
    new_row = lax.broadcasted_iota(jnp.int32, (rows, 16), 0)
    new_column = lax.broadcasted_iota(jnp.int32, (rows, 16), 1)
    seen = (
        (new_column < 8) & (new_column % 4 == new_row % 4) & (new_column // 4 <= (new_row // 4) % 2)
    )
    new_scores = jnp.where(seen, new_scores * scale, -1e30)
    peak = jnp.maximum(old_peak, jnp.max(new_scores, axis=-1, keepdims=True))
    new_raised = jnp.exp(new_scores - peak)
    shrink = jnp.exp(old_peak - peak)
    all_sum = old_sum * shrink + jnp.sum(new_raised, axis=-1, keepdims=True)
    mixed = old_mixed * shrink + jnp.dot(new_raised.astype(BF16), fresh_values, preferred_element_type=F32)
    mixed = mixed / all_sum
    wide = jnp.concatenate([mixed[i * 8 : i * 8 + 8] for i in range(heads)], axis=1)
    attended_out[0, 0] = wide[:4].astype(BF16)
    attended_out[0, 1] = wide[4:].astype(BF16)

    for chip in range(CHIPS):
        @pl.when(chip != l)
        def _():
            hidden_copy(chip).wait_send()

        core_copy(chip).wait_send()

    for number in range(GROUPS):
        @pl.when((number < 2) | ((number == 2) & (h != 3)) | (h == 0))
        def _():
            tile_copy(None, 0, number).wait_send()
            flag_copy(None, 0, number).wait_send()

    for number in range(PLACES - 1):
        give_copy(number).wait_send()
        ret_copy(number).wait_send()


def hand_over(entries, attended, entries_out, attended_out, sem):
    copies = (
        pltpu.make_async_copy(entries, entries_out, sem.at[0]),
        pltpu.make_async_copy(attended, attended_out, sem.at[1]),
    )
    for copy in copies:
        copy.start()
    for copy in copies:
        copy.wait()


def shards(hidden, norm_gain, kv_weight, delta_tiles, tile_blocks, tile_counts, queries, kv_cache, positions):
    def hbm(array):
        return pltpu.with_memory_space_constraint(array, pltpu.HBM)

    anywhere = pl.BlockSpec(memory_space=pltpu.HBM)
    scalar = pl.BlockSpec(memory_space=pltpu.SMEM)
    vmem = pl.BlockSpec(memory_space=pltpu.VMEM)
    dma = pltpu.SemaphoreType.DMA
    regular = pltpu.SemaphoreType.REGULAR
    entries, attended = pl.pallas_call(
        kernel,
        out_shape=(
            jax.ShapeDtypeStruct((1, 2, 4, 256), BF16),
            jax.ShapeDtypeStruct((1, 2, 4, 1024), BF16),
        ),
        in_specs=[anywhere] * 4 + [scalar] * 2 + [anywhere] * 3,
        out_specs=(vmem, vmem),
        scratch_shapes=[
            pltpu.VMEM((1, 2, 4, 1024), BF16),
            pltpu.VMEM((TP, 16, 512), BF16),
            pltpu.VMEM((TP, ROWS, 1024), BF16),
            pltpu.VMEM((PLACES, 32, 128), BF16),
            pltpu.VMEM((PLACES, 32, 128), BF16),
            pltpu.VMEM((GROUPS, 128, 128), BF16),
            pltpu.VMEM((GROUPS, 128, 128), BF16),
            pltpu.VMEM((GROUPS, 2, 128), F32),
            pltpu.VMEM((8192, 256), BF16),
            pltpu.VMEM((64, 128), BF16),
            pltpu.VMEM((1, 2, 4, 1024), BF16),
            pltpu.VMEM((4, 256, 256), BF16),
            pltpu.VMEM((PLACES, 16, 128), BF16),
            pltpu.VMEM((PLACES, 16, 128), BF16),
            pltpu.SMEM((1, 4), jnp.int32),
            dma((7,)),
            regular,
            regular,
            regular,
            regular((GROUPS,)),
            dma((CHIPS,)),
            dma((TP,)),
            dma((CHIPS,)),
            dma((PLACES - 1,)),
            dma((PLACES,)),
            dma((GROUPS,)),
            dma((GROUPS,)),
            dma((GROUPS,)),
            dma((GROUPS,)),
            dma((PLACES - 1,)),
            dma((PLACES,)),
        ],
        compiler_params=pltpu.CompilerParams(
            collective_id=0, has_side_effects=True, vmem_limit_bytes=24 * 1024 * 1024
        ),
    )(
        hbm(hidden),
        hbm(norm_gain.reshape(64, 128)),
        hbm(kv_weight),
        hbm(delta_tiles),
        tile_blocks,
        tile_counts,
        hbm(queries),
        hbm(kv_cache),
        hbm(positions),
    )
    return pl.pallas_call(
        hand_over,
        out_shape=(
            jax.ShapeDtypeStruct((1, 2, 4, 256), BF16),
            jax.ShapeDtypeStruct((1, 2, 4, 1024), BF16),
        ),
        in_specs=[vmem, vmem],
        out_specs=(anywhere, anywhere),
        scratch_shapes=[dma((2,))],
        compiler_params=pltpu.CompilerParams(vmem_limit_bytes=1024 * 1024),
    )(
        pltpu.with_memory_space_constraint(entries, pltpu.VMEM),
        pltpu.with_memory_space_constraint(attended, pltpu.VMEM),
    )


def solution(mesh):
    return jax.shard_map(
        shards,
        mesh=mesh,
        in_specs=(
            P("rep", None, None, "tp"),
            P(),
            P(None, "tp"),
            P("rep", None, "tp"),
            P("rep", "tp"),
            P("rep", "tp"),
            P("rep", None, None, "tp"),
            P("rep", None, None, "tp"),
            P("rep", None),
        ),
        out_specs=(P("rep", None, None, "tp"), P("rep", None, None, "tp")),
        check_vma=False,
    )
```

```python
import math

import jax
import jax.numpy as jnp
from jax import lax
from jax.experimental import pallas as pl
from jax.experimental.pallas import tpu as pltpu
from jax.sharding import PartitionSpec as P

EPS = 1e-06
THETA = 1000000.0
F32 = jnp.float32
BF16 = jnp.bfloat16
MESH = pl.DeviceIdType.MESH

GROUPS = 4
PLACES = 16
SIDE = 4
TP = 8
CHIPS = 4
ROWS = 8
GREETED = {0: (2, 3, 1), 1: (2,), 2: (), 3: ()}


def kernel(
    hidden,
    gain,
    weight,
    tile,
    blocks,
    counts,
    queries,
    cache,
    positions,
    entries_out,
    attended_out,
    hidden_v,
    all_v,
    x_v,
    give_v,
    got_v,
    xh_v,
    tile_v,
    flag_v,
    weight_v,
    gain_v,
    query_v,
    cache_v,
    ret_send,
    ret_recv,
    positions_s,
    local_sem,
    core_ready,
    tp_ready,
    plane_ready,
    z_ready,
    hid_send_sem,
    hid_recv_sem,
    core_send_sem,
    give_send_sem,
    give_recv_sem,
    tile_send_sem,
    tile_recv_sem,
    flag_send_sem,
    flag_recv_sem,
    ret_send_sem,
    ret_recv_sem,
):
    rep = lax.axis_index("rep")
    tp = lax.axis_index("tp")
    h, place = rep // PLACES, rep % PLACES
    l, c = tp // 2, tp % 2
    partner = {"rep": rep, "tp": tp + 1 - 2 * c}
    y, x = place // SIDE, place % SIDE
    listens = (h == 2) & (l > 0) & (c == 1)
    greetings = jnp.where(h == 2, 2, jnp.where(h == 0, 0, 1)) + jnp.where(listens, jnp.where(l == 1, 4, 2), 0)

    def in_chip(chip):
        return {"rep": rep, "tp": chip * 2 + c}

    def in_plane(p):
        return {"rep": h * PLACES + p, "tp": tp}

    def in_z(group):
        return {"rep": group * PLACES + place, "tp": tp}

    def neighbour(offset, sign):
        dy, dx = offset // SIDE, offset % SIDE
        if sign > 0:
            return ((y + dy) % SIDE) * SIDE + (x + dx) % SIDE
        return ((y + SIDE - dy) % SIDE) * SIDE + (x + SIDE - dx) % SIDE

    def hops(offset):
        dy, dx = offset // SIDE, offset % SIDE
        return min(dy, SIDE - dy) + min(dx, SIDE - dx)

    offsets = sorted(range(1, PLACES), key=lambda o: -hops(o))

    def local(source, target, index):
        return pltpu.make_async_copy(source, target, local_sem.at[index])

    hidden_load = local(hidden, hidden_v, 0)
    tile_load = local(tile.at[0], tile_v.at[h], 1)
    positions_load = local(positions, positions_s, 2)
    query_load = local(queries, query_v, 3)
    cache_load = local(cache.at[0], cache_v, 4)
    gain_load = local(gain, gain_v, 5)
    weight_load = local(weight, weight_v, 6)
    tile_load.start()
    hidden_load.start()

    barrier = pltpu.get_barrier_semaphore()

    def signal(semaphore, where):
        pl.semaphore_signal(semaphore, inc=1, device_id=where, device_id_type=MESH)

    for group in range(GROUPS):
        @pl.when(h == group)
        def _():
            for later in GREETED[group]:
                signal(barrier, in_z(later))

    @pl.when(h == 3)
    def _():
        signal(barrier, {"rep": 2 * PLACES + place, "tp": jnp.where(l == 0, 1, l) * 2 + 1})

    @pl.when(c == 0)
    def _():
        signal(barrier, partner)

    for chip in range(1, CHIPS):
        @pl.when(chip > l)
        def _():
            signal(barrier, in_chip(chip))

    for p in range(1, PLACES):
        @pl.when(p > place)
        def _():
            signal(barrier, in_plane(p))

    valid = jnp.where(counts[0, 0] > 0, 1.0, 0.0)
    is_key = jnp.where(blocks[0, 0] % 2 == 0, 1.0, 0.0)
    flag_v[h] = jnp.concatenate(
        [jnp.full((1, 128), valid * is_key, F32), jnp.full((1, 128), valid * (1.0 - is_key), F32)], axis=0
    )

    @pl.when(place + l + c + greetings > 0)
    def _():
        pl.semaphore_wait(barrier, place + l + c + greetings)


    def tile_copy(source, group, number):
        return pltpu.make_async_remote_copy(
            src_ref=tile_v.at[h if source is None else source],
            dst_ref=tile_v.at[h if source is None else source],
            send_sem=tile_send_sem.at[number],
            recv_sem=tile_recv_sem.at[h if source is None else source],
            device_id=in_z(group),
            device_id_type=MESH,
        )

    def flag_copy(source, group, number):
        slot = h if source is None else source
        return pltpu.make_async_remote_copy(
            src_ref=flag_v.at[slot],
            dst_ref=flag_v.at[slot],
            send_sem=flag_send_sem.at[number],
            recv_sem=flag_recv_sem.at[slot],
            device_id=in_z(group),
            device_id_type=MESH,
        )

    def tile_start(source, group, number):
        tile_copy(source, group, number).start()
        flag_copy(source, group, number).start()

    def arrive(group):
        pltpu.make_async_copy(tile_v.at[group], tile_v.at[group], tile_recv_sem.at[group]).wait()
        pltpu.make_async_copy(flag_v.at[group], flag_v.at[group], flag_recv_sem.at[group]).wait()

    tile_load.wait()

    @pl.when((h == 1) | (h == 3))
    def _():
        signal(z_ready.at[h], in_z(0))
        pl.when(c == 0)(lambda: tile_start(None, 0, 0))

    @pl.when(h == 2)
    def _():
        pl.when(c == 0)(lambda: tile_start(None, 0, 0))
        signal(z_ready.at[h], in_z(1))
        pl.when(listens)(lambda: signal(z_ready.at[3], partner))
        pl.when(listens & (l == 1))(lambda: signal(z_ready.at[3], in_chip(0)))

    @pl.when(c == 1)
    def _():
        signal(core_ready, partner)

    for chip in range(CHIPS - 1):
        @pl.when(chip < l)
        def _():
            signal(tp_ready, in_chip(chip))

    hidden_load.wait()
    mine = jnp.concatenate([hidden_v[0, 0].astype(F32), hidden_v[0, 1].astype(F32)], axis=0)
    all_v[tp] = jnp.concatenate([mine[:, :512], mine[:, 512:]], axis=0).astype(BF16)


    def hidden_copy(chip):
        return pltpu.make_async_remote_copy(
            src_ref=all_v.at[tp],
            dst_ref=all_v.at[tp],
            send_sem=hid_send_sem.at[chip],
            recv_sem=hid_recv_sem.at[tp],
            device_id=in_chip(chip),
            device_id_type=MESH,
        )

    def core_copy(chip):
        source = chip * 2 + c
        return pltpu.make_async_remote_copy(
            src_ref=all_v.at[source],
            dst_ref=all_v.at[source],
            send_sem=core_send_sem.at[chip],
            recv_sem=hid_recv_sem.at[source],
            device_id=partner,
            device_id_type=MESH,
        )

    def hidden_arrive(t):
        pltpu.make_async_copy(all_v.at[t], all_v.at[t], hid_recv_sem.at[t]).wait()

    def hidden_back():
        for chip in range(CHIPS - 1):
            @pl.when(chip < l)
            def _():
                hidden_copy(chip).start()

    def hidden_on():
        @pl.when(l < CHIPS - 1)
        def _():
            pl.semaphore_wait(tp_ready, CHIPS - 1 - l)

        for chip in range(CHIPS - 1, 0, -1):
            @pl.when(chip > l)
            def _():
                hidden_copy(chip).start()

        @pl.when(c == 0)
        def _():
            pl.semaphore_wait(core_ready, 1)

        core_copy(l).start()

    pl.when(h != 2)(hidden_back)
    for p in range(PLACES - 1):
        @pl.when(p < place)
        def _():
            signal(plane_ready, in_plane(p))

    gain_load.start()
    query_load.start()
    positions_load.start()
    cache_load.start()
    weight_load.start()

    pl.when((h != 0) & (c == 1))(lambda: tile_start(None, 0, 0))
    pl.when(h != 2)(hidden_on)
    query_load.wait()
    positions_load.wait()
    all_queries = jnp.concatenate([query_v[0, 0].astype(F32), query_v[0, 1].astype(F32)], axis=0)
    heads = all_queries.shape[1] // 128
    query = jnp.concatenate([all_queries[:, i * 128 : i * 128 + 128] for i in range(heads)], axis=0).astype(BF16)
    rows = heads * ROWS
    cache_load.wait()
    length = cache_v.shape[1]
    row = lax.broadcasted_iota(jnp.int32, (rows, length), 0)
    column = lax.broadcasted_iota(jnp.int32, (rows, length), 1)
    sequence = row % 4
    scores = jnp.zeros((rows, length), F32)
    filled = jnp.zeros((rows, length), jnp.int32)
    for r in range(4):
        keys = cache_v[r, :, :128]
        product = lax.dot_general(query, keys, (((1,), (1,)), ((), ())), preferred_element_type=F32)
        scores = jnp.where(sequence == r, product, scores)
        filled = jnp.where(sequence == r, positions_s[0, r], filled)
    scale = 128 ** (-0.5)
    scores = jnp.where(column < filled, scores * scale, -1e30)
    old_peak = jnp.max(scores, axis=-1, keepdims=True)
    raised = jnp.exp(scores - old_peak)
    old_sum = jnp.sum(raised, axis=-1, keepdims=True)
    old_mixed = jnp.zeros((rows, 128), F32)
    for r in range(4):
        chosen = jnp.where(sequence == r, raised, 0.0).astype(BF16)
        old_mixed = old_mixed + jnp.dot(chosen, cache_v[r, :, 128:], preferred_element_type=F32)

    token = lax.broadcasted_iota(jnp.int32, (ROWS, 128), 0)
    lane = lax.broadcasted_iota(jnp.int32, (ROWS, 128), 1)
    moment = token // 4
    for r in range(4):
        moment = jnp.where(token % 4 == r, token // 4 + positions_s[0, r], moment)
    inverse = jnp.exp((lane % 64).astype(F32) * (-2.0 * math.log(THETA) / 128))
    angle = moment.astype(F32) * inverse
    cosine = jnp.cos(angle)
    sine = jnp.where(lane < 64, -1.0, 1.0) * jnp.sin(angle)

    @pl.when(h == 2)
    def _():
        hidden_back()
        hidden_on()
        tile_start(None, 1, 1)

        @pl.when((c == 0) | (l == 0))
        def _():
            pl.semaphore_wait(z_ready.at[3], 1)

        pl.when((c == 1) & (l == 0))(lambda: signal(z_ready.at[3], partner))
        signal(z_ready.at[2], in_z(3))
        tile_start(None, 3, 2)

    @pl.when(h == 0)
    def _():
        pl.semaphore_wait(z_ready.at[1], 1)
        tile_start(None, 1, 0)

    for chip in range(CHIPS):
        @pl.when(chip != l)
        def _():
            hidden_arrive(chip * 2 + c)
            core_copy(chip).start()

    @pl.when(h == 1)
    def _():
        pl.semaphore_wait(z_ready.at[2], 1)
        tile_start(None, 2, 1)

    for chip in range(CHIPS):
        hidden_arrive(chip * 2 + 1 - c)

    squares = jnp.zeros((ROWS, 128), F32)
    for t in range(TP):
        piece = all_v[t].astype(F32)
        for b in range(8):
            part = piece[(b // 4) * 8 : (b // 4) * 8 + 8, (b % 4) * 128 : (b % 4) * 128 + 128]
            squares = squares + part * part
    rate = lax.rsqrt(jnp.sum(squares, axis=-1, keepdims=True) / 8192.0 + EPS)
    rate = jnp.broadcast_to(rate, (ROWS, 128))
    gain_load.wait()
    gains = gain_v[...].astype(F32)
    normed = []
    for t in range(TP):
        piece = all_v[t].astype(F32)
        for b in range(8):
            part = piece[(b // 4) * 8 : (b // 4) * 8 + 8, (b % 4) * 128 : (b % 4) * 128 + 128]
            normed.append(part * rate * gains[t * 8 + b : t * 8 + b + 1])
    for p in range(PLACES):
        give_v[p] = jnp.concatenate([normed[group * 16 + p] for group in range(GROUPS)], axis=0).astype(BF16)

    def give_copy(number):
        there = neighbour(offsets[number], 1)
        return pltpu.make_async_remote_copy(
            src_ref=give_v.at[there],
            dst_ref=got_v.at[place],
            send_sem=give_send_sem.at[number],
            recv_sem=give_recv_sem.at[place],
            device_id=in_plane(there),
            device_id_type=MESH,
        )

    @pl.when(place < PLACES - 1)
    def _():
        pl.semaphore_wait(plane_ready, PLACES - 1 - place)

    for number in range(PLACES - 1):
        give_copy(number).start()
    got_v[place] = give_v[place]

    @pl.when(h == 0)
    def _():
        pl.semaphore_wait(z_ready.at[3], 1)
        tile_start(None, 3, 1)


    @pl.when(h == 1)
    def _():
        arrive(0)
        tile_start(0, 2, 2)

    first = jnp.where((h == 0) | (h == 2), 1, 0)
    second = jnp.where(h == 0, 3, jnp.where(h == 1, 2, jnp.where(h == 2, 0, 1)))
    third = jnp.where((h == 0) | (h == 3), 2, 3)

    @pl.when(h == 3)
    def _():
        pl.semaphore_wait(z_ready.at[2], 1)
        tile_start(None, 2, 1)

    @pl.when(h != 1)
    def _():
        arrive(first)

    @pl.when(h == 0)
    def _():
        tile_start(1, 3, 2)

    for t in range(TP):
        x_v[t] = jnp.concatenate(normed[t * 8 : t * 8 + 8], axis=1).astype(BF16)
    weight_load.wait()

    def project(t, total):
        rows_of = weight_v[pl.ds(pl.multiple_of(t * 1024, 1024), 1024)]
        return total + jnp.dot(x_v[t], rows_of, preferred_element_type=F32)

    base = lax.fori_loop(0, TP, project, jnp.zeros((ROWS, 256), F32))

    arrive(second)
    pl.when(h == 0)(lambda: tile_start(3, 1, 3))

    for number in range(PLACES - 1):
        there = neighbour(offsets[number], -1)
        pltpu.make_async_copy(got_v.at[there], got_v.at[there], give_recv_sem.at[there]).wait()
    for p in range(0, PLACES, 2):
        even, odd = got_v[p].astype(F32), got_v[p + 1].astype(F32)
        for group in range(GROUPS):
            xh_v[group, p * 8 : p * 8 + 16] = jnp.concatenate(
                [even[group * 8 : group * 8 + 8], odd[group * 8 : group * 8 + 8]], axis=0
            ).astype(BF16)

    def multiply(group, key_part, value_part):
        product = jnp.dot(xh_v[group], tile_v[group], preferred_element_type=F32)
        flags = flag_v[group]
        return key_part + product * flags[0:1], value_part + product * flags[1:2]

    blank = jnp.zeros((PLACES * ROWS, 128), F32)
    key_part, value_part = multiply(h, blank, blank)
    key_part, value_part = multiply(first, key_part, value_part)
    key_part, value_part = multiply(second, key_part, value_part)
    arrive(third)

    key_part, value_part = multiply(third, key_part, value_part)

    def ret_copy(number):
        there = neighbour(offsets[number], 1)
        return pltpu.make_async_remote_copy(
            src_ref=ret_send.at[there],
            dst_ref=ret_recv.at[place],
            send_sem=ret_send_sem.at[number],
            recv_sem=ret_recv_sem.at[place],
            device_id=in_plane(there),
            device_id_type=MESH,
        )

    for p in range(PLACES):
        ret_send[p] = jnp.concatenate([key_part[p * 8 : p * 8 + 8], value_part[p * 8 : p * 8 + 8]], axis=0).astype(BF16)
    for number in range(PLACES - 1):
        ret_copy(number).start()

    total = ret_send[place].astype(F32)
    for number in range(PLACES - 2, -1, -1):
        there = neighbour(offsets[number], -1)
        pltpu.make_async_copy(ret_recv.at[there], ret_recv.at[there], ret_recv_sem.at[there]).wait()
        total = total + ret_recv[there].astype(F32)
    new_keys = base[:, :128] + total[:8]
    new_values = base[:, 128:] + total[8:]

    rotated = new_keys * cosine + pltpu.roll(new_keys, 64, 1) * sine
    new_entries = jnp.concatenate([rotated, new_values], axis=1)
    entries_out[0, 0] = new_entries[:4].astype(BF16)
    entries_out[0, 1] = new_entries[4:].astype(BF16)

    empty = jnp.zeros((ROWS, 128), F32)
    fresh_keys = jnp.concatenate([rotated, empty], axis=0).astype(BF16)
    fresh_values = jnp.concatenate([new_values, empty], axis=0).astype(BF16)
    new_scores = lax.dot_general(query, fresh_keys, (((1,), (1,)), ((), ())), preferred_element_type=F32)
    new_row = lax.broadcasted_iota(jnp.int32, (rows, 16), 0)
    new_column = lax.broadcasted_iota(jnp.int32, (rows, 16), 1)
    seen = (
        (new_column < 8) & (new_column % 4 == new_row % 4) & (new_column // 4 <= (new_row // 4) % 2)
    )
    new_scores = jnp.where(seen, new_scores * scale, -1e30)
    peak = jnp.maximum(old_peak, jnp.max(new_scores, axis=-1, keepdims=True))
    new_raised = jnp.exp(new_scores - peak)
    shrink = jnp.exp(old_peak - peak)
    all_sum = old_sum * shrink + jnp.sum(new_raised, axis=-1, keepdims=True)
    mixed = old_mixed * shrink + jnp.dot(new_raised.astype(BF16), fresh_values, preferred_element_type=F32)
    mixed = mixed / all_sum
    wide = jnp.concatenate([mixed[i * 8 : i * 8 + 8] for i in range(heads)], axis=1)
    attended_out[0, 0] = wide[:4].astype(BF16)
    attended_out[0, 1] = wide[4:].astype(BF16)

    for chip in range(CHIPS):
        @pl.when(chip != l)
        def _():
            hidden_copy(chip).wait_send()

        core_copy(chip).wait_send()

    for number in range(GROUPS):
        @pl.when((number < 2) | ((number == 2) & (h != 3)) | (h == 0))
        def _():
            tile_copy(None, 0, number).wait_send()
            flag_copy(None, 0, number).wait_send()

    for number in range(PLACES - 1):
        give_copy(number).wait_send()
        ret_copy(number).wait_send()


def hand_over(entries, attended, entries_out, attended_out, sem):
    copies = (
        pltpu.make_async_copy(entries, entries_out, sem.at[0]),
        pltpu.make_async_copy(attended, attended_out, sem.at[1]),
    )
    for copy in copies:
        copy.start()
    for copy in copies:
        copy.wait()


def shards(hidden, norm_gain, kv_weight, delta_tiles, tile_blocks, tile_counts, queries, kv_cache, positions):
    def hbm(array):
        return pltpu.with_memory_space_constraint(array, pltpu.HBM)

    anywhere = pl.BlockSpec(memory_space=pltpu.HBM)
    scalar = pl.BlockSpec(memory_space=pltpu.SMEM)
    vmem = pl.BlockSpec(memory_space=pltpu.VMEM)
    dma = pltpu.SemaphoreType.DMA
    regular = pltpu.SemaphoreType.REGULAR
    entries, attended = pl.pallas_call(
        kernel,
        out_shape=(
            jax.ShapeDtypeStruct((1, 2, 4, 256), BF16),
            jax.ShapeDtypeStruct((1, 2, 4, 1024), BF16),
        ),
        in_specs=[anywhere] * 4 + [scalar] * 2 + [anywhere] * 3,
        out_specs=(vmem, vmem),
        scratch_shapes=[
            pltpu.VMEM((1, 2, 4, 1024), BF16),
            pltpu.VMEM((TP, 16, 512), BF16),
            pltpu.VMEM((TP, ROWS, 1024), BF16),
            pltpu.VMEM((PLACES, 32, 128), BF16),
            pltpu.VMEM((PLACES, 32, 128), BF16),
            pltpu.VMEM((GROUPS, 128, 128), BF16),
            pltpu.VMEM((GROUPS, 128, 128), BF16),
            pltpu.VMEM((GROUPS, 2, 128), F32),
            pltpu.VMEM((8192, 256), BF16),
            pltpu.VMEM((64, 128), BF16),
            pltpu.VMEM((1, 2, 4, 1024), BF16),
            pltpu.VMEM((4, 256, 256), BF16),
            pltpu.VMEM((PLACES, 16, 128), BF16),
            pltpu.VMEM((PLACES, 16, 128), BF16),
            pltpu.SMEM((1, 4), jnp.int32),
            dma((7,)),
            regular,
            regular,
            regular,
            regular((GROUPS,)),
            dma((CHIPS,)),
            dma((TP,)),
            dma((CHIPS,)),
            dma((PLACES - 1,)),
            dma((PLACES,)),
            dma((GROUPS,)),
            dma((GROUPS,)),
            dma((GROUPS,)),
            dma((GROUPS,)),
            dma((PLACES - 1,)),
            dma((PLACES,)),
        ],
        compiler_params=pltpu.CompilerParams(
            collective_id=0, has_side_effects=True, vmem_limit_bytes=24 * 1024 * 1024
        ),
    )(
        hbm(hidden),
        hbm(norm_gain.reshape(64, 128)),
        hbm(kv_weight),
        hbm(delta_tiles),
        tile_blocks,
        tile_counts,
        hbm(queries),
        hbm(kv_cache),
        hbm(positions),
    )
    return pl.pallas_call(
        hand_over,
        out_shape=(
            jax.ShapeDtypeStruct((1, 2, 4, 256), BF16),
            jax.ShapeDtypeStruct((1, 2, 4, 1024), BF16),
        ),
        in_specs=[vmem, vmem],
        out_specs=(anywhere, anywhere),
        scratch_shapes=[dma((2,))],
        compiler_params=pltpu.CompilerParams(vmem_limit_bytes=1024 * 1024),
    )(
        pltpu.with_memory_space_constraint(entries, pltpu.VMEM),
        pltpu.with_memory_space_constraint(attended, pltpu.VMEM),
    )


def solution(mesh):
    return jax.shard_map(
        shards,
        mesh=mesh,
        in_specs=(
            P("rep", None, None, "tp"),
            P(),
            P(None, "tp"),
            P("rep", None, "tp"),
            P("rep", "tp"),
            P("rep", "tp"),
            P("rep", None, None, "tp"),
            P("rep", None, None, "tp"),
            P("rep", None),
        ),
        out_specs=(P("rep", None, None, "tp"), P("rep", None, None, "tp")),
        check_vma=False,
    )
```

```python
import math

import jax
import jax.numpy as jnp
from jax import lax
from jax.experimental import pallas as pl
from jax.experimental.pallas import tpu as pltpu
from jax.sharding import PartitionSpec as P

EPS = 1e-06
THETA = 1000000.0
F32 = jnp.float32
BF16 = jnp.bfloat16
MESH = pl.DeviceIdType.MESH

GROUPS = 4
PLACES = 16
SIDE = 4
TP = 8
CHIPS = 4
ROWS = 8
GREETED = {0: (2, 3, 1), 1: (2,), 2: (), 3: ()}


def kernel(
    hidden,
    gain,
    weight,
    tile,
    blocks,
    counts,
    queries,
    cache,
    positions,
    entries_out,
    attended_out,
    hidden_v,
    all_v,
    x_v,
    give_v,
    got_v,
    xh_v,
    tile_v,
    flag_v,
    weight_v,
    gain_v,
    query_v,
    cache_v,
    ret_send,
    ret_recv,
    positions_s,
    local_sem,
    core_ready,
    tp_ready,
    plane_ready,
    z_ready,
    hid_send_sem,
    hid_recv_sem,
    core_send_sem,
    give_send_sem,
    give_recv_sem,
    tile_send_sem,
    tile_recv_sem,
    flag_send_sem,
    flag_recv_sem,
    ret_send_sem,
    ret_recv_sem,
):
    rep = lax.axis_index("rep")
    tp = lax.axis_index("tp")
    h, place = rep // PLACES, rep % PLACES
    l, c = tp // 2, tp % 2
    partner = {"rep": rep, "tp": tp + 1 - 2 * c}
    y, x = place // SIDE, place % SIDE
    listens = (h == 2) & (l > 0) & (c == 1)
    greetings = jnp.where(h == 2, 2, jnp.where(h == 0, 0, 1)) + jnp.where(listens, jnp.where(l == 1, 4, 2), 0)

    def in_chip(chip):
        return {"rep": rep, "tp": chip * 2 + c}

    def in_plane(p):
        return {"rep": h * PLACES + p, "tp": tp}

    def in_z(group):
        return {"rep": group * PLACES + place, "tp": tp}

    def neighbour(offset, sign):
        dy, dx = offset // SIDE, offset % SIDE
        if sign > 0:
            return ((y + dy) % SIDE) * SIDE + (x + dx) % SIDE
        return ((y + SIDE - dy) % SIDE) * SIDE + (x + SIDE - dx) % SIDE

    def hops(offset):
        dy, dx = offset // SIDE, offset % SIDE
        return min(dy, SIDE - dy) + min(dx, SIDE - dx)

    offsets = sorted(range(1, PLACES), key=lambda o: -hops(o))

    def local(source, target, index):
        return pltpu.make_async_copy(source, target, local_sem.at[index])

    hidden_load = local(hidden, hidden_v, 0)
    tile_load = local(tile.at[0], tile_v.at[h], 1)
    positions_load = local(positions, positions_s, 2)
    query_load = local(queries, query_v, 3)
    cache_load = local(cache.at[0], cache_v, 4)
    gain_load = local(gain, gain_v, 5)
    weight_load = local(weight, weight_v, 6)
    tile_load.start()
    hidden_load.start()

    barrier = pltpu.get_barrier_semaphore()

    def signal(semaphore, where):
        pl.semaphore_signal(semaphore, inc=1, device_id=where, device_id_type=MESH)

    for group in range(GROUPS):
        @pl.when(h == group)
        def _():
            for later in GREETED[group]:
                signal(barrier, in_z(later))

    @pl.when(h == 3)
    def _():
        signal(barrier, {"rep": 2 * PLACES + place, "tp": jnp.where(l == 0, 1, l) * 2 + 1})

    @pl.when(c == 0)
    def _():
        signal(barrier, partner)

    for chip in range(1, CHIPS):
        @pl.when(chip > l)
        def _():
            signal(barrier, in_chip(chip))

    for p in range(1, PLACES):
        @pl.when(p > place)
        def _():
            signal(barrier, in_plane(p))

    valid = jnp.where(counts[0, 0] > 0, 1.0, 0.0)
    is_key = jnp.where(blocks[0, 0] % 2 == 0, 1.0, 0.0)
    flag_v[h] = jnp.concatenate(
        [jnp.full((1, 128), valid * is_key, F32), jnp.full((1, 128), valid * (1.0 - is_key), F32)], axis=0
    )

    @pl.when(place + l + c + greetings > 0)
    def _():
        pl.semaphore_wait(barrier, place + l + c + greetings)


    def tile_copy(source, group, number):
        return pltpu.make_async_remote_copy(
            src_ref=tile_v.at[h if source is None else source],
            dst_ref=tile_v.at[h if source is None else source],
            send_sem=tile_send_sem.at[number],
            recv_sem=tile_recv_sem.at[h if source is None else source],
            device_id=in_z(group),
            device_id_type=MESH,
        )

    def flag_copy(source, group, number):
        slot = h if source is None else source
        return pltpu.make_async_remote_copy(
            src_ref=flag_v.at[slot],
            dst_ref=flag_v.at[slot],
            send_sem=flag_send_sem.at[number],
            recv_sem=flag_recv_sem.at[slot],
            device_id=in_z(group),
            device_id_type=MESH,
        )

    def tile_start(source, group, number):
        flag_copy(source, group, number).start()
        tile_copy(source, group, number).start()

    def arrive(group):
        pltpu.make_async_copy(tile_v.at[group], tile_v.at[group], tile_recv_sem.at[group]).wait()
        pltpu.make_async_copy(flag_v.at[group], flag_v.at[group], flag_recv_sem.at[group]).wait()

    tile_load.wait()

    @pl.when((h == 1) | (h == 3))
    def _():
        signal(z_ready.at[h], in_z(0))
        pl.when(c == 0)(lambda: tile_start(None, 0, 0))

    @pl.when(h == 2)
    def _():
        pl.when(c == 0)(lambda: tile_start(None, 0, 0))
        signal(z_ready.at[h], in_z(1))
        pl.when(listens)(lambda: signal(z_ready.at[3], partner))
        pl.when(listens & (l == 1))(lambda: signal(z_ready.at[3], in_chip(0)))

    @pl.when(c == 1)
    def _():
        signal(core_ready, partner)

    for chip in range(CHIPS - 1):
        @pl.when(chip < l)
        def _():
            signal(tp_ready, in_chip(chip))

    hidden_load.wait()
    mine = jnp.concatenate([hidden_v[0, 0].astype(F32), hidden_v[0, 1].astype(F32)], axis=0)
    all_v[tp] = jnp.concatenate([mine[:, :512], mine[:, 512:]], axis=0).astype(BF16)


    def hidden_copy(chip):
        return pltpu.make_async_remote_copy(
            src_ref=all_v.at[tp],
            dst_ref=all_v.at[tp],
            send_sem=hid_send_sem.at[chip],
            recv_sem=hid_recv_sem.at[tp],
            device_id=in_chip(chip),
            device_id_type=MESH,
        )

    def core_copy(chip):
        source = chip * 2 + c
        return pltpu.make_async_remote_copy(
            src_ref=all_v.at[source],
            dst_ref=all_v.at[source],
            send_sem=core_send_sem.at[chip],
            recv_sem=hid_recv_sem.at[source],
            device_id=partner,
            device_id_type=MESH,
        )

    def hidden_arrive(t):
        pltpu.make_async_copy(all_v.at[t], all_v.at[t], hid_recv_sem.at[t]).wait()

    def hidden_back():
        for chip in range(CHIPS - 1):
            @pl.when(chip < l)
            def _():
                hidden_copy(chip).start()

    def hidden_on():
        @pl.when(l < CHIPS - 1)
        def _():
            pl.semaphore_wait(tp_ready, CHIPS - 1 - l)

        for chip in range(CHIPS - 1, 0, -1):
            @pl.when(chip > l)
            def _():
                hidden_copy(chip).start()

        @pl.when(c == 0)
        def _():
            pl.semaphore_wait(core_ready, 1)

        core_copy(l).start()

    pl.when(h != 2)(hidden_back)
    for p in range(PLACES - 1):
        @pl.when(p < place)
        def _():
            signal(plane_ready, in_plane(p))

    gain_load.start()
    query_load.start()
    positions_load.start()
    cache_load.start()
    weight_load.start()

    pl.when((h != 0) & (c == 1))(lambda: tile_start(None, 0, 0))
    pl.when(h != 2)(hidden_on)
    query_load.wait()
    positions_load.wait()
    all_queries = jnp.concatenate([query_v[0, 0].astype(F32), query_v[0, 1].astype(F32)], axis=0)
    heads = all_queries.shape[1] // 128
    query_rows = jnp.concatenate([all_queries[:, i * 128 : i * 128 + 128] for i in range(heads)], axis=0)
    query = query_rows.astype(BF16)
    rows = heads * ROWS
    cache_load.wait()
    length = cache_v.shape[1]
    row = lax.broadcasted_iota(jnp.int32, (rows, length), 0)
    column = lax.broadcasted_iota(jnp.int32, (rows, length), 1)
    sequence = row % 4
    scores = jnp.zeros((rows, length), F32)
    filled = jnp.zeros((rows, length), jnp.int32)
    for r in range(4):
        keys = cache_v[r, :, :128]
        product = lax.dot_general(query, keys, (((1,), (1,)), ((), ())), preferred_element_type=F32)
        scores = jnp.where(sequence == r, product, scores)
        filled = jnp.where(sequence == r, positions_s[0, r], filled)
    scale = 128 ** (-0.5)
    scores = jnp.where(column < filled, scores * scale, -1e30)
    old_peak = jnp.max(scores, axis=-1, keepdims=True)
    raised = jnp.exp(scores - old_peak)
    old_sum = jnp.sum(raised, axis=-1, keepdims=True)
    old_mixed = jnp.zeros((rows, 128), F32)
    for r in range(4):
        chosen = jnp.where(sequence == r, raised, 0.0).astype(BF16)
        old_mixed = old_mixed + jnp.dot(chosen, cache_v[r, :, 128:], preferred_element_type=F32)

    token = lax.broadcasted_iota(jnp.int32, (ROWS, 128), 0)
    lane = lax.broadcasted_iota(jnp.int32, (ROWS, 128), 1)
    moment = token // 4
    for r in range(4):
        moment = jnp.where(token % 4 == r, token // 4 + positions_s[0, r], moment)
    inverse = jnp.exp((lane % 64).astype(F32) * (-2.0 * math.log(THETA) / 128))
    angle = moment.astype(F32) * inverse
    cosine = jnp.cos(angle)
    sine = jnp.where(lane < 64, -1.0, 1.0) * jnp.sin(angle)

    @pl.when(h == 2)
    def _():
        hidden_back()
        hidden_on()
        tile_start(None, 1, 1)

        @pl.when((c == 0) | (l == 0))
        def _():
            pl.semaphore_wait(z_ready.at[3], 1)

        pl.when((c == 1) & (l == 0))(lambda: signal(z_ready.at[3], partner))
        signal(z_ready.at[2], in_z(3))
        tile_start(None, 3, 2)

    @pl.when(h == 0)
    def _():
        pl.semaphore_wait(z_ready.at[1], 1)
        tile_start(None, 1, 0)

    for chip in range(CHIPS):
        @pl.when(chip != l)
        def _():
            hidden_arrive(chip * 2 + c)
            core_copy(chip).start()

    @pl.when(h == 1)
    def _():
        pl.semaphore_wait(z_ready.at[2], 1)
        tile_start(None, 2, 1)

    for chip in range(CHIPS):
        hidden_arrive(chip * 2 + 1 - c)

    squares = jnp.zeros((ROWS, 128), F32)
    for t in range(TP):
        piece = all_v[t].astype(F32)
        for b in range(8):
            part = piece[(b // 4) * 8 : (b // 4) * 8 + 8, (b % 4) * 128 : (b % 4) * 128 + 128]
            squares = squares + part * part
    rate = lax.rsqrt(jnp.sum(squares, axis=-1, keepdims=True) / 8192.0 + EPS)
    rate = jnp.broadcast_to(rate, (ROWS, 128))
    gain_load.wait()
    gains = gain_v[...].astype(F32)
    normed = []
    for t in range(TP):
        piece = all_v[t].astype(F32)
        for b in range(8):
            part = piece[(b // 4) * 8 : (b // 4) * 8 + 8, (b % 4) * 128 : (b % 4) * 128 + 128]
            normed.append(part * rate * gains[t * 8 + b : t * 8 + b + 1])
    for p in range(PLACES):
        give_v[p] = jnp.concatenate([normed[group * 16 + p] for group in range(GROUPS)], axis=0).astype(BF16)

    def give_copy(number):
        there = neighbour(offsets[number], 1)
        return pltpu.make_async_remote_copy(
            src_ref=give_v.at[there],
            dst_ref=got_v.at[place],
            send_sem=give_send_sem.at[number],
            recv_sem=give_recv_sem.at[place],
            device_id=in_plane(there),
            device_id_type=MESH,
        )

    @pl.when(place < PLACES - 1)
    def _():
        pl.semaphore_wait(plane_ready, PLACES - 1 - place)

    def give():
        for number in range(PLACES - 1):
            give_copy(number).start()

    pl.when(c == 0)(give)

    for t in range(TP):
        x_v[t] = jnp.concatenate(normed[t * 8 : t * 8 + 8], axis=1).astype(BF16)
    weight_load.wait()

    def project(t, total):
        rows_of = weight_v[pl.ds(pl.multiple_of(t * 1024, 1024), 1024)]
        return total + jnp.dot(x_v[t], rows_of, preferred_element_type=F32)

    base = lax.fori_loop(0, 2, project, jnp.zeros((ROWS, 256), F32))
    pl.when(c == 1)(give)
    got_v[place] = give_v[place]

    @pl.when(h == 0)
    def _():
        pl.semaphore_wait(z_ready.at[3], 1)
        tile_start(None, 3, 1)


    @pl.when(h == 1)
    def _():
        arrive(0)
        tile_start(0, 2, 2)

    first = jnp.where((h == 0) | (h == 2), 1, 0)
    second = jnp.where(h == 0, 3, jnp.where(h == 1, 2, jnp.where(h == 2, 0, 1)))
    third = jnp.where((h == 0) | (h == 3), 2, 3)

    @pl.when(h == 3)
    def _():
        pl.semaphore_wait(z_ready.at[2], 1)
        tile_start(None, 2, 1)

    @pl.when(h != 1)
    def _():
        arrive(first)

    @pl.when(h == 0)
    def _():
        tile_start(1, 3, 2)

    base = lax.fori_loop(2, TP, project, base)

    arrive(second)
    pl.when(h == 0)(lambda: tile_start(3, 1, 3))

    for number in range(PLACES - 1):
        there = neighbour(offsets[number], -1)
        pltpu.make_async_copy(got_v.at[there], got_v.at[there], give_recv_sem.at[there]).wait()
    for p in range(0, PLACES, 2):
        even, odd = got_v[p].astype(F32), got_v[p + 1].astype(F32)
        for group in range(GROUPS):
            xh_v[group, p * 8 : p * 8 + 16] = jnp.concatenate(
                [even[group * 8 : group * 8 + 8], odd[group * 8 : group * 8 + 8]], axis=0
            ).astype(BF16)

    def multiply(group, key_part, value_part):
        product = jnp.dot(xh_v[group], tile_v[group], preferred_element_type=F32)
        flags = flag_v[group]
        return key_part + product * flags[0:1], value_part + product * flags[1:2]

    blank = jnp.zeros((PLACES * ROWS, 128), F32)
    key_part, value_part = multiply(h, blank, blank)
    key_part, value_part = multiply(first, key_part, value_part)
    key_part, value_part = multiply(second, key_part, value_part)
    arrive(third)

    key_part, value_part = multiply(third, key_part, value_part)

    def ret_copy(number):
        there = neighbour(offsets[number], 1)
        return pltpu.make_async_remote_copy(
            src_ref=ret_send.at[there],
            dst_ref=ret_recv.at[place],
            send_sem=ret_send_sem.at[number],
            recv_sem=ret_recv_sem.at[place],
            device_id=in_plane(there),
            device_id_type=MESH,
        )

    for p in range(PLACES):
        ret_send[p] = jnp.concatenate([key_part[p * 8 : p * 8 + 8], value_part[p * 8 : p * 8 + 8]], axis=0).astype(BF16)
    for number in range(PLACES - 1):
        ret_copy(number).start()

    total = ret_send[place].astype(F32)
    for number in range(PLACES - 2, -1, -1):
        there = neighbour(offsets[number], -1)
        pltpu.make_async_copy(ret_recv.at[there], ret_recv.at[there], ret_recv_sem.at[there]).wait()
        total = total + ret_recv[there].astype(F32)
    new_keys = base[:, :128] + total[:8]
    new_values = base[:, 128:] + total[8:]

    rotated = new_keys * cosine + pltpu.roll(new_keys, 64, 1) * sine
    new_entries = jnp.concatenate([rotated, new_values], axis=1)
    entries_out[0, 0] = new_entries[:4].astype(BF16)
    entries_out[0, 1] = new_entries[4:].astype(BF16)

    rounded_keys = rotated.astype(BF16).astype(F32)
    rounded_values = new_values.astype(BF16).astype(F32)

    def spread(entry, step):
        return jnp.concatenate([entry[step * 4 : step * 4 + 4]] * (rows // 4), axis=0)

    score_0 = jnp.sum(query_rows * spread(rounded_keys, 0), axis=-1, keepdims=True) * scale
    score_1 = jnp.sum(query_rows * spread(rounded_keys, 1), axis=-1, keepdims=True) * scale
    late = (lax.broadcasted_iota(jnp.int32, (rows, 1), 0) // 4) % 2 == 1
    score_1 = jnp.where(late, score_1, -1e30)
    peak = jnp.maximum(old_peak, jnp.maximum(score_0, score_1))
    raised_0 = jnp.exp(score_0 - peak)
    raised_1 = jnp.exp(score_1 - peak)
    shrink = jnp.exp(old_peak - peak)
    all_sum = old_sum * shrink + raised_0 + raised_1
    mixed = old_mixed * shrink + raised_0 * spread(rounded_values, 0) + raised_1 * spread(rounded_values, 1)
    mixed = mixed * (1.0 / all_sum)
    wide = jnp.concatenate([mixed[i * 8 : i * 8 + 8] for i in range(heads)], axis=1)
    attended_out[0, 0] = wide[:4].astype(BF16)
    attended_out[0, 1] = wide[4:].astype(BF16)

    for chip in range(CHIPS):
        @pl.when(chip != l)
        def _():
            hidden_copy(chip).wait_send()

        core_copy(chip).wait_send()

    for number in range(GROUPS):
        @pl.when((number < 2) | ((number == 2) & (h != 3)) | (h == 0))
        def _():
            tile_copy(None, 0, number).wait_send()
            flag_copy(None, 0, number).wait_send()

    for number in range(PLACES - 1):
        give_copy(number).wait_send()
        ret_copy(number).wait_send()


def hand_over(entries, attended, entries_out, attended_out, sem):
    copies = (
        pltpu.make_async_copy(entries, entries_out, sem.at[0]),
        pltpu.make_async_copy(attended, attended_out, sem.at[1]),
    )
    for copy in copies:
        copy.start()
    for copy in copies:
        copy.wait()


def shards(hidden, norm_gain, kv_weight, delta_tiles, tile_blocks, tile_counts, queries, kv_cache, positions):
    def hbm(array):
        return pltpu.with_memory_space_constraint(array, pltpu.HBM)

    anywhere = pl.BlockSpec(memory_space=pltpu.HBM)
    scalar = pl.BlockSpec(memory_space=pltpu.SMEM)
    vmem = pl.BlockSpec(memory_space=pltpu.VMEM)
    dma = pltpu.SemaphoreType.DMA
    regular = pltpu.SemaphoreType.REGULAR
    entries, attended = pl.pallas_call(
        kernel,
        out_shape=(
            jax.ShapeDtypeStruct((1, 2, 4, 256), BF16),
            jax.ShapeDtypeStruct((1, 2, 4, 1024), BF16),
        ),
        in_specs=[anywhere] * 4 + [scalar] * 2 + [anywhere] * 3,
        out_specs=(vmem, vmem),
        scratch_shapes=[
            pltpu.VMEM((1, 2, 4, 1024), BF16),
            pltpu.VMEM((TP, 16, 512), BF16),
            pltpu.VMEM((TP, ROWS, 1024), BF16),
            pltpu.VMEM((PLACES, 32, 128), BF16),
            pltpu.VMEM((PLACES, 32, 128), BF16),
            pltpu.VMEM((GROUPS, 128, 128), BF16),
            pltpu.VMEM((GROUPS, 128, 128), BF16),
            pltpu.VMEM((GROUPS, 2, 128), F32),
            pltpu.VMEM((8192, 256), BF16),
            pltpu.VMEM((64, 128), BF16),
            pltpu.VMEM((1, 2, 4, 1024), BF16),
            pltpu.VMEM((4, 256, 256), BF16),
            pltpu.VMEM((PLACES, 16, 128), BF16),
            pltpu.VMEM((PLACES, 16, 128), BF16),
            pltpu.SMEM((1, 4), jnp.int32),
            dma((7,)),
            regular,
            regular,
            regular,
            regular((GROUPS,)),
            dma((CHIPS,)),
            dma((TP,)),
            dma((CHIPS,)),
            dma((PLACES - 1,)),
            dma((PLACES,)),
            dma((GROUPS,)),
            dma((GROUPS,)),
            dma((GROUPS,)),
            dma((GROUPS,)),
            dma((PLACES - 1,)),
            dma((PLACES,)),
        ],
        compiler_params=pltpu.CompilerParams(
            collective_id=0, has_side_effects=True, vmem_limit_bytes=24 * 1024 * 1024
        ),
    )(
        hbm(hidden),
        hbm(norm_gain.reshape(64, 128)),
        hbm(kv_weight),
        hbm(delta_tiles),
        tile_blocks,
        tile_counts,
        hbm(queries),
        hbm(kv_cache),
        hbm(positions),
    )
    return pl.pallas_call(
        hand_over,
        out_shape=(
            jax.ShapeDtypeStruct((1, 2, 4, 256), BF16),
            jax.ShapeDtypeStruct((1, 2, 4, 1024), BF16),
        ),
        in_specs=[vmem, vmem],
        out_specs=(anywhere, anywhere),
        scratch_shapes=[dma((2,))],
        compiler_params=pltpu.CompilerParams(vmem_limit_bytes=1024 * 1024),
    )(
        pltpu.with_memory_space_constraint(entries, pltpu.VMEM),
        pltpu.with_memory_space_constraint(attended, pltpu.VMEM),
    )


def solution(mesh):
    return jax.shard_map(
        shards,
        mesh=mesh,
        in_specs=(
            P("rep", None, None, "tp"),
            P(),
            P(None, "tp"),
            P("rep", None, "tp"),
            P("rep", "tp"),
            P("rep", "tp"),
            P("rep", None, None, "tp"),
            P("rep", None, None, "tp"),
            P("rep", None),
        ),
        out_specs=(P("rep", None, None, "tp"), P("rep", None, None, "tp")),
        check_vma=False,
    )
```

```python
import math

import jax
import jax.numpy as jnp
from jax import lax
from jax.experimental import pallas as pl
from jax.experimental.pallas import tpu as pltpu
from jax.sharding import PartitionSpec as P

EPS = 1e-06
THETA = 1000000.0
F32 = jnp.float32
BF16 = jnp.bfloat16
MESH = pl.DeviceIdType.MESH

GROUPS = 4
PLACES = 16
SIDE = 4
TP = 8
CHIPS = 4
ROWS = 8
GREETED = {0: (2, 3, 1), 1: (2,), 2: (), 3: ()}


def kernel(
    hidden,
    gain,
    weight,
    tile,
    blocks,
    counts,
    queries,
    cache,
    positions,
    entries_out,
    attended_out,
    hidden_v,
    all_v,
    x_v,
    give_v,
    got_v,
    xh_v,
    tile_v,
    flag_v,
    weight_v,
    gain_v,
    query_v,
    cache_v,
    ret_send,
    ret_recv,
    positions_s,
    local_sem,
    core_ready,
    tp_ready,
    plane_ready,
    z_ready,
    hid_send_sem,
    hid_recv_sem,
    core_send_sem,
    give_send_sem,
    give_recv_sem,
    tile_send_sem,
    tile_recv_sem,
    flag_send_sem,
    flag_recv_sem,
    ret_send_sem,
    ret_recv_sem,
):
    rep = lax.axis_index("rep")
    tp = lax.axis_index("tp")
    h, place = rep // PLACES, rep % PLACES
    l, c = tp // 2, tp % 2
    partner = {"rep": rep, "tp": tp + 1 - 2 * c}
    y, x = place // SIDE, place % SIDE
    listens = (h == 2) & (l > 0) & (c == 1)
    greetings = jnp.where(h == 2, 2, jnp.where(h == 0, 0, 1)) + jnp.where(listens, jnp.where(l == 1, 4, 2), 0)

    def in_chip(chip):
        return {"rep": rep, "tp": chip * 2 + c}

    def in_plane(p):
        return {"rep": h * PLACES + p, "tp": tp}

    def in_z(group):
        return {"rep": group * PLACES + place, "tp": tp}

    def neighbour(offset, sign):
        dy, dx = offset // SIDE, offset % SIDE
        if sign > 0:
            return ((y + dy) % SIDE) * SIDE + (x + dx) % SIDE
        return ((y + SIDE - dy) % SIDE) * SIDE + (x + SIDE - dx) % SIDE

    def hops(offset):
        dy, dx = offset // SIDE, offset % SIDE
        return min(dy, SIDE - dy) + min(dx, SIDE - dx)

    offsets = sorted(range(1, PLACES), key=lambda o: -hops(o))

    def local(source, target, index):
        return pltpu.make_async_copy(source, target, local_sem.at[index])

    hidden_load = local(hidden, hidden_v, 0)
    tile_load = local(tile.at[0], tile_v.at[h], 1)
    positions_load = local(positions, positions_s, 2)
    query_load = local(queries, query_v, 3)
    cache_load = local(cache.at[0], cache_v, 4)
    gain_load = local(gain, gain_v, 5)
    weight_load = local(weight, weight_v, 6)
    tile_load.start()
    hidden_load.start()

    barrier = pltpu.get_barrier_semaphore()

    def signal(semaphore, where):
        pl.semaphore_signal(semaphore, inc=1, device_id=where, device_id_type=MESH)

    for group in range(GROUPS):
        @pl.when(h == group)
        def _():
            for later in GREETED[group]:
                signal(barrier, in_z(later))

    @pl.when(h == 3)
    def _():
        signal(barrier, {"rep": 2 * PLACES + place, "tp": jnp.where(l == 0, 1, l) * 2 + 1})

    @pl.when(c == 0)
    def _():
        signal(barrier, partner)

    for chip in range(1, CHIPS):
        @pl.when(chip > l)
        def _():
            signal(barrier, in_chip(chip))

    for p in range(1, PLACES):
        @pl.when(p > place)
        def _():
            signal(barrier, in_plane(p))

    valid = jnp.where(counts[0, 0] > 0, 1.0, 0.0)
    is_key = jnp.where(blocks[0, 0] % 2 == 0, 1.0, 0.0)
    flag_v[h] = jnp.concatenate(
        [jnp.full((1, 128), valid * is_key, F32), jnp.full((1, 128), valid * (1.0 - is_key), F32)], axis=0
    )

    @pl.when(place + l + c + greetings > 0)
    def _():
        pl.semaphore_wait(barrier, place + l + c + greetings)


    def tile_copy(source, group, number):
        return pltpu.make_async_remote_copy(
            src_ref=tile_v.at[h if source is None else source],
            dst_ref=tile_v.at[h if source is None else source],
            send_sem=tile_send_sem.at[number],
            recv_sem=tile_recv_sem.at[h if source is None else source],
            device_id=in_z(group),
            device_id_type=MESH,
        )

    def flag_copy(source, group, number):
        slot = h if source is None else source
        return pltpu.make_async_remote_copy(
            src_ref=flag_v.at[slot],
            dst_ref=flag_v.at[slot],
            send_sem=flag_send_sem.at[number],
            recv_sem=flag_recv_sem.at[slot],
            device_id=in_z(group),
            device_id_type=MESH,
        )

    def tile_start(source, group, number):
        flag_copy(source, group, number).start()
        tile_copy(source, group, number).start()

    def arrive(group):
        pltpu.make_async_copy(tile_v.at[group], tile_v.at[group], tile_recv_sem.at[group]).wait()
        pltpu.make_async_copy(flag_v.at[group], flag_v.at[group], flag_recv_sem.at[group]).wait()

    tile_load.wait()

    @pl.when((h == 1) | (h == 3))
    def _():
        signal(z_ready.at[h], in_z(0))
        pl.when(c == 0)(lambda: tile_start(None, 0, 0))

    @pl.when(h == 2)
    def _():
        pl.when(c == 0)(lambda: tile_start(None, 0, 0))
        signal(z_ready.at[h], in_z(1))
        pl.when(listens)(lambda: signal(z_ready.at[3], partner))
        pl.when(listens & (l == 1))(lambda: signal(z_ready.at[3], in_chip(0)))

    @pl.when(c == 1)
    def _():
        signal(core_ready, partner)

    for chip in range(CHIPS - 1):
        @pl.when(chip < l)
        def _():
            signal(tp_ready, in_chip(chip))

    hidden_load.wait()
    mine = jnp.concatenate([hidden_v[0, 0].astype(F32), hidden_v[0, 1].astype(F32)], axis=0)
    all_v[tp] = jnp.concatenate([mine[:, :512], mine[:, 512:]], axis=0).astype(BF16)


    def hidden_copy(chip):
        return pltpu.make_async_remote_copy(
            src_ref=all_v.at[tp],
            dst_ref=all_v.at[tp],
            send_sem=hid_send_sem.at[chip],
            recv_sem=hid_recv_sem.at[tp],
            device_id=in_chip(chip),
            device_id_type=MESH,
        )

    def core_copy(chip):
        source = chip * 2 + c
        return pltpu.make_async_remote_copy(
            src_ref=all_v.at[source],
            dst_ref=all_v.at[source],
            send_sem=core_send_sem.at[chip],
            recv_sem=hid_recv_sem.at[source],
            device_id=partner,
            device_id_type=MESH,
        )

    def hidden_arrive(t):
        pltpu.make_async_copy(all_v.at[t], all_v.at[t], hid_recv_sem.at[t]).wait()

    def hidden_back():
        for chip in range(CHIPS - 1):
            @pl.when(chip < l)
            def _():
                hidden_copy(chip).start()

    def hidden_on():
        @pl.when(l < CHIPS - 1)
        def _():
            pl.semaphore_wait(tp_ready, CHIPS - 1 - l)

        for chip in range(CHIPS - 1, 0, -1):
            @pl.when(chip > l)
            def _():
                hidden_copy(chip).start()

        @pl.when(c == 0)
        def _():
            pl.semaphore_wait(core_ready, 1)

        core_copy(l).start()

    pl.when(h != 2)(hidden_back)
    for p in range(PLACES - 1):
        @pl.when(p < place)
        def _():
            signal(plane_ready, in_plane(p))

    gain_load.start()
    query_load.start()
    positions_load.start()
    cache_load.start()
    weight_load.start()

    pl.when((h != 0) & (c == 1))(lambda: tile_start(None, 0, 0))
    pl.when(h != 2)(hidden_on)
    query_load.wait()
    positions_load.wait()
    all_queries = jnp.concatenate([query_v[0, 0].astype(F32), query_v[0, 1].astype(F32)], axis=0)
    heads = all_queries.shape[1] // 128
    query_rows = jnp.concatenate([all_queries[:, i * 128 : i * 128 + 128] for i in range(heads)], axis=0)
    query = query_rows.astype(BF16)
    rows = heads * ROWS
    cache_load.wait()
    length = cache_v.shape[1]
    row = lax.broadcasted_iota(jnp.int32, (rows, length), 0)
    column = lax.broadcasted_iota(jnp.int32, (rows, length), 1)
    sequence = row % 4
    scores = jnp.zeros((rows, length), F32)
    filled = jnp.zeros((rows, length), jnp.int32)
    for r in range(4):
        keys = cache_v[r, :, :128]
        product = lax.dot_general(query, keys, (((1,), (1,)), ((), ())), preferred_element_type=F32)
        scores = jnp.where(sequence == r, product, scores)
        filled = jnp.where(sequence == r, positions_s[0, r], filled)
    scale = 128 ** (-0.5)
    scores = jnp.where(column < filled, scores * scale, -1e30)
    old_peak = jnp.max(scores, axis=-1, keepdims=True)
    raised = jnp.exp(scores - old_peak)
    old_sum = jnp.sum(raised, axis=-1, keepdims=True)
    old_mixed = jnp.zeros((rows, 128), F32)
    for r in range(4):
        chosen = jnp.where(sequence == r, raised, 0.0).astype(BF16)
        old_mixed = old_mixed + jnp.dot(chosen, cache_v[r, :, 128:], preferred_element_type=F32)

    token = lax.broadcasted_iota(jnp.int32, (ROWS, 128), 0)
    lane = lax.broadcasted_iota(jnp.int32, (ROWS, 128), 1)
    moment = token // 4
    for r in range(4):
        moment = jnp.where(token % 4 == r, token // 4 + positions_s[0, r], moment)
    inverse = jnp.exp((lane % 64).astype(F32) * (-2.0 * math.log(THETA) / 128))
    angle = moment.astype(F32) * inverse
    cosine = jnp.cos(angle)
    sine = jnp.where(lane < 64, -1.0, 1.0) * jnp.sin(angle)

    @pl.when(h == 2)
    def _():
        hidden_back()
        hidden_on()
        tile_start(None, 1, 1)

        @pl.when((c == 0) | (l == 0))
        def _():
            pl.semaphore_wait(z_ready.at[3], 1)

        pl.when((c == 1) & (l == 0))(lambda: signal(z_ready.at[3], partner))
        signal(z_ready.at[2], in_z(3))
        tile_start(None, 3, 2)

    @pl.when(h == 0)
    def _():
        pl.semaphore_wait(z_ready.at[1], 1)
        tile_start(None, 1, 0)

    for chip in range(CHIPS):
        @pl.when(chip != l)
        def _():
            hidden_arrive(chip * 2 + c)
            core_copy(chip).start()

    @pl.when(h == 1)
    def _():
        pl.semaphore_wait(z_ready.at[2], 1)
        tile_start(None, 2, 1)

    for chip in range(CHIPS):
        hidden_arrive(chip * 2 + 1 - c)

    squares = jnp.zeros((ROWS, 128), F32)
    for t in range(TP):
        piece = all_v[t].astype(F32)
        for b in range(8):
            part = piece[(b // 4) * 8 : (b // 4) * 8 + 8, (b % 4) * 128 : (b % 4) * 128 + 128]
            squares = squares + part * part
    rate = lax.rsqrt(jnp.sum(squares, axis=-1, keepdims=True) / 8192.0 + EPS)
    rate = jnp.broadcast_to(rate, (ROWS, 128))
    gain_load.wait()
    gains = gain_v[...].astype(F32)
    normed = []
    for t in range(TP):
        piece = all_v[t].astype(F32)
        for b in range(8):
            part = piece[(b // 4) * 8 : (b // 4) * 8 + 8, (b % 4) * 128 : (b % 4) * 128 + 128]
            normed.append(part * rate * gains[t * 8 + b : t * 8 + b + 1])
    for p in range(PLACES):
        give_v[p] = jnp.concatenate([normed[group * 16 + p] for group in range(GROUPS)], axis=0).astype(BF16)

    def give_copy(number):
        there = neighbour(offsets[number], 1)
        return pltpu.make_async_remote_copy(
            src_ref=give_v.at[there],
            dst_ref=got_v.at[place],
            send_sem=give_send_sem.at[number],
            recv_sem=give_recv_sem.at[place],
            device_id=in_plane(there),
            device_id_type=MESH,
        )

    @pl.when(place < PLACES - 1)
    def _():
        pl.semaphore_wait(plane_ready, PLACES - 1 - place)

    def give():
        for number in range(PLACES - 1):
            give_copy(number).start()

    pl.when(c == 0)(give)

    for t in range(TP):
        x_v[t] = jnp.concatenate(normed[t * 8 : t * 8 + 8], axis=1).astype(BF16)
    weight_load.wait()

    def project(t, total):
        rows_of = weight_v[pl.ds(pl.multiple_of(t * 1024, 1024), 1024)]
        return total + jnp.dot(x_v[t], rows_of, preferred_element_type=F32)

    base = lax.fori_loop(0, 2, project, jnp.zeros((ROWS, 256), F32))
    pl.when(c == 1)(give)
    got_v[place] = give_v[place]

    @pl.when(h == 0)
    def _():
        pl.semaphore_wait(z_ready.at[3], 1)
        tile_start(None, 3, 1)


    @pl.when(h == 1)
    def _():
        arrive(0)
        tile_start(0, 2, 2)

    first = jnp.where((h == 0) | (h == 2), 1, 0)
    second = jnp.where(h == 0, 3, jnp.where(h == 1, 2, jnp.where(h == 2, 0, 1)))
    third = jnp.where((h == 0) | (h == 3), 2, 3)

    @pl.when(h == 3)
    def _():
        pl.semaphore_wait(z_ready.at[2], 1)
        tile_start(None, 2, 1)

    @pl.when(h != 1)
    def _():
        arrive(first)

    @pl.when(h == 0)
    def _():
        tile_start(1, 3, 2)

    base = lax.fori_loop(2, TP, project, base)

    arrive(second)
    pl.when(h == 0)(lambda: tile_start(3, 1, 3))

    for number in range(PLACES - 1):
        there = neighbour(offsets[number], -1)
        pltpu.make_async_copy(got_v.at[there], got_v.at[there], give_recv_sem.at[there]).wait()
    turns = [neighbour(offset, 1) for offset in offsets] + [place]
    for turn in range(0, PLACES, 2):
        even, odd = got_v[turns[turn]].astype(F32), got_v[turns[turn + 1]].astype(F32)
        for group in range(GROUPS):
            xh_v[group, turn * 8 : turn * 8 + 16] = jnp.concatenate(
                [even[group * 8 : group * 8 + 8], odd[group * 8 : group * 8 + 8]], axis=0
            ).astype(BF16)

    def multiply(group, key_part, value_part):
        product = jnp.dot(xh_v[group], tile_v[group], preferred_element_type=F32)
        flags = flag_v[group]
        return key_part + product * flags[0:1], value_part + product * flags[1:2]

    blank = jnp.zeros((PLACES * ROWS, 128), F32)
    key_part, value_part = multiply(h, blank, blank)
    key_part, value_part = multiply(first, key_part, value_part)
    key_part, value_part = multiply(second, key_part, value_part)
    arrive(third)

    key_part, value_part = multiply(third, key_part, value_part)

    def ret_copy(number):
        there = neighbour(offsets[number], 1)
        return pltpu.make_async_remote_copy(
            src_ref=ret_send.at[number],
            dst_ref=ret_recv.at[place],
            send_sem=ret_send_sem.at[number],
            recv_sem=ret_recv_sem.at[place],
            device_id=in_plane(there),
            device_id_type=MESH,
        )

    def share(turn):
        rows_of = slice(turn * 8, turn * 8 + 8)
        return jnp.concatenate([key_part[rows_of], value_part[rows_of]], axis=0)

    for number in range(PLACES - 1):
        ret_send[number] = share(number).astype(BF16)
        ret_copy(number).start()

    total = share(PLACES - 1)
    for number in range(PLACES - 2, -1, -1):
        there = neighbour(offsets[number], -1)
        pltpu.make_async_copy(ret_recv.at[there], ret_recv.at[there], ret_recv_sem.at[there]).wait()
        total = total + ret_recv[there].astype(F32)
    new_keys = base[:, :128] + total[:8]
    new_values = base[:, 128:] + total[8:]

    rotated = new_keys * cosine + pltpu.roll(new_keys, 64, 1) * sine
    new_entries = jnp.concatenate([rotated, new_values], axis=1)
    entries_out[0, 0] = new_entries[:4].astype(BF16)
    entries_out[0, 1] = new_entries[4:].astype(BF16)

    rounded_keys = rotated.astype(BF16).astype(F32)
    rounded_values = new_values.astype(BF16).astype(F32)

    def spread(entry, step):
        return jnp.concatenate([entry[step * 4 : step * 4 + 4]] * (rows // 4), axis=0)

    score_0 = jnp.sum(query_rows * spread(rounded_keys, 0), axis=-1, keepdims=True) * scale
    score_1 = jnp.sum(query_rows * spread(rounded_keys, 1), axis=-1, keepdims=True) * scale
    late = (lax.broadcasted_iota(jnp.int32, (rows, 1), 0) // 4) % 2 == 1
    score_1 = jnp.where(late, score_1, -1e30)
    peak = jnp.maximum(old_peak, jnp.maximum(score_0, score_1))
    raised_0 = jnp.exp(score_0 - peak)
    raised_1 = jnp.exp(score_1 - peak)
    shrink = jnp.exp(old_peak - peak)
    all_sum = old_sum * shrink + raised_0 + raised_1
    mixed = old_mixed * shrink + raised_0 * spread(rounded_values, 0) + raised_1 * spread(rounded_values, 1)
    mixed = mixed * (1.0 / all_sum)
    wide = jnp.concatenate([mixed[i * 8 : i * 8 + 8] for i in range(heads)], axis=1)
    attended_out[0, 0] = wide[:4].astype(BF16)
    attended_out[0, 1] = wide[4:].astype(BF16)

    for chip in range(CHIPS):
        @pl.when(chip != l)
        def _():
            hidden_copy(chip).wait_send()

        core_copy(chip).wait_send()

    for number in range(GROUPS):
        @pl.when((number < 2) | ((number == 2) & (h != 3)) | (h == 0))
        def _():
            tile_copy(None, 0, number).wait_send()
            flag_copy(None, 0, number).wait_send()

    for number in range(PLACES - 1):
        give_copy(number).wait_send()
        ret_copy(number).wait_send()


def hand_over(entries, attended, entries_out, attended_out, sem):
    copies = (
        pltpu.make_async_copy(entries, entries_out, sem.at[0]),
        pltpu.make_async_copy(attended, attended_out, sem.at[1]),
    )
    for copy in copies:
        copy.start()
    for copy in copies:
        copy.wait()


def shards(hidden, norm_gain, kv_weight, delta_tiles, tile_blocks, tile_counts, queries, kv_cache, positions):
    def hbm(array):
        return pltpu.with_memory_space_constraint(array, pltpu.HBM)

    anywhere = pl.BlockSpec(memory_space=pltpu.HBM)
    scalar = pl.BlockSpec(memory_space=pltpu.SMEM)
    vmem = pl.BlockSpec(memory_space=pltpu.VMEM)
    dma = pltpu.SemaphoreType.DMA
    regular = pltpu.SemaphoreType.REGULAR
    entries, attended = pl.pallas_call(
        kernel,
        out_shape=(
            jax.ShapeDtypeStruct((1, 2, 4, 256), BF16),
            jax.ShapeDtypeStruct((1, 2, 4, 1024), BF16),
        ),
        in_specs=[anywhere] * 4 + [scalar] * 2 + [anywhere] * 3,
        out_specs=(vmem, vmem),
        scratch_shapes=[
            pltpu.VMEM((1, 2, 4, 1024), BF16),
            pltpu.VMEM((TP, 16, 512), BF16),
            pltpu.VMEM((TP, ROWS, 1024), BF16),
            pltpu.VMEM((PLACES, 32, 128), BF16),
            pltpu.VMEM((PLACES, 32, 128), BF16),
            pltpu.VMEM((GROUPS, 128, 128), BF16),
            pltpu.VMEM((GROUPS, 128, 128), BF16),
            pltpu.VMEM((GROUPS, 2, 128), F32),
            pltpu.VMEM((8192, 256), BF16),
            pltpu.VMEM((64, 128), BF16),
            pltpu.VMEM((1, 2, 4, 1024), BF16),
            pltpu.VMEM((4, 256, 256), BF16),
            pltpu.VMEM((PLACES, 16, 128), BF16),
            pltpu.VMEM((PLACES, 16, 128), BF16),
            pltpu.SMEM((1, 4), jnp.int32),
            dma((7,)),
            regular,
            regular,
            regular,
            regular((GROUPS,)),
            dma((CHIPS,)),
            dma((TP,)),
            dma((CHIPS,)),
            dma((PLACES - 1,)),
            dma((PLACES,)),
            dma((GROUPS,)),
            dma((GROUPS,)),
            dma((GROUPS,)),
            dma((GROUPS,)),
            dma((PLACES - 1,)),
            dma((PLACES,)),
        ],
        compiler_params=pltpu.CompilerParams(
            collective_id=0, has_side_effects=True, vmem_limit_bytes=24 * 1024 * 1024
        ),
    )(
        hbm(hidden),
        hbm(norm_gain.reshape(64, 128)),
        hbm(kv_weight),
        hbm(delta_tiles),
        tile_blocks,
        tile_counts,
        hbm(queries),
        hbm(kv_cache),
        hbm(positions),
    )
    return pl.pallas_call(
        hand_over,
        out_shape=(
            jax.ShapeDtypeStruct((1, 2, 4, 256), BF16),
            jax.ShapeDtypeStruct((1, 2, 4, 1024), BF16),
        ),
        in_specs=[vmem, vmem],
        out_specs=(anywhere, anywhere),
        scratch_shapes=[dma((2,))],
        compiler_params=pltpu.CompilerParams(vmem_limit_bytes=1024 * 1024),
    )(
        pltpu.with_memory_space_constraint(entries, pltpu.VMEM),
        pltpu.with_memory_space_constraint(attended, pltpu.VMEM),
    )


def solution(mesh):
    return jax.shard_map(
        shards,
        mesh=mesh,
        in_specs=(
            P("rep", None, None, "tp"),
            P(),
            P(None, "tp"),
            P("rep", None, "tp"),
            P("rep", "tp"),
            P("rep", "tp"),
            P("rep", None, None, "tp"),
            P("rep", None, None, "tp"),
            P("rep", None),
        ),
        out_specs=(P("rep", None, None, "tp"), P("rep", None, None, "tp")),
        check_vma=False,
    )
```

```python
import math

import jax
import jax.numpy as jnp
from jax import lax
from jax.experimental import pallas as pl
from jax.experimental.pallas import tpu as pltpu
from jax.sharding import PartitionSpec as P

EPS = 1e-06
THETA = 1000000.0
F32 = jnp.float32
BF16 = jnp.bfloat16
MESH = pl.DeviceIdType.MESH

GROUPS = 4
PLACES = 16
SIDE = 4
TP = 8
CHIPS = 4
ROWS = 8
GREETED = {0: (2, 3, 1), 1: (2,), 2: (), 3: ()}


def kernel(
    hidden,
    gain,
    weight,
    tile,
    blocks,
    counts,
    queries,
    cache,
    positions,
    entries_out,
    attended_out,
    hidden_v,
    all_v,
    x_v,
    give_v,
    got_v,
    xh_v,
    tile_v,
    flag_v,
    weight_v,
    gain_v,
    query_v,
    cache_v,
    ret_send,
    ret_recv,
    positions_s,
    local_sem,
    core_ready,
    tp_ready,
    plane_ready,
    z_ready,
    hid_send_sem,
    hid_recv_sem,
    core_send_sem,
    give_send_sem,
    give_recv_sem,
    tile_send_sem,
    tile_recv_sem,
    flag_send_sem,
    flag_recv_sem,
    ret_send_sem,
    ret_recv_sem,
):
    rep = lax.axis_index("rep")
    tp = lax.axis_index("tp")
    h, place = rep // PLACES, rep % PLACES
    l, c = tp // 2, tp % 2
    partner = {"rep": rep, "tp": tp + 1 - 2 * c}
    y, x = place // SIDE, place % SIDE
    listens = (h == 2) & (l > 0) & (c == 1)
    greetings = jnp.where(h == 2, 2, jnp.where(h == 0, 0, 1)) + jnp.where(listens, jnp.where(l == 2, 4, 2), 0)

    def in_chip(chip):
        return {"rep": rep, "tp": chip * 2 + c}

    def in_plane(p):
        return {"rep": h * PLACES + p, "tp": tp}

    def in_z(group):
        return {"rep": group * PLACES + place, "tp": tp}

    def neighbour(offset, sign):
        dy, dx = offset // SIDE, offset % SIDE
        if sign > 0:
            return ((y + dy) % SIDE) * SIDE + (x + dx) % SIDE
        return ((y + SIDE - dy) % SIDE) * SIDE + (x + SIDE - dx) % SIDE

    def hops(offset):
        dy, dx = offset // SIDE, offset % SIDE
        return min(dy, SIDE - dy) + min(dx, SIDE - dx)

    offsets = sorted(range(1, PLACES), key=lambda o: -hops(o))

    def local(source, target, index):
        return pltpu.make_async_copy(source, target, local_sem.at[index])

    hidden_load = local(hidden, hidden_v, 0)
    tile_load = local(tile.at[0], tile_v.at[h], 1)
    positions_load = local(positions, positions_s, 2)
    query_load = local(queries, query_v, 3)
    cache_load = local(cache.at[0], cache_v, 4)
    gain_load = local(gain, gain_v, 5)
    weight_load = local(weight, weight_v, 6)
    tile_load.start()
    hidden_load.start()

    hurried = (h == 2) & (c == 0) & (l == 0)
    extra = jnp.where((h == 2) & (l == 2) & (c == 1), place, 0)
    awaited = jnp.where(hurried, 0, place) + extra + l + c + greetings

    barrier = pltpu.get_barrier_semaphore()

    def signal(semaphore, where):
        pl.semaphore_signal(semaphore, inc=1, device_id=where, device_id_type=MESH)

    for group in range(GROUPS):
        @pl.when(h == group)
        def _():
            for later in GREETED[group]:
                signal(barrier, in_z(later))

    @pl.when(h == 3)
    def _():
        signal(barrier, {"rep": 2 * PLACES + place, "tp": jnp.where(l == 0, 2, l) * 2 + 1})

    @pl.when(c == 0)
    def _():
        signal(barrier, partner)

    for chip in range(1, CHIPS):
        @pl.when(chip > l)
        def _():
            signal(barrier, in_chip(chip))

    for p in range(1, PLACES):
        @pl.when(p > place)
        def _():
            signal(barrier, {"rep": h * PLACES + p, "tp": jnp.where(hurried, 5, tp)})

    valid = jnp.where(counts[0, 0] > 0, 1.0, 0.0)
    is_key = jnp.where(blocks[0, 0] % 2 == 0, 1.0, 0.0)
    flag_v[h] = jnp.concatenate(
        [jnp.full((1, 128), valid * is_key, F32), jnp.full((1, 128), valid * (1.0 - is_key), F32)], axis=0
    )

    @pl.when(awaited > 0)
    def _():
        pl.semaphore_wait(barrier, awaited)


    def tile_copy(source, group, number):
        return pltpu.make_async_remote_copy(
            src_ref=tile_v.at[h if source is None else source],
            dst_ref=tile_v.at[h if source is None else source],
            send_sem=tile_send_sem.at[number],
            recv_sem=tile_recv_sem.at[h if source is None else source],
            device_id=in_z(group),
            device_id_type=MESH,
        )

    def flag_copy(source, group, number):
        slot = h if source is None else source
        return pltpu.make_async_remote_copy(
            src_ref=flag_v.at[slot],
            dst_ref=flag_v.at[slot],
            send_sem=flag_send_sem.at[number],
            recv_sem=flag_recv_sem.at[slot],
            device_id=in_z(group),
            device_id_type=MESH,
        )

    def tile_start(source, group, number):
        flag_copy(source, group, number).start()
        tile_copy(source, group, number).start()

    def arrive(group):
        pltpu.make_async_copy(tile_v.at[group], tile_v.at[group], tile_recv_sem.at[group]).wait()
        pltpu.make_async_copy(flag_v.at[group], flag_v.at[group], flag_recv_sem.at[group]).wait()

    tile_load.wait()

    @pl.when((h == 1) | (h == 3))
    def _():
        signal(z_ready.at[h], in_z(0))
        pl.when(c == 0)(lambda: tile_start(None, 0, 0))

    @pl.when(h == 2)
    def _():
        pl.when(c == 0)(lambda: tile_start(None, 0, 0))
        signal(z_ready.at[h], in_z(1))
        pl.when(listens)(lambda: signal(z_ready.at[3], partner))
        pl.when(listens & (l == 2))(lambda: signal(z_ready.at[3], in_chip(0)))

    @pl.when(c == 1)
    def _():
        signal(core_ready, partner)

    for chip in range(CHIPS - 1):
        @pl.when(chip < l)
        def _():
            signal(tp_ready, in_chip(chip))

    hidden_load.wait()
    mine = jnp.concatenate([hidden_v[0, 0].astype(F32), hidden_v[0, 1].astype(F32)], axis=0)
    all_v[tp] = jnp.concatenate([mine[:, :512], mine[:, 512:]], axis=0).astype(BF16)


    def hidden_copy(chip):
        return pltpu.make_async_remote_copy(
            src_ref=all_v.at[tp],
            dst_ref=all_v.at[tp],
            send_sem=hid_send_sem.at[chip],
            recv_sem=hid_recv_sem.at[tp],
            device_id=in_chip(chip),
            device_id_type=MESH,
        )

    def core_copy(chip):
        source = chip * 2 + c
        return pltpu.make_async_remote_copy(
            src_ref=all_v.at[source],
            dst_ref=all_v.at[source],
            send_sem=core_send_sem.at[chip],
            recv_sem=hid_recv_sem.at[source],
            device_id=partner,
            device_id_type=MESH,
        )

    def hidden_arrive(t):
        pltpu.make_async_copy(all_v.at[t], all_v.at[t], hid_recv_sem.at[t]).wait()

    def hidden_back():
        for chip in range(CHIPS - 1):
            @pl.when(chip < l)
            def _():
                hidden_copy(chip).start()

    def hidden_on():
        @pl.when(l < CHIPS - 1)
        def _():
            pl.semaphore_wait(tp_ready, CHIPS - 1 - l)

        for chip in range(CHIPS - 1, 0, -1):
            @pl.when(chip > l)
            def _():
                hidden_copy(chip).start()

        @pl.when(c == 0)
        def _():
            pl.semaphore_wait(core_ready, 1)

        core_copy(l).start()

    pl.when(h != 2)(hidden_back)
    def plane_word():
        for p in range(PLACES - 1):
            @pl.when(p < place)
            def _():
                signal(plane_ready, in_plane(p))

    pl.when(jnp.logical_not(hurried))(plane_word)

    gain_load.start()
    query_load.start()
    positions_load.start()
    cache_load.start()
    weight_load.start()

    pl.when((h != 0) & (c == 1))(lambda: tile_start(None, 0, 0))
    pl.when(h != 2)(hidden_on)
    query_load.wait()
    positions_load.wait()
    all_queries = jnp.concatenate([query_v[0, 0].astype(F32), query_v[0, 1].astype(F32)], axis=0)
    heads = all_queries.shape[1] // 128
    query_rows = jnp.concatenate([all_queries[:, i * 128 : i * 128 + 128] for i in range(heads)], axis=0)
    query = query_rows.astype(BF16)
    rows = heads * ROWS
    cache_load.wait()
    length = cache_v.shape[1]
    row = lax.broadcasted_iota(jnp.int32, (rows, length), 0)
    column = lax.broadcasted_iota(jnp.int32, (rows, length), 1)
    sequence = row % 4
    scores = jnp.zeros((rows, length), F32)
    filled = jnp.zeros((rows, length), jnp.int32)
    for r in range(4):
        keys = cache_v[r, :, :128]
        product = lax.dot_general(query, keys, (((1,), (1,)), ((), ())), preferred_element_type=F32)
        scores = jnp.where(sequence == r, product, scores)
        filled = jnp.where(sequence == r, positions_s[0, r], filled)
    scale = 128 ** (-0.5)
    scores = jnp.where(column < filled, scores * scale, -1e30)
    old_peak = jnp.max(scores, axis=-1, keepdims=True)
    raised = jnp.exp(scores - old_peak)
    old_sum = jnp.sum(raised, axis=-1, keepdims=True)
    old_mixed = jnp.zeros((rows, 128), F32)
    for r in range(4):
        chosen = jnp.where(sequence == r, raised, 0.0).astype(BF16)
        old_mixed = old_mixed + jnp.dot(chosen, cache_v[r, :, 128:], preferred_element_type=F32)

    token = lax.broadcasted_iota(jnp.int32, (ROWS, 128), 0)
    lane = lax.broadcasted_iota(jnp.int32, (ROWS, 128), 1)
    moment = token // 4
    for r in range(4):
        moment = jnp.where(token % 4 == r, token // 4 + positions_s[0, r], moment)
    inverse = jnp.exp((lane % 64).astype(F32) * (-2.0 * math.log(THETA) / 128))
    angle = moment.astype(F32) * inverse
    cosine = jnp.cos(angle)
    sine = jnp.where(lane < 64, -1.0, 1.0) * jnp.sin(angle)

    @pl.when(h == 2)
    def _():
        hidden_back()
        hidden_on()
        tile_start(None, 1, 1)

        @pl.when((c == 0) | (l == 0))
        def _():
            pl.semaphore_wait(z_ready.at[3], 1)

        pl.when((c == 1) & (l == 0))(lambda: signal(z_ready.at[3], partner))
        pl.when(hurried)(plane_word)
        signal(z_ready.at[2], in_z(3))
        tile_start(None, 3, 2)

    @pl.when(h == 0)
    def _():
        pl.semaphore_wait(z_ready.at[1], 1)
        tile_start(None, 1, 0)

    for chip in range(CHIPS):
        @pl.when(chip != l)
        def _():
            hidden_arrive(chip * 2 + c)
            core_copy(chip).start()

    @pl.when(h == 1)
    def _():
        pl.semaphore_wait(z_ready.at[2], 1)
        tile_start(None, 2, 1)

    for chip in range(CHIPS):
        hidden_arrive(chip * 2 + 1 - c)

    squares = jnp.zeros((ROWS, 128), F32)
    for t in range(TP):
        piece = all_v[t].astype(F32)
        for b in range(8):
            part = piece[(b // 4) * 8 : (b // 4) * 8 + 8, (b % 4) * 128 : (b % 4) * 128 + 128]
            squares = squares + part * part
    rate = lax.rsqrt(jnp.sum(squares, axis=-1, keepdims=True) / 8192.0 + EPS)
    rate = jnp.broadcast_to(rate, (ROWS, 128))
    gain_load.wait()
    gains = gain_v[...].astype(F32)
    normed = []
    for t in range(TP):
        piece = all_v[t].astype(F32)
        for b in range(8):
            part = piece[(b // 4) * 8 : (b // 4) * 8 + 8, (b % 4) * 128 : (b % 4) * 128 + 128]
            normed.append(part * rate * gains[t * 8 + b : t * 8 + b + 1])
    for p in range(PLACES):
        give_v[p] = jnp.concatenate([normed[group * 16 + p] for group in range(GROUPS)], axis=0).astype(BF16)

    def give_copy(number):
        there = neighbour(offsets[number], 1)
        return pltpu.make_async_remote_copy(
            src_ref=give_v.at[there],
            dst_ref=got_v.at[place],
            send_sem=give_send_sem.at[number],
            recv_sem=give_recv_sem.at[place],
            device_id=in_plane(there),
            device_id_type=MESH,
        )

    @pl.when(place < PLACES - 1)
    def _():
        pl.semaphore_wait(plane_ready, PLACES - 1 - place)

    def give():
        for number in range(PLACES - 1):
            give_copy(number).start()

    pl.when(c == 0)(give)

    for t in range(TP):
        x_v[t] = jnp.concatenate(normed[t * 8 : t * 8 + 8], axis=1).astype(BF16)
    weight_load.wait()

    def project(t, total):
        rows_of = weight_v[pl.ds(pl.multiple_of(t * 1024, 1024), 1024)]
        return total + jnp.dot(x_v[t], rows_of, preferred_element_type=F32)

    base = lax.fori_loop(0, 2, project, jnp.zeros((ROWS, 256), F32))
    pl.when(c == 1)(give)
    got_v[place] = give_v[place]

    @pl.when(h == 0)
    def _():
        pl.semaphore_wait(z_ready.at[3], 1)
        tile_start(None, 3, 1)


    @pl.when(h == 1)
    def _():
        arrive(0)
        tile_start(0, 2, 2)

    first = jnp.where((h == 0) | (h == 2), 1, 0)
    second = jnp.where(h == 0, 3, jnp.where(h == 1, 2, jnp.where(h == 2, 0, 1)))
    third = jnp.where((h == 0) | (h == 3), 2, 3)

    @pl.when(h == 3)
    def _():
        pl.semaphore_wait(z_ready.at[2], 1)
        tile_start(None, 2, 1)

    @pl.when(h != 1)
    def _():
        arrive(first)

    @pl.when(h == 0)
    def _():
        tile_start(1, 3, 2)

    base = lax.fori_loop(2, TP, project, base)

    arrive(second)
    pl.when(h == 0)(lambda: tile_start(3, 1, 3))

    for number in range(PLACES - 1):
        there = neighbour(offsets[number], -1)
        pltpu.make_async_copy(got_v.at[there], got_v.at[there], give_recv_sem.at[there]).wait()
    turns = [neighbour(offset, 1) for offset in offsets] + [place]
    for turn in range(0, PLACES, 2):
        even, odd = got_v[turns[turn]].astype(F32), got_v[turns[turn + 1]].astype(F32)
        for group in range(GROUPS):
            xh_v[group, turn * 8 : turn * 8 + 16] = jnp.concatenate(
                [even[group * 8 : group * 8 + 8], odd[group * 8 : group * 8 + 8]], axis=0
            ).astype(BF16)

    def multiply(group, key_part, value_part):
        product = jnp.dot(xh_v[group], tile_v[group], preferred_element_type=F32)
        flags = flag_v[group]
        return key_part + product * flags[0:1], value_part + product * flags[1:2]

    blank = jnp.zeros((PLACES * ROWS, 128), F32)
    key_part, value_part = multiply(h, blank, blank)
    key_part, value_part = multiply(first, key_part, value_part)
    key_part, value_part = multiply(second, key_part, value_part)
    arrive(third)

    key_part, value_part = multiply(third, key_part, value_part)

    def ret_copy(number):
        there = neighbour(offsets[number], 1)
        return pltpu.make_async_remote_copy(
            src_ref=ret_send.at[number],
            dst_ref=ret_recv.at[place],
            send_sem=ret_send_sem.at[number],
            recv_sem=ret_recv_sem.at[place],
            device_id=in_plane(there),
            device_id_type=MESH,
        )

    def share(turn):
        rows_of = slice(turn * 8, turn * 8 + 8)
        return jnp.concatenate([key_part[rows_of], value_part[rows_of]], axis=0)

    for number in range(PLACES - 1):
        ret_send[number] = share(number).astype(BF16)
        ret_copy(number).start()

    total = share(PLACES - 1)
    for number in range(PLACES - 2, -1, -1):
        there = neighbour(offsets[number], -1)
        pltpu.make_async_copy(ret_recv.at[there], ret_recv.at[there], ret_recv_sem.at[there]).wait()
        total = total + ret_recv[there].astype(F32)
    new_keys = base[:, :128] + total[:8]
    new_values = base[:, 128:] + total[8:]

    rotated = new_keys * cosine + pltpu.roll(new_keys, 64, 1) * sine
    new_entries = jnp.concatenate([rotated, new_values], axis=1)
    entries_out[0, 0] = new_entries[:4].astype(BF16)
    entries_out[0, 1] = new_entries[4:].astype(BF16)

    rounded_keys = rotated.astype(BF16).astype(F32)
    rounded_values = new_values.astype(BF16).astype(F32)

    def spread(entry, step):
        return jnp.concatenate([entry[step * 4 : step * 4 + 4]] * (rows // 4), axis=0)

    score_0 = jnp.sum(query_rows * spread(rounded_keys, 0), axis=-1, keepdims=True) * scale
    score_1 = jnp.sum(query_rows * spread(rounded_keys, 1), axis=-1, keepdims=True) * scale
    late = (lax.broadcasted_iota(jnp.int32, (rows, 1), 0) // 4) % 2 == 1
    score_1 = jnp.where(late, score_1, -1e30)
    peak = jnp.maximum(old_peak, jnp.maximum(score_0, score_1))
    raised_0 = jnp.exp(score_0 - peak)
    raised_1 = jnp.exp(score_1 - peak)
    shrink = jnp.exp(old_peak - peak)
    all_sum = old_sum * shrink + raised_0 + raised_1
    mixed = old_mixed * shrink + raised_0 * spread(rounded_values, 0) + raised_1 * spread(rounded_values, 1)
    mixed = mixed * (1.0 / all_sum)
    wide = jnp.concatenate([mixed[i * 8 : i * 8 + 8] for i in range(heads)], axis=1)
    attended_out[0, 0] = wide[:4].astype(BF16)
    attended_out[0, 1] = wide[4:].astype(BF16)

    for chip in range(CHIPS):
        @pl.when(chip != l)
        def _():
            hidden_copy(chip).wait_send()

        core_copy(chip).wait_send()

    for number in range(GROUPS):
        @pl.when((number < 2) | ((number == 2) & (h != 3)) | (h == 0))
        def _():
            tile_copy(None, 0, number).wait_send()
            flag_copy(None, 0, number).wait_send()

    for number in range(PLACES - 1):
        give_copy(number).wait_send()
        ret_copy(number).wait_send()


def hand_over(entries, attended, entries_out, attended_out, sem):
    copies = (
        pltpu.make_async_copy(entries, entries_out, sem.at[0]),
        pltpu.make_async_copy(attended, attended_out, sem.at[1]),
    )
    for copy in copies:
        copy.start()
    for copy in copies:
        copy.wait()


def shards(hidden, norm_gain, kv_weight, delta_tiles, tile_blocks, tile_counts, queries, kv_cache, positions):
    def hbm(array):
        return pltpu.with_memory_space_constraint(array, pltpu.HBM)

    anywhere = pl.BlockSpec(memory_space=pltpu.HBM)
    scalar = pl.BlockSpec(memory_space=pltpu.SMEM)
    vmem = pl.BlockSpec(memory_space=pltpu.VMEM)
    dma = pltpu.SemaphoreType.DMA
    regular = pltpu.SemaphoreType.REGULAR
    entries, attended = pl.pallas_call(
        kernel,
        out_shape=(
            jax.ShapeDtypeStruct((1, 2, 4, 256), BF16),
            jax.ShapeDtypeStruct((1, 2, 4, 1024), BF16),
        ),
        in_specs=[anywhere] * 4 + [scalar] * 2 + [anywhere] * 3,
        out_specs=(vmem, vmem),
        scratch_shapes=[
            pltpu.VMEM((1, 2, 4, 1024), BF16),
            pltpu.VMEM((TP, 16, 512), BF16),
            pltpu.VMEM((TP, ROWS, 1024), BF16),
            pltpu.VMEM((PLACES, 32, 128), BF16),
            pltpu.VMEM((PLACES, 32, 128), BF16),
            pltpu.VMEM((GROUPS, 128, 128), BF16),
            pltpu.VMEM((GROUPS, 128, 128), BF16),
            pltpu.VMEM((GROUPS, 2, 128), F32),
            pltpu.VMEM((8192, 256), BF16),
            pltpu.VMEM((64, 128), BF16),
            pltpu.VMEM((1, 2, 4, 1024), BF16),
            pltpu.VMEM((4, 256, 256), BF16),
            pltpu.VMEM((PLACES, 16, 128), BF16),
            pltpu.VMEM((PLACES, 16, 128), BF16),
            pltpu.SMEM((1, 4), jnp.int32),
            dma((7,)),
            regular,
            regular,
            regular,
            regular((GROUPS,)),
            dma((CHIPS,)),
            dma((TP,)),
            dma((CHIPS,)),
            dma((PLACES - 1,)),
            dma((PLACES,)),
            dma((GROUPS,)),
            dma((GROUPS,)),
            dma((GROUPS,)),
            dma((GROUPS,)),
            dma((PLACES - 1,)),
            dma((PLACES,)),
        ],
        compiler_params=pltpu.CompilerParams(
            collective_id=0, has_side_effects=True, vmem_limit_bytes=24 * 1024 * 1024
        ),
    )(
        hbm(hidden),
        hbm(norm_gain.reshape(64, 128)),
        hbm(kv_weight),
        hbm(delta_tiles),
        tile_blocks,
        tile_counts,
        hbm(queries),
        hbm(kv_cache),
        hbm(positions),
    )
    return pl.pallas_call(
        hand_over,
        out_shape=(
            jax.ShapeDtypeStruct((1, 2, 4, 256), BF16),
            jax.ShapeDtypeStruct((1, 2, 4, 1024), BF16),
        ),
        in_specs=[vmem, vmem],
        out_specs=(anywhere, anywhere),
        scratch_shapes=[dma((2,))],
        compiler_params=pltpu.CompilerParams(vmem_limit_bytes=1024 * 1024),
    )(
        pltpu.with_memory_space_constraint(entries, pltpu.VMEM),
        pltpu.with_memory_space_constraint(attended, pltpu.VMEM),
    )


def solution(mesh):
    return jax.shard_map(
        shards,
        mesh=mesh,
        in_specs=(
            P("rep", None, None, "tp"),
            P(),
            P(None, "tp"),
            P("rep", None, "tp"),
            P("rep", "tp"),
            P("rep", "tp"),
            P("rep", None, None, "tp"),
            P("rep", None, None, "tp"),
            P("rep", None),
        ),
        out_specs=(P("rep", None, None, "tp"), P("rep", None, None, "tp")),
        check_vma=False,
    )
```
